128 devices in a mesh: seq: 16 (over z, x_lo, core), tensor: 8 (over y, x_hi).
Axes of the slice: x: 4 (x_hi: 2, x_lo: 2; x = x_hi * 2 + x_lo), y: 4, z: 4, core: 2. Of those that a mesh axis runs over, the one named last changes fastest.
Arguments:
- tokens: bfloat16 [4096, 2048], P('seq'), may hold values from -6 to 6
- cotangent: bfloat16 [4096, 2048], P('seq'), may hold values from -6 to 6
- exits: int32 [4096], P('seq'), may hold values from 0 to 23, as said below
- lengths: int32 [4], replicated, may hold values from 1 to 2048, 4096 in all
- panels: float32 [384, 64, 2048], P(('tensor', 'seq'))
- panel_mom: float32 [384, 64, 2048], P(('tensor', 'seq')), may hold values from -80 to 80
- unit_bias: float32 [32, 384], P('tensor'), may hold values from -1.75 to 1.75
- unit_bias_mom: float32 [32, 384], P('tensor'), may hold values from -112 to 112
- gains: float32 [2, 2048], replicated, may hold values from 0.5 to 1.5
- gains_mom: float32 [2, 2048], replicated, may hold values from -192 to 192
- vec_bias: float32 [4, 2048], replicated, may hold values from -1.75 to 1.75
- vec_bias_mom: float32 [4, 2048], replicated, may hold values from -192 to 192
Outputs:
- output: bfloat16 [4096, 2048], P('seq')
- input_grad: float32 [4096, 2048], P('seq')
- new_panels: float32 [384, 64, 2048], P(('tensor', 'seq'))
- new_panel_mom: float32 [384, 64, 2048], P(('tensor', 'seq'))
- new_unit_bias: float32 [32, 384], P('tensor')
- new_unit_bias_mom: float32 [32, 384], P('tensor')
- new_gains: float32 [2, 2048], replicated
- new_gains_mom: float32 [2, 2048], replicated
- new_vec_bias: float32 [4, 2048], replicated
- new_vec_bias_mom: float32 [4, 2048], replicated
The draws below stay inside these ranges and needn't reach their ends.
Inputs may be any that keep to these rules, and one draw needn't show every extreme that they name: `exits`: constant over aligned bands of 32 positions; the share of bands with exit layer 12 or more rises from about 0.3 at the first position to 0.9 at the last. `lengths`: they sum to 4096; the longest is 2048.
All inputs are finite; a program needn't handle non-finite values.
Results may differ from the reference program's by a relative error of at most 0.035.
Values may be sent and summed in bfloat16 or wider, within the bound.
A program may use at most 128 MiB of HBM per device.

```python
import math
import jax
import jax.numpy as jnp
import numpy as np
from jax import lax

D = 2048
HEADS = 32
HD = 64
SEQS = 4
LAYER = 12
LAYERS = 24
BAND = 32
NS_ITERS = 5
TOKENS = 4096
PANELS = 384


def draw_exits(key, part):
    key = jax.random.fold_in(key, 11)
    bands = TOKENS // BAND
    first, second, third = jax.random.split(key, 3)
    roll = jax.random.randint(first, (bands,), 0, 100)
    share = 30 + 60 * jnp.arange(bands, dtype=jnp.int32) // bands
    deep = jax.random.randint(second, (bands,), LAYER, LAYERS)
    shallow = jax.random.randint(third, (bands,), 0, LAYER)
    exit_band = jnp.where(roll < share, deep, shallow).astype(jnp.int32)
    exit_band = exit_band.at[0].set(0)
    exit_band = exit_band.at[bands - 1].set(LAYERS - 1)
    return jnp.repeat(exit_band, BAND, total_repeat_length=TOKENS).astype(jnp.int32)


def draw_panels(key, part):
    key = jax.random.fold_in(key, 5)
    factor = jnp.array([1.4, 1.4, 1.0, 4.0, 1.0, 1.0, 1.0, 1.0, 0.75, 0.75, 0.75, 0.75], dtype=jnp.float32) * D ** (-0.5)
    spread = jnp.tile(factor, HEADS)[:, None, None]
    raw = jax.random.normal(key, (PANELS, HD, D), jnp.float32)
    return raw * spread


def shard_levels(rng, extent, pieces, low, largest):
    def one(dim, blocks):
        steps = jax.random.uniform(jax.random.fold_in(jax.random.fold_in(rng, 6), dim), (blocks,), jnp.float32, low / len(pieces), largest / len(pieces))
        return jnp.repeat(jnp.exp(steps), extent[dim] // blocks).reshape((-1,) + (1,) * (len(extent) - dim - 1))

    factor_of = one(*pieces[0])
    for cut in pieces[1:]:
        factor_of = factor_of * one(*cut)
    return factor_of


def split_up(amount, total, bound, slope):
    loads = [(1 << 20) // math.isqrt(grade ** slope) + 1 for grade in range(2, amount + 1)]
    surplus, given = total - bound - (amount - 1), [1] * (amount - 1)
    while surplus > 0:
        candidates = [i for i in range(amount - 1) if given[i] < bound]
        mass, budget = sum([loads[i] for i in candidates]), surplus
        for i in candidates:
            addition = min(bound - given[i], max(1, budget * loads[i] // mass), surplus)
            given[i] = given[i] + addition
            surplus = surplus - addition
    return np.array([bound] + given)


def uneven(key, number_of, total, most, lean):
    if number_of == 2:
        one = jax.random.randint(key, (), max(1, total - most), min(most, total - 1) + 1)
        return jnp.stack([one, total - one])
    tallies = jnp.asarray(split_up(number_of, total, most, lean), jnp.int32)
    twos = (number_of - 1) // 2
    source_of, sink = tallies[1:1 + 2 * twos:2], tallies[2:2 + 2 * twos:2]
    room = jnp.minimum(source_of - 1, most - sink)
    passed = jax.random.randint(jax.random.fold_in(key, 1), (twos,), 0, 1 << 20) % (room + 1)
    tallies = tallies.at[1:1 + 2 * twos:2].set(source_of - passed).at[2:2 + 2 * twos:2].set(sink + passed)
    return tallies[jax.random.permutation(jax.random.fold_in(key, 2), number_of)]


def noise(stream_key, extent, width, most, shards=(), kind=jnp.bfloat16):
    values = jax.random.normal(stream_key, extent, jnp.float32) * width
    if len(shards) > 0:
        values = shard_levels(stream_key, extent, shards, -0.22, 0.18) * values
    return jnp.clip(values, min=-most, max=most).astype(kind)


def setup_inputs(seed: int = 0) -> dict:
    key_of = jax.random.split(jax.random.key(seed), 13)
    return {
        "tokens": noise(key_of[0], (TOKENS, D), 1.0, 6.0, ((0, 16),)),
        "cotangent": noise(key_of[1], (TOKENS, D), 1.0, 6.0, ((0, 16),)),
        "exits": draw_exits(jax.random.fold_in(key_of[12], 71), 0),
        "lengths": uneven(key_of[3], SEQS, TOKENS, TOKENS // 2, 1).astype(jnp.int32),
        "panels": draw_panels(jax.random.fold_in(key_of[12], 71), 0),
        "panel_mom": noise(key_of[5], (PANELS, HD, D), (0.2 * TOKENS ** 0.5), 80.0, ((0, 128),), jnp.float32),
        "unit_bias": noise(key_of[6], (HEADS, 6 * HD), 0.3, 1.75, ((0, 8),), jnp.float32),
        "unit_bias_mom": noise(key_of[7], (HEADS, 6 * HD), (0.3 * TOKENS ** 0.5), 112.0, ((0, 8),), jnp.float32),
        "gains": jnp.clip(1.0 + 0.1 * jax.random.normal(key_of[8], (2, D), jnp.float32), 0.5, 1.5),
        "gains_mom": noise(key_of[9], (2, D), (0.5 * TOKENS ** 0.5), 192.0, (), jnp.float32),
        "vec_bias": noise(key_of[10], (4, D), 0.3, 1.75, (), jnp.float32),
        "vec_bias_mom": noise(key_of[11], (4, D), (0.5 * TOKENS ** 0.5), 192.0, (), jnp.float32),
    }


EPS = 1e-05
NS_A = 3.4445
NS_B = -4.775
NS_C = 2.0315
LR_MATRIX = 0.5
LR_VECTOR = 0.002
DECAY = 0.5
HIGH = lax.Precision.HIGHEST

@jax.custom_vjp
def low(v):
    return lax.optimization_barrier(v.astype(jnp.bfloat16)).astype(jnp.float32)

@jax.custom_vjp
def low_back(v):
    return v

def low_keep(v):
    return (low(v), None)

def low_pass(kept, grad):
    return (grad,)

def back_keep(v):
    return (v, None)

def back_low(kept, grad):
    return (low(grad),)
low.defvjp(low_keep, low_pass)
low_back.defvjp(back_keep, back_low)

def matmul(left, right):
    return jnp.dot(left, right, precision=HIGH)

def normalize(values, gain, shift):
    mean = lax.optimization_barrier(jnp.mean(values, axis=-1, keepdims=True))
    centred = values - mean
    scale = lax.rsqrt(lax.optimization_barrier(jnp.mean(centred * centred, axis=-1, keepdims=True)) + EPS)
    return centred * scale * gain + shift

def attention(query, keys, values, active, segment, positions):
    scale = HD ** (-0.5)
    q_heads = query.reshape(TOKENS, HEADS, HD)
    k_heads = keys.reshape(TOKENS, HEADS, HD)
    v_heads = values.reshape(TOKENS, HEADS, HD)
    block = math.gcd(TOKENS, 512)
    count = TOKENS // block

    def one_block(blocked):
        q_blk, s_blk, p_blk, a_blk = blocked
        score = low_back(jnp.einsum('qhe,khe->hqk', q_blk, k_heads, precision=HIGH) * scale)
        allowed = (s_blk[:, None] == segment[None, :]) & (p_blk[:, None] >= positions[None, :])
        allowed = allowed & (a_blk[:, None] > 0) & (active[None, :] > 0)
        score = jnp.where(allowed[None], score, -1e+30)
        prob = low(jax.nn.softmax(score, axis=-1))
        return jnp.einsum('hqk,khe->qhe', prob, v_heads, precision=HIGH)
    mixed = lax.map(jax.checkpoint(one_block), (q_heads.reshape(count, block, HEADS, HD), segment.reshape(count, block), positions.reshape(count, block), active.reshape(count, block)))
    return mixed.reshape(TOKENS, HEADS * HD)

def forward(x, panels, unit_bias, gains, vec_bias, active, segment, positions):
    stack = panels.reshape(HEADS, 12, HD, D)
    w_query = stack[:, 0].reshape(HEADS * HD, D)
    w_key = stack[:, 1].reshape(HEADS * HD, D)
    w_value = stack[:, 2].reshape(HEADS * HD, D)
    w_out = stack[:, 3].reshape(HEADS * HD, D)
    w_in = stack[:, 4:8].reshape(HEADS * 4 * HD, D)
    w_back = stack[:, 8:12].reshape(HEADS * 4 * HD, D)
    b_query = unit_bias[:, :HD].reshape(-1)
    b_value = unit_bias[:, HD:2 * HD].reshape(-1)
    b_in = unit_bias[:, 2 * HD:].reshape(-1)
    live = active.astype(jnp.float32)[:, None]
    normed1 = low(normalize(x, gains[0], vec_bias[2]))
    query = low_back(low(matmul(normed1, w_query.T) + b_query))
    keys = low_back(low(matmul(normed1, w_key.T)))
    values = low_back(low(matmul(normed1, w_value.T) + b_value))
    mixed = low_back(low(attention(query, keys, values, active, segment, positions)))
    branch = low_back(matmul(mixed, w_out) + vec_bias[0])
    hidden = x + live * branch
    normed2 = low(normalize(hidden, gains[1], vec_bias[3]))
    pre = low_back(matmul(normed2, w_in.T) + b_in)
    acted = low(jax.nn.gelu(pre, approximate=False))
    ffn = low_back(matmul(acted, w_back) + vec_bias[1])
    return hidden + live * ffn

def orthogonalize(moment):
    current = moment * lax.rsqrt(lax.optimization_barrier(jnp.sum(moment * moment, axis=(1, 2), keepdims=True)) + 1e-06)
    for sweep in range(NS_ITERS):
        gram = jnp.einsum('pij,pkj->pik', current, current, precision=HIGH)
        poly = NS_B * gram + NS_C * jnp.einsum('pij,pjk->pik', gram, gram, precision=HIGH)
        current = NS_A * current + jnp.einsum('pij,pjk->pik', poly, current, precision=HIGH)
    return current

def reference(tokens, cotangent, exits, lengths, panels, panel_mom, unit_bias, unit_bias_mom, gains, gains_mom, vec_bias, vec_bias_mom):
    active = (exits >= LAYER).astype(jnp.int32)
    positions = jnp.arange(TOKENS, dtype=jnp.int32)
    ends = jnp.cumsum(lengths).astype(jnp.int32)
    segment = lax.optimization_barrier(jnp.sum((positions[:, None] >= ends[None, :]).astype(jnp.int32), axis=1)).astype(jnp.int32)

    def layer(x, p, u, g, b):
        return forward(x, p, u, g, b, active, segment, positions)
    result, pull = jax.vjp(layer, tokens.astype(jnp.float32), panels, unit_bias, gains, vec_bias)
    input_grad, grad_panels, grad_unit, grad_gains, grad_vec = pull(cotangent.astype(jnp.float32))
    moment = DECAY * panel_mom + grad_panels
    direction = orthogonalize(moment)
    size_w = lax.optimization_barrier(jnp.sum(panels * panels, axis=(1, 2), keepdims=True))
    size_u = lax.optimization_barrier(jnp.sum(direction * direction, axis=(1, 2), keepdims=True))
    new_panels = panels - LR_MATRIX * jnp.sqrt(size_w) * lax.rsqrt(size_u + 1e-06) * direction
    unit_moment = DECAY * unit_bias_mom + grad_unit
    gains_moment = DECAY * gains_mom + grad_gains
    vec_moment = DECAY * vec_bias_mom + grad_vec
    return (result.astype(jnp.bfloat16), input_grad, new_panels, moment, unit_bias - LR_VECTOR * unit_moment, unit_moment, gains - LR_VECTOR * gains_moment, gains_moment, vec_bias - LR_VECTOR * vec_moment, vec_moment)
```

```python
import functools
import math

import jax
import jax.numpy as jnp
from jax import lax
from jax.experimental import pallas as pl
from jax.experimental.pallas import tpu as pltpu
from jax.sharding import PartitionSpec as P

LAYER = 12
NS_ITERS = 5
EPS = 1e-05
NS_A = 3.4445
NS_B = -4.775
NS_C = 2.0315
LR_MATRIX = 0.5
LR_VECTOR = 0.002
DECAY = 0.5
HIGH = lax.Precision.HIGHEST
MESH = pl.DeviceIdType.MESH

ROWS = 256
WIDTH = 2048
GROUPS = 4
HD = 64
SPAN = GROUPS * HD
UNITS = 4 * SPAN
SHARD = 32
EXT = ROWS + 16
MASKED = -1e30
FLOOR = -1e28
BF = jnp.bfloat16
F32 = jnp.float32

Z_STEPS = (1, 3, 2)
T_STEPS = tuple((dy, dx) for dy in (2, 1, 3, 0) for dx in (1, 0) if (dy, dx) != (0, 0))


def nt(left, right):
    return lax.dot_general(left, right, (((1,), (1,)), ((), ())), preferred_element_type=F32)


def nn(left, right):
    return jnp.dot(left, right, preferred_element_type=F32)


def normalize(values, gain, shift):
    mean = jnp.mean(values, axis=-1, keepdims=True)
    centred = values - mean
    factor = lax.rsqrt(jnp.mean(centred * centred, axis=-1, keepdims=True) + EPS)
    return centred * factor * gain + shift, centred * factor, factor


class Place:
    def __init__(self):
        self.s = lax.axis_index("seq")
        self.t = lax.axis_index("tensor")
        self.z, self.x, self.c = self.s // 4, (self.s // 2) % 2, self.s % 2
        self.chip = self.s // 2
        self.y, self.h = self.t // 2, self.t % 2

    def seq(self, z, x, c):
        return {"seq": z * 4 + x * 2 + c}

    def sibling(self):
        return self.seq(self.z, self.x, 1 - self.c)

    def across(self):
        return self.seq(self.z, 1 - self.x, self.c)

    def along(self, step):
        return self.seq((self.z + step) % 4, self.x, self.c)

    def chip_at(self, step):
        return {"seq": (self.chip + step) * 2 + self.c}

    def tensor_at(self, dy, dx):
        return ((self.y + dy) % 4) * 2 + (self.h + dx) % 2

    def greet(self):
        barrier = pltpu.get_barrier_semaphore()
        count = 0
        for dz in range(4):
            for dx in range(2):
                if (dz, dx) != (0, 0):
                    to = self.seq((self.z + dz) % 4, (self.x + dx) % 2, self.c)
                    pl.semaphore_signal(barrier, inc=1, device_id=to, device_id_type=MESH)
                    count += 1
        pl.semaphore_signal(barrier, inc=1, device_id=self.sibling(), device_id_type=MESH)
        count += 1
        for dy, dx in T_STEPS:
            to = {"tensor": self.tensor_at(dy, dx)}
            pl.semaphore_signal(barrier, inc=1, device_id=to, device_id_type=MESH)
            count += 1
        pl.semaphore_wait(barrier, count)


def remote(src, dst, send, recv, to):
    return pltpu.make_async_remote_copy(
        src_ref=src, dst_ref=dst, send_sem=send, recv_sem=recv, device_id=to, device_id_type=MESH
    )


def scatter_copies(place, part, land, send, recv):
    out = []
    for i, (dy, dx) in enumerate(T_STEPS):
        to = place.tensor_at(dy, dx)
        rows = pl.ds(pl.multiple_of(to * SHARD, SHARD), SHARD)
        out.append(remote(part.at[rows], land.at[i], send.at[i], recv.at[i], {"tensor": to}))
    return out


def scatter_sum(place, part, land):
    mine = pl.ds(pl.multiple_of(place.t * SHARD, SHARD), SHARD)
    total = part[mine, :].astype(F32)
    for i in range(len(T_STEPS)):
        total = total + land[i].astype(F32)
    return total


def gather_copies(place, whole, send, recv):
    mine = pl.ds(pl.multiple_of(place.t * SHARD, SHARD), SHARD)
    out = []
    for i, (dy, dx) in enumerate(T_STEPS):
        to = place.tensor_at(dy, dx)
        out.append(remote(whole.at[mine], whole.at[mine], send.at[i], recv.at[i], {"tensor": to}))
    return out


def column_of(row):
    n = row.shape[1]
    down = lax.broadcasted_iota(jnp.int32, (n, n), 0)
    over = lax.broadcasted_iota(jnp.int32, (n, n), 1)
    return jnp.sum(jnp.where(down == over, row, 0.0), axis=1, keepdims=True)


def segment_of(positions, lengths):
    end = jnp.int32(0)
    segment = jnp.zeros(positions.shape, F32)
    for i in range(4):
        end = end + lengths[i]
        segment = segment + jnp.where(positions >= end, 1.0, 0.0)
    return segment


def query_code(place, lengths, alive_row):
    at = place.s * ROWS + lax.broadcasted_iota(jnp.int32, (1, ROWS), 1)
    return jnp.where(alive_row > 0.5, segment_of(at, lengths), -2.0), at


def block_bias(place, lengths, window, dist, core, code, at):
    first = ((place.chip - dist) * 2 + core) * ROWS
    keys = first + lax.broadcasted_iota(jnp.int32, (ROWS, 1), 0)
    live = column_of(window[dist, core, ROWS:EXT, 0:ROWS].astype(F32)[0:1])
    key_code = jnp.where(live > 0.5, segment_of(keys, lengths), -1.0)
    same = jnp.where(key_code == code, 0.0, MASKED)
    return jnp.where(keys <= at, same, MASKED)


def head_rows(values, head):
    owner = lax.broadcasted_iota(jnp.int32, values.shape, 0) // HD
    return jnp.where(owner == head, values, jnp.zeros_like(values))


class Panels:
    def __init__(self, place, store, recv, across, along, beside):
        self.p, self.store, self.recv = place, store, recv
        self.sx, self.sz, self.sc = across, along, beside
        p = place
        self.own = 4 * p.z + 2 * p.x + p.c
        self.nbr = 4 * p.z + 2 * (1 - p.x) + p.c

    def piece(self, which, i, send, to):
        ref = self.store.at[which, i]
        return remote(ref, ref, send, self.recv.at[which, i], to)

    def to_across(self, i):
        return self.piece(self.own, i, self.sx.at[i], self.p.across())

    def to_along(self, kind, n, i):
        which = self.own if kind == 0 else self.nbr
        return self.piece(which, i, self.sz.at[kind, n, i], self.p.along(Z_STEPS[n]))

    def to_beside(self, slot, which, i):
        return self.piece(which, i, self.sc.at[slot, i], self.p.sibling())

    def from_along(self, kind, n):
        x = self.p.x if kind == 0 else 1 - self.p.x
        return 4 * ((self.p.z - Z_STEPS[n]) % 4) + 2 * x + self.p.c

    def arrived(self, which, i):
        self.piece(which, i, self.sx.at[0], self.p.sibling()).wait_recv()

    def own_across(self, i):
        self.to_across(i).start()

    def own_along(self, i):
        for n in range(3):
            self.to_along(0, n, i).start()
        self.to_beside(0, self.own, i).start()

    def nbr_on(self, i):
        self.arrived(self.nbr, i)
        for n in range(3):
            self.to_along(1, n, i).start()
        self.to_beside(1, self.nbr, i).start()

    def along_on(self, kind, i):
        for n in range(3):
            which = self.from_along(kind, n)
            self.arrived(which, i)
            self.to_beside(2 + 3 * kind + n, which, i).start()

    def beside_in(self, x, i):
        for u in range(4):
            self.arrived(4 * u + 2 * x + 1 - self.p.c, i)

    def drain(self, i):
        self.to_across(i).wait_send()
        for kind in range(2):
            for n in range(3):
                self.to_along(kind, n, i).wait_send()
        self.to_beside(0, self.own, i).wait_send()
        self.to_beside(1, self.nbr, i).wait_send()
        for kind in range(2):
            for n in range(3):
                self.to_beside(2 + 3 * kind + n, self.from_along(kind, n), i).wait_send()

    def kind_panels(self, j):
        return jnp.concatenate([self.store[4 * u + j // 3, j % 3] for u in range(GROUPS)], axis=0)

    def kind_columns(self, first, count, cols):
        parts = [
            self.store[4 * u + j // 3, j % 3, :, cols]
            for j in range(first, first + count)
            for u in range(GROUPS)
        ]
        return jnp.concatenate(parts, axis=0)


def gelu_parts(f):
    cdf = 0.5 * (1.0 + lax.erf(f * (2.0 ** -0.5)))
    pdf = jnp.exp(-0.5 * f * f) * (1.0 / math.sqrt(2.0 * math.pi))
    return f * cdf, cdf + f * pdf


def forward_kernel(
    lengths, tokens, cotangent, alive_row, alive_col, panels, bias_t, gains, shifts,
    low1_out, qt_out, window_out, ot_out, lse_out, hidden_out, low2_out, gt_out, dft_out, ffn_out, dn2_out, store_out,
    store, window, low1, qt, acc, top, mass, part, land, whole, g_rows, df_rows, dft, gt, dffn,
    w_recv, w_across, w_along, w_beside, kv_send, kv_recv, kv_bsend, kv_brecv, rs_send, rs_recv, ag_send, ag_recv, out_sem,
):
    p = Place()
    w = Panels(p, store, w_recv, w_across, w_along, w_beside)
    first = 1 - p.c
    p.greet()

    for i in range(3):
        store[w.own, i] = panels[i].astype(BF)

    order = (1, 2, 0)

    @pl.when((p.x == 0) & (p.c == 0))
    def _():
        for i in order:
            w.own_across(i)
            w.own_along(i)

    def norm1(r, carry):
        rows = pl.ds(pl.multiple_of(r * 32, 32), 32)
        normed, _, _ = normalize(tokens[rows, :].astype(F32), gains[0:1, :], shifts[2:3, :])
        low1[rows, :] = normed.astype(BF)
        dffn[rows, :] = (cotangent[rows, :].astype(F32) * alive_col[rows, :]).astype(BF)
        return carry

    lax.fori_loop(0, ROWS // 32, norm1, 0)

    for i in order:
        @pl.when((p.x == 1) & (p.c == 0))
        def _():
            w.nbr_on(i)
            w.along_on(1, i)

        @pl.when((p.x == 0) & (p.c == 0))
        def _():
            w.along_on(0, i)

        @pl.when(p.c == 1)
        def _():
            w.beside_in(0, i)

        made = nt(w.kind_panels(i), low1[...])
        if i == 1:
            window[0, p.c, 0:ROWS, 0:SPAN] = made.astype(BF).T
        elif i == 2:
            bias = jnp.concatenate([bias_t[HD : 2 * HD, u : u + 1] for u in range(GROUPS)], axis=0)
            window[0, p.c, 0:ROWS, SPAN : 2 * SPAN] = (made + bias).astype(BF).T
            row = jnp.broadcast_to(alive_row[...], (16, ROWS)).astype(BF)
            window[0, p.c, ROWS:EXT, 0:SPAN] = row
            window[0, p.c, ROWS:EXT, SPAN : 2 * SPAN] = jnp.zeros((16, SPAN), BF)
            mine = window.at[0, p.c]
            remote(mine, mine, kv_bsend.at[0], kv_brecv.at[0], p.sibling()).start()
            for d in (2, 1, 4, 3):
                @pl.when(p.chip + d < 8)
                def _():
                    remote(mine, window.at[d, p.c], kv_send.at[d], kv_recv.at[d], p.chip_at(d)).start()
        else:
            bias = jnp.concatenate([bias_t[0:HD, u : u + 1] for u in range(GROUPS)], axis=0)
            qt[...] = (made + bias).astype(BF)

    @pl.when(p.c == 1)
    def _():
        w.own_across(0)

        @pl.when(p.x == 0)
        def _():
            w.own_along(0)

    @pl.when((p.c == 0) & (p.x == 1))
    def _():
        w.own_across(0)

    @pl.when((p.c == 1) | (p.x == 1))
    def _():
        for i in (1, 2):
            w.own_across(i)

    acc[...] = jnp.zeros_like(acc)
    top[...] = jnp.full_like(top, FLOOR)
    mass[...] = jnp.zeros_like(mass)
    code, at = query_code(p, lengths, alive_row[...])
    scaled = (qt[...].astype(F32) * (HD ** -0.5)).astype(BF)

    def attend(d, core):
        bias = block_bias(p, lengths, window, d, core, code, at)
        keys = window[d, core, 0:ROWS, 0:SPAN]
        values_t = window[d, core, 0:ROWS, SPAN : 2 * SPAN].T
        for u in range(GROUPS):
            heads = slice(u * HD, (u + 1) * HD)
            score = nn(keys, head_rows(scaled, u)) + bias
            old = top[u : u + 1, :]
            new = jnp.maximum(old, jnp.max(score, axis=0, keepdims=True))
            weight = jnp.exp(score - new)
            fade = jnp.exp(old - new)
            top[u : u + 1, :] = new
            mass[u : u + 1, :] = mass[u : u + 1, :] * fade + jnp.sum(weight, axis=0, keepdims=True)
            acc[heads, :] = acc[heads, :] * fade + nn(values_t[heads, :], weight.astype(BF))

    def attend_chip(d):
        def body(core, carry):
            use = (p.chip - d >= 0) & ~((d == 0) & (core > p.c)) & ~((d == 4) & (core < p.c))

            @pl.when(use)
            def _():
                attend(d, core)

            return carry

        lax.fori_loop(0, 2, body, 0)

    def kv_in(d):
        @pl.when(p.chip - d >= 0)
        def _():
            got = window.at[d, p.c]
            remote(got, got, kv_send.at[d], kv_recv.at[d], p.sibling()).wait_recv()
            remote(got, got, kv_bsend.at[d], kv_brecv.at[d], p.sibling()).start()

    def kv_beside(d):
        @pl.when(p.chip - d >= 0)
        def _():
            got = window.at[d, 1 - p.c]
            remote(got, got, kv_bsend.at[d], kv_brecv.at[d], p.sibling()).wait_recv()

    kv_beside(0)
    kv_in(1)
    attend_chip(0)

    @pl.when((p.c == 1) & (p.x == 1))
    def _():
        w.nbr_on(0)

    kv_beside(1)
    kv_in(2)
    attend_chip(1)
    kv_beside(2)
    kv_in(3)
    attend_chip(2)
    kv_beside(3)
    kv_in(4)

    @pl.when((p.c == 1) & (p.x == 1))
    def _():
        w.own_along(0)

    @pl.when((p.c == 0) & (p.x == 1))
    def _():
        w.own_along(0)

    @pl.when((p.c == 1) | (p.x == 1))
    def _():
        for i in (1, 2):
            w.own_along(i)

    attend_chip(3)
    kv_beside(4)

    @pl.when(p.c == 1)
    def _():
        @pl.when(p.x == 0)
        def _():
            w.along_on(0, 0)

        @pl.when(p.x == 1)
        def _():
            w.along_on(1, 0)

    attend_chip(4)

    total = jnp.maximum(mass[...], 1e-30)
    lse_out[...] = top[...] + jnp.log(total)
    for u in range(GROUPS):
        heads = slice(u * HD, (u + 1) * HD)
        acc[heads, :] = acc[heads, :] / total[u : u + 1, :]
    ot_out[...] = acc[...]
    o_rows = acc[...].astype(BF).T

    @pl.when(p.c == 0)
    def _():
        w.beside_in(0, 0)

    def project(n, carry):
        cols = pl.ds(pl.multiple_of(n * 256, 256), 256)
        part[:, cols] = nn(o_rows, w.kind_columns(3, 1, cols)).astype(BF)
        return carry

    lax.fori_loop(0, WIDTH // 256, project, 0)
    scatter = scatter_copies(p, part, land, rs_send, rs_recv)
    for copy in scatter:
        copy.start()

    @pl.when((p.c == 0) & (p.x == 0))
    def _():
        w.nbr_on(0)

    @pl.when((p.c == 1) & (p.x == 0))
    def _():
        w.nbr_on(0)

    @pl.when((p.c == 1) | (p.x == 0))
    def _():
        for i in (1, 2):
            w.nbr_on(i)

    for copy in scatter:
        copy.wait()
    mine = pl.ds(pl.multiple_of(p.t * SHARD, SHARD), SHARD)
    summed = scatter_sum(p, part, land)
    hidden = tokens[mine, :].astype(F32) + alive_col[mine, :] * (summed + shifts[0:1, :])
    hidden_out[...] = hidden
    normed, _, _ = normalize(hidden, gains[1:2, :], shifts[3:4, :])
    whole[mine, :] = normed.astype(BF)
    gather = gather_copies(p, whole, ag_send, ag_recv)
    for copy in gather:
        copy.start()

    @pl.when((p.c == 1) & (p.x == 0))
    def _():
        w.along_on(1, 0)

    @pl.when((p.c == 1) & (p.x == 1))
    def _():
        w.along_on(0, 0)

    @pl.when((p.c == 0) & (p.x == 0))
    def _():
        w.along_on(1, 0)

    @pl.when((p.c == 0) & (p.x == 1))
    def _():
        w.along_on(0, 0)

    for i in (1, 2):
        @pl.when((p.c == 1) | (p.x == 1))
        def _():
            w.along_on(0, i)

        @pl.when((p.c == 1) | (p.x == 0))
        def _():
            w.along_on(1, i)

    for copy in gather:
        copy.wait()

    @pl.when(p.c == 0)
    def _():
        w.beside_in(0, 1)
        w.beside_in(0, 2)

    for i in range(3):
        w.beside_in(1, i)

    out_copies = [
        pltpu.make_async_copy(store, store_out, out_sem.at[0]),
        pltpu.make_async_copy(window, window_out, out_sem.at[1]),
        pltpu.make_async_copy(whole, low2_out, out_sem.at[2]),
        pltpu.make_async_copy(low1, low1_out, out_sem.at[3]),
        pltpu.make_async_copy(qt, qt_out, out_sem.at[4]),
    ]
    for copy in out_copies:
        copy.start()

    for n in range(4):
        pre = nt(w.kind_panels(4 + n), whole[...])
        at_bias = 2 * HD + n * HD
        pre = pre + jnp.concatenate([bias_t[at_bias : at_bias + HD, u : u + 1] for u in range(GROUPS)], axis=0)
        value, slope = gelu_parts(pre)
        d_act = nt(w.kind_panels(8 + n), dffn[...])
        low_value, low_grad = value.astype(BF), (d_act * slope).astype(BF)
        units = slice(n * SPAN, (n + 1) * SPAN)
        gt[units, :] = low_value
        dft[units, :] = low_grad
        g_rows[:, units] = low_value.T
        df_rows[:, units] = low_grad.T
    gt_out[...] = gt[...]
    dft_out[...] = dft[...]

    def feed(n, carry):
        cols = pl.ds(pl.multiple_of(n * 256, 256), 256)
        dn2_out[:, cols] = nn(df_rows[...], w.kind_columns(4, 4, cols)).astype(BF)
        ffn_out[:, cols] = nn(g_rows[...], w.kind_columns(8, 4, cols)).astype(BF)
        return carry

    lax.fori_loop(0, WIDTH // 256, feed, 0)

    for i in range(3):
        w.drain(i)
    mine_kv = window.at[0, p.c]
    for d in range(1, 5):
        @pl.when(p.chip + d < 8)
        def _():
            remote(mine_kv, mine_kv, kv_send.at[d], kv_recv.at[d], p.sibling()).wait_send()
    for d in range(5):
        @pl.when(p.chip - d >= 0)
        def _():
            remote(mine_kv, mine_kv, kv_bsend.at[d], kv_brecv.at[d], p.sibling()).wait_send()
    for copy in out_copies:
        copy.wait()


def forward_call(lengths, tokens, cotangent, alive_row, alive_col, panels, bias_t, gains, shifts):
    vmem = pl.BlockSpec(memory_space=pltpu.VMEM)
    anywhere = pl.BlockSpec(memory_space=pl.ANY)
    shape = jax.ShapeDtypeStruct
    dma = pltpu.SemaphoreType.DMA
    return pl.pallas_call(
        forward_kernel,
        in_specs=[pl.BlockSpec(memory_space=pltpu.SMEM)] + [vmem] * 8,
        out_specs=[anywhere, anywhere, anywhere, vmem, vmem, vmem, anywhere, vmem, vmem, vmem, vmem, anywhere],
        out_shape=[
            shape((ROWS, WIDTH), BF),
            shape((SPAN, ROWS), BF),
            shape((5, 2, EXT, 2 * SPAN), BF),
            shape((SPAN, ROWS), F32),
            shape((8, ROWS), F32),
            shape((SHARD, WIDTH), F32),
            shape((ROWS, WIDTH), BF),
            shape((UNITS, ROWS), BF),
            shape((UNITS, ROWS), BF),
            shape((ROWS, WIDTH), BF),
            shape((ROWS, WIDTH), BF),
            shape((16, 3, HD, WIDTH), BF),
        ],
        scratch_shapes=[
            pltpu.VMEM((16, 3, HD, WIDTH), BF),
            pltpu.VMEM((5, 2, EXT, 2 * SPAN), BF),
            pltpu.VMEM((ROWS, WIDTH), BF),
            pltpu.VMEM((SPAN, ROWS), BF),
            pltpu.VMEM((SPAN, ROWS), F32),
            pltpu.VMEM((8, ROWS), F32),
            pltpu.VMEM((8, ROWS), F32),
            pltpu.VMEM((ROWS, WIDTH), BF),
            pltpu.VMEM((7, SHARD, WIDTH), BF),
            pltpu.VMEM((ROWS, WIDTH), BF),
            pltpu.VMEM((ROWS, UNITS), BF),
            pltpu.VMEM((ROWS, UNITS), BF),
            pltpu.VMEM((UNITS, ROWS), BF),
            pltpu.VMEM((UNITS, ROWS), BF),
            pltpu.VMEM((ROWS, WIDTH), BF),
            dma((16, 3)), dma((3,)), dma((2, 3, 3)), dma((8, 3)),
            dma((5,)), dma((5,)), dma((5,)), dma((5,)),
            dma((7,)), dma((7,)), dma((7,)), dma((7,)), dma((5,)),
        ],
        compiler_params=pltpu.CompilerParams(
            collective_id=0, has_side_effects=True, vmem_limit_bytes=56 * 2**20
        ),
        name="layer_forward",
    )(lengths, tokens, cotangent, alive_row, alive_col, panels, bias_t, gains, shifts)


def times_t(left, right):
    return nt(left, right)


def inner_rows(left, right):
    return lax.dot_general(left, right, (((0,), (0,)), ((), ())), preferred_element_type=F32)


plain = nn


def norm_back(grad, unit, factor, gain):
    d_gain = jnp.sum(grad * unit, axis=0)
    d_shift = jnp.sum(grad, axis=0)
    d_unit = grad * gain
    d_in = factor * (
        d_unit
        - jnp.mean(d_unit, axis=-1, keepdims=True)
        - unit * jnp.mean(d_unit * unit, axis=-1, keepdims=True)
    )
    return (d_in, d_gain, d_shift)


def orthogonalize(moment):
    current = moment * lax.rsqrt(jnp.sum(moment * moment, axis=(1, 2), keepdims=True) + 1e-06)
    for sweep in range(NS_ITERS):
        gram = jnp.einsum("pij,pkj->pik", current, current, precision=HIGH)
        poly = NS_B * gram + NS_C * jnp.einsum("pij,pjk->pik", gram, gram, precision=HIGH)
        current = NS_A * current + jnp.einsum("pij,pjk->pik", poly, current, precision=HIGH)
    return current


def per_device(
    tokens, cotangent, exits, lengths, panels, panel_mom,
    unit_bias, unit_bias_mom, gains, gains_mom, vec_bias, vec_bias_mom,
):
    rows, width = tokens.shape
    groups, head_dim = GROUPS, HD
    total = rows * lax.axis_size("seq")
    scale = head_dim ** (-0.5)
    live = (exits >= LAYER).astype(F32)[:, None]
    alive = (exits >= LAYER).astype(jnp.int32)
    positions = lax.axis_index("seq") * rows + jnp.arange(rows, dtype=jnp.int32)
    ends = jnp.cumsum(lengths)
    segment = jnp.sum((positions[:, None] >= ends[None, :]).astype(jnp.int32), axis=1)
    block = math.gcd(total, 512)
    count = total // block
    begins = jnp.arange(count, dtype=jnp.int32) * block
    low1, qt, window, ot, lse, hidden32, low2, gt, dft, ffn_part, dn2_part, store = forward_call(
        lengths, tokens, cotangent, live.reshape(1, rows), live, panels, unit_bias.T, gains, vec_bias
    )
    core = lax.axis_index("seq") % 2
    mine_kv = lax.dynamic_index_in_dim(window[0], core, 0, keepdims=False)
    keys, values = mine_kv[:rows, :SPAN], mine_kv[:rows, SPAN:]
    query = qt.T
    q_heads = query.reshape(rows, groups, head_dim)
    log_total = lse[:groups]
    attn_full = ot.T.reshape(rows, groups, head_dim)
    attn_low = ot.T.astype(BF)
    stack = store.reshape(groups, 12, head_dim, width)
    w_query = stack[:, 0].reshape(groups * head_dim, width)
    w_key = stack[:, 1].reshape(groups * head_dim, width)
    w_value = stack[:, 2].reshape(groups * head_dim, width)
    w_out = stack[:, 3].reshape(groups * head_dim, width)
    x_full = tokens.astype(F32)
    _, unit1, factor1 = normalize(x_full, gains[0], vec_bias[2])
    hidden = lax.all_gather(hidden32, "tensor", axis=0, tiled=True)
    _, unit2, factor2 = normalize(hidden, gains[1], vec_bias[3])
    ffn_whole = lax.psum(ffn_part, "tensor").astype(F32)
    output = hidden + live * (ffn_whole + vec_bias[1])
    grad_out = cotangent.astype(F32)
    d_ffn = (live * grad_out).astype(BF)
    d_b2 = jnp.sum(d_ffn.astype(F32), axis=0)
    d_w_back = nn(gt, d_ffn).reshape(4, groups, head_dim, width).transpose(1, 0, 2, 3)
    d_b1 = jnp.sum(dft.astype(F32), axis=1).reshape(4, groups, head_dim).transpose(1, 0, 2)
    d_w_in = nn(dft, low2).reshape(4, groups, head_dim, width).transpose(1, 0, 2, 3)
    d_norm2 = lax.psum(dn2_part, "tensor").astype(F32)
    d_hidden_norm, d_gain2, d_shift2 = norm_back(d_norm2, unit2, factor2, gains[1])
    d_hidden = grad_out + d_hidden_norm
    d_branch = (live * d_hidden).astype(BF)
    d_bo = jnp.sum(d_branch.astype(F32), axis=0)
    d_w_out = inner_rows(attn_low, d_branch)
    d_attn = times_t(d_branch, w_out).astype(BF)
    d_heads = d_attn.reshape(rows, groups, head_dim)
    delta = jnp.einsum("qhe,qhe->hq", d_heads.astype(F32), attn_full)
    all_keys, all_values, all_seg, all_alive = (
        lax.all_gather(keys, "seq", axis=0, tiled=True),
        lax.all_gather(values, "seq", axis=0, tiled=True),
        lax.all_gather(segment, "seq", axis=0, tiled=True),
        lax.all_gather(alive, "seq", axis=0, tiled=True),
    )

    def back_block(d_query, blocked):
        k_blk, v_blk, s_blk, a_blk, begin = blocked
        k_pos = begin + jnp.arange(block, dtype=jnp.int32)
        allowed = (segment[:, None] == s_blk[None, :]) & (positions[:, None] >= k_pos[None, :])
        allowed = allowed & (alive[:, None] > 0) & (a_blk[None, :] > 0)
        k_h = k_blk.reshape(block, groups, head_dim)
        v_h = v_blk.reshape(block, groups, head_dim)
        score = jnp.einsum("qhe,khe->hqk", q_heads, k_h, preferred_element_type=F32) * scale
        prob = jnp.where(allowed[None], jnp.exp(score - log_total[:, :, None]), 0.0)
        d_val = jnp.einsum("hqk,qhe->khe", prob.astype(BF), d_heads, preferred_element_type=F32)
        d_prob = jnp.einsum("qhe,khe->hqk", d_heads, v_h, preferred_element_type=F32)
        d_score = (prob * (d_prob - delta[:, :, None])).astype(BF)
        d_query = d_query + jnp.einsum("hqk,khe->qhe", d_score, k_h, preferred_element_type=F32)
        d_key = jnp.einsum("hqk,qhe->khe", d_score, q_heads, preferred_element_type=F32)
        return (d_query, (d_key.reshape(block, SPAN), d_val.reshape(block, SPAN)))

    blocked_in = (
        all_keys.reshape(count, block, -1),
        all_values.reshape(count, block, -1),
        all_seg.reshape(count, block),
        all_alive.reshape(count, block),
        begins,
    )
    d_query, (d_key_all, d_val_all) = lax.scan(
        back_block, jnp.zeros((rows, groups, head_dim), F32), blocked_in
    )
    d_key_all = d_key_all.reshape(total, SPAN) * scale
    d_val_all = d_val_all.reshape(total, SPAN)
    d_key_mine, d_val_mine = (
        lax.psum_scatter(d_key_all.astype(BF), "seq", scatter_dimension=0, tiled=True).astype(F32),
        lax.psum_scatter(d_val_all.astype(BF), "seq", scatter_dimension=0, tiled=True).astype(F32),
    )
    d_q = (d_query.reshape(rows, SPAN) * scale).astype(BF)
    d_k = d_key_mine.astype(BF)
    d_v = d_val_mine.astype(BF)
    d_bq = jnp.sum(d_q.astype(F32), axis=0)
    d_bv = jnp.sum(d_v.astype(F32), axis=0)
    d_w_query = inner_rows(d_q, low1)
    d_w_key = inner_rows(d_k, low1)
    d_w_value = inner_rows(d_v, low1)
    d_norm1_part = plain(d_q, w_query) + plain(d_k, w_key) + plain(d_v, w_value)
    d_norm1 = lax.psum(d_norm1_part.astype(BF), "tensor").astype(F32)
    d_input_norm, d_gain1, d_shift1 = norm_back(d_norm1, unit1, factor1, gains[0])
    input_grad = d_hidden + d_input_norm
    grad_stack = jnp.concatenate(
        [
            d_w_query.reshape(groups, 1, head_dim, width),
            d_w_key.reshape(groups, 1, head_dim, width),
            d_w_value.reshape(groups, 1, head_dim, width),
            d_w_out.reshape(groups, 1, head_dim, width),
            d_w_in,
            d_w_back,
        ],
        axis=1,
    ).reshape(groups * 12, head_dim, width)
    unit_grad = jnp.concatenate(
        [
            d_bq.reshape(groups, head_dim),
            d_bv.reshape(groups, head_dim),
            d_b1.reshape(groups, 4 * head_dim),
        ],
        axis=1,
    )
    gain_grad = jnp.stack([d_gain1, d_gain2])
    shift_grad = jnp.stack([d_bo, d_b2, d_shift1, d_shift2])
    unit_sum, gain_sum, shift_sum = (
        lax.psum(unit_grad.astype(BF), "seq").astype(F32),
        lax.psum(gain_grad.astype(BF), "seq").astype(F32),
        lax.psum(shift_grad.astype(BF), "seq").astype(F32),
    )
    mine = lax.psum_scatter(grad_stack.astype(BF), "seq", scatter_dimension=0, tiled=True).astype(F32)
    moment = DECAY * panel_mom + mine
    direction = orthogonalize(moment)
    size_w = jnp.sum(panels * panels, axis=(1, 2), keepdims=True)
    size_u = jnp.sum(direction * direction, axis=(1, 2), keepdims=True)
    new_panels = panels - LR_MATRIX * jnp.sqrt(size_w) * lax.rsqrt(size_u + 1e-06) * direction
    unit_moment = DECAY * unit_bias_mom + unit_sum
    gains_moment = DECAY * gains_mom + gain_sum
    vec_moment = DECAY * vec_bias_mom + shift_sum
    return (
        output.astype(BF), input_grad, new_panels, moment,
        unit_bias - LR_VECTOR * unit_moment, unit_moment,
        gains - LR_VECTOR * gains_moment, gains_moment,
        vec_bias - LR_VECTOR * vec_moment, vec_moment,
    )


def solution(mesh):
    held = P(("tensor", "seq"), None, None)
    return jax.shard_map(
        per_device,
        mesh=mesh,
        in_specs=(
            P("seq", None), P("seq", None), P("seq"), P(), held, held,
            P("tensor", None), P("tensor", None), P(), P(), P(), P(),
        ),
        out_specs=(
            P("seq", None), P("seq", None), held, held,
            P("tensor", None), P("tensor", None), P(), P(), P(), P(),
        ),
        check_vma=False,
    )
```

```python
import functools
import math

import jax
import jax.numpy as jnp
from jax import lax
from jax.experimental import pallas as pl
from jax.experimental.pallas import tpu as pltpu
from jax.sharding import PartitionSpec as P

LAYER = 12
NS_ITERS = 5
EPS = 1e-05
NS_A = 3.4445
NS_B = -4.775
NS_C = 2.0315
LR_MATRIX = 0.5
LR_VECTOR = 0.002
DECAY = 0.5
HIGH = lax.Precision.HIGHEST
MESH = pl.DeviceIdType.MESH

ROWS = 256
WIDTH = 2048
GROUPS = 4
HD = 64
SPAN = GROUPS * HD
UNITS = 4 * SPAN
SHARD = 32
EXT = ROWS + 16
MASKED = -1e30
FLOOR = -1e28
BF = jnp.bfloat16
F32 = jnp.float32

Z_STEPS = (1, 3, 2)
T_STEPS = tuple((dy, dx) for dy in (2, 1, 3, 0) for dx in (1, 0) if (dy, dx) != (0, 0))


def nt(left, right):
    return lax.dot_general(left, right, (((1,), (1,)), ((), ())), preferred_element_type=F32)


def nn(left, right):
    return jnp.dot(left, right, preferred_element_type=F32)


def normalize(values, gain, shift):
    mean = jnp.mean(values, axis=-1, keepdims=True)
    centred = values - mean
    factor = lax.rsqrt(jnp.mean(centred * centred, axis=-1, keepdims=True) + EPS)
    return centred * factor * gain + shift, centred * factor, factor


class Place:
    def __init__(self):
        self.s = lax.axis_index("seq")
        self.t = lax.axis_index("tensor")
        self.z, self.x, self.c = self.s // 4, (self.s // 2) % 2, self.s % 2
        self.chip = self.s // 2
        self.y, self.h = self.t // 2, self.t % 2

    def seq(self, z, x, c):
        return {"seq": z * 4 + x * 2 + c}

    def sibling(self):
        return self.seq(self.z, self.x, 1 - self.c)

    def across(self):
        return self.seq(self.z, 1 - self.x, self.c)

    def along(self, step):
        return self.seq((self.z + step) % 4, self.x, self.c)

    def chip_at(self, step):
        return {"seq": (self.chip + step) * 2 + self.c}

    def tensor_at(self, dy, dx):
        return ((self.y + dy) % 4) * 2 + (self.h + dx) % 2

    def greet(self):
        barrier = pltpu.get_barrier_semaphore()
        count = 0
        for dz in range(4):
            for dx in range(2):
                if (dz, dx) != (0, 0):
                    to = self.seq((self.z + dz) % 4, (self.x + dx) % 2, self.c)
                    pl.semaphore_signal(barrier, inc=1, device_id=to, device_id_type=MESH)
                    count += 1
        pl.semaphore_signal(barrier, inc=1, device_id=self.sibling(), device_id_type=MESH)
        count += 1
        for dy, dx in T_STEPS:
            to = {"tensor": self.tensor_at(dy, dx)}
            pl.semaphore_signal(barrier, inc=1, device_id=to, device_id_type=MESH)
            count += 1
        pl.semaphore_wait(barrier, count)


def remote(src, dst, send, recv, to):
    return pltpu.make_async_remote_copy(
        src_ref=src, dst_ref=dst, send_sem=send, recv_sem=recv, device_id=to, device_id_type=MESH
    )


def scatter_copies(place, part, land, send, recv):
    out = []
    for i, (dy, dx) in enumerate(T_STEPS):
        to = place.tensor_at(dy, dx)
        rows = pl.ds(pl.multiple_of(to * SHARD, SHARD), SHARD)
        out.append(remote(part.at[rows], land.at[i], send.at[i], recv.at[i], {"tensor": to}))
    return out


def scatter_sum(place, part, land):
    mine = pl.ds(pl.multiple_of(place.t * SHARD, SHARD), SHARD)
    total = part[mine, :].astype(F32)
    for i in range(len(T_STEPS)):
        total = total + land[i].astype(F32)
    return total


def gather_copies(place, whole, send, recv):
    mine = pl.ds(pl.multiple_of(place.t * SHARD, SHARD), SHARD)
    out = []
    for i, (dy, dx) in enumerate(T_STEPS):
        to = place.tensor_at(dy, dx)
        out.append(remote(whole.at[mine], whole.at[mine], send.at[i], recv.at[i], {"tensor": to}))
    return out


def column_of(row):
    n = row.shape[1]
    down = lax.broadcasted_iota(jnp.int32, (n, n), 0)
    over = lax.broadcasted_iota(jnp.int32, (n, n), 1)
    return jnp.sum(jnp.where(down == over, row, 0.0), axis=1, keepdims=True)


def segment_of(positions, lengths):
    end = jnp.int32(0)
    segment = jnp.zeros(positions.shape, F32)
    for i in range(4):
        end = end + lengths[i]
        segment = segment + jnp.where(positions >= end, 1.0, 0.0)
    return segment


def query_code(place, lengths, alive_row):
    at = place.s * ROWS + lax.broadcasted_iota(jnp.int32, (1, ROWS), 1)
    return jnp.where(alive_row > 0.5, segment_of(at, lengths), -2.0), at


def block_bias(place, lengths, window, dist, core, code, at):
    first = ((place.chip - dist) * 2 + core) * ROWS
    keys = first + lax.broadcasted_iota(jnp.int32, (ROWS, 1), 0)
    live = column_of(window[dist, core, ROWS:EXT, 0:ROWS].astype(F32)[0:1])
    key_code = jnp.where(live > 0.5, segment_of(keys, lengths), -1.0)
    same = jnp.where(key_code == code, 0.0, MASKED)
    return jnp.where(keys <= at, same, MASKED)


def head_rows(values, head):
    owner = lax.broadcasted_iota(jnp.int32, values.shape, 0) // HD
    return jnp.where(owner == head, values, jnp.zeros_like(values))


class Panels:
    def __init__(self, place, store, recv, across, along, beside):
        self.p, self.store, self.recv = place, store, recv
        self.sx, self.sz, self.sc = across, along, beside
        p = place
        self.own = 4 * p.z + 2 * p.x + p.c
        self.nbr = 4 * p.z + 2 * (1 - p.x) + p.c

    def piece(self, which, i, send, to):
        ref = self.store.at[which, i]
        return remote(ref, ref, send, self.recv.at[which, i], to)

    def to_across(self, i):
        return self.piece(self.own, i, self.sx.at[i], self.p.across())

    def to_along(self, kind, n, i):
        which = self.own if kind == 0 else self.nbr
        return self.piece(which, i, self.sz.at[kind, n, i], self.p.along(Z_STEPS[n]))

    def to_beside(self, slot, which, i):
        return self.piece(which, i, self.sc.at[slot, i], self.p.sibling())

    def from_along(self, kind, n):
        x = self.p.x if kind == 0 else 1 - self.p.x
        return 4 * ((self.p.z - Z_STEPS[n]) % 4) + 2 * x + self.p.c

    def arrived(self, which, i):
        self.piece(which, i, self.sx.at[0], self.p.sibling()).wait_recv()

    def own_across(self, i):
        self.to_across(i).start()

    def own_along(self, i):
        for n in range(3):
            self.to_along(0, n, i).start()
        self.to_beside(0, self.own, i).start()

    def nbr_on(self, i):
        self.arrived(self.nbr, i)
        for n in range(3):
            self.to_along(1, n, i).start()
        self.to_beside(1, self.nbr, i).start()

    def along_on(self, kind, i):
        for n in range(3):
            which = self.from_along(kind, n)
            self.arrived(which, i)
            self.to_beside(2 + 3 * kind + n, which, i).start()

    def beside_in(self, x, i):
        for u in range(4):
            self.arrived(4 * u + 2 * x + 1 - self.p.c, i)

    def drain(self, i):
        self.to_across(i).wait_send()
        for kind in range(2):
            for n in range(3):
                self.to_along(kind, n, i).wait_send()
        self.to_beside(0, self.own, i).wait_send()
        self.to_beside(1, self.nbr, i).wait_send()
        for kind in range(2):
            for n in range(3):
                self.to_beside(2 + 3 * kind + n, self.from_along(kind, n), i).wait_send()

    def kind_panels(self, j):
        return jnp.concatenate([self.store[4 * u + j // 3, j % 3] for u in range(GROUPS)], axis=0)

    def kind_columns(self, first, count, cols):
        parts = [
            self.store[4 * u + j // 3, j % 3, :, cols]
            for j in range(first, first + count)
            for u in range(GROUPS)
        ]
        return jnp.concatenate(parts, axis=0)


def gelu_parts(f):
    cdf = 0.5 * (1.0 + lax.erf(f * (2.0 ** -0.5)))
    pdf = jnp.exp(-0.5 * f * f) * (1.0 / math.sqrt(2.0 * math.pi))
    return f * cdf, cdf + f * pdf


def forward_kernel(
    lengths, tokens, cotangent, alive_row, alive_col, panels, bias_t, gains, shifts,
    low1_out, qt_out, window_out, ot_out, lse_out, hidden_out, low2_out, gt_out, dft_out, ffn_out, dn2_out, proj_out,
    dffn_out, unit_out,
    store, window, low1, qt, acc, top, mass, part, land, whole, g_rows, df_rows, dft, gt, dffn,
    w_recv, w_across, w_along, w_beside, kv_send, kv_recv, kv_bsend, kv_brecv, rs_send, rs_recv, ag_send, ag_recv, out_sem,
):
    p = Place()
    w = Panels(p, store, w_recv, w_across, w_along, w_beside)
    first = 1 - p.c
    p.greet()

    for i in range(3):
        store[w.own, i] = panels[i].astype(BF)

    order = (1, 2, 0)

    @pl.when((p.x == 0) & (p.c == 0))
    def _():
        for i in order:
            w.own_across(i)
            w.own_along(i)

    def norm1(r, carry):
        rows = pl.ds(pl.multiple_of(r * 32, 32), 32)
        normed, _, _ = normalize(tokens[rows, :].astype(F32), gains[0:1, :], shifts[2:3, :])
        low1[rows, :] = normed.astype(BF)
        dffn[rows, :] = (cotangent[rows, :].astype(F32) * alive_col[rows, :]).astype(BF)
        return carry

    lax.fori_loop(0, ROWS // 32, norm1, 0)

    for i in order:
        @pl.when((p.x == 1) & (p.c == 0))
        def _():
            w.nbr_on(i)
            w.along_on(1, i)

        @pl.when((p.x == 0) & (p.c == 0))
        def _():
            w.along_on(0, i)

        @pl.when(p.c == 1)
        def _():
            w.beside_in(0, i)

        made = nt(w.kind_panels(i), low1[...])
        if i == 1:
            window[0, p.c, 0:ROWS, 0:SPAN] = made.astype(BF).T
        elif i == 2:
            bias = jnp.concatenate([bias_t[HD : 2 * HD, u : u + 1] for u in range(GROUPS)], axis=0)
            window[0, p.c, 0:ROWS, SPAN : 2 * SPAN] = (made + bias).astype(BF).T
            row = jnp.broadcast_to(alive_row[...], (16, ROWS)).astype(BF)
            window[0, p.c, ROWS:EXT, 0:SPAN] = row
            window[0, p.c, ROWS:EXT, SPAN : 2 * SPAN] = jnp.zeros((16, SPAN), BF)
            mine = window.at[0, p.c]
            remote(mine, mine, kv_bsend.at[0], kv_brecv.at[0], p.sibling()).start()
            for d in (2, 1, 4, 3):
                @pl.when(p.chip + d < 8)
                def _():
                    remote(mine, window.at[d, p.c], kv_send.at[d], kv_recv.at[d], p.chip_at(d)).start()
        else:
            bias = jnp.concatenate([bias_t[0:HD, u : u + 1] for u in range(GROUPS)], axis=0)
            qt[...] = (made + bias).astype(BF)

    @pl.when(p.c == 1)
    def _():
        w.own_across(0)

        @pl.when(p.x == 0)
        def _():
            w.own_along(0)

    @pl.when((p.c == 0) & (p.x == 1))
    def _():
        w.own_across(0)

    @pl.when((p.c == 1) | (p.x == 1))
    def _():
        for i in (1, 2):
            w.own_across(i)

    acc[...] = jnp.zeros_like(acc)
    top[...] = jnp.full_like(top, FLOOR)
    mass[...] = jnp.zeros_like(mass)
    code, at = query_code(p, lengths, alive_row[...])
    scaled = (qt[...].astype(F32) * (HD ** -0.5)).astype(BF)

    def attend(d, core):
        bias = block_bias(p, lengths, window, d, core, code, at)
        keys = window[d, core, 0:ROWS, 0:SPAN]
        values_t = window[d, core, 0:ROWS, SPAN : 2 * SPAN].T
        for u in range(GROUPS):
            heads = slice(u * HD, (u + 1) * HD)
            score = nn(keys, head_rows(scaled, u)) + bias
            old = top[u : u + 1, :]
            new = jnp.maximum(old, jnp.max(score, axis=0, keepdims=True))
            weight = jnp.exp(score - new)
            fade = jnp.exp(old - new)
            top[u : u + 1, :] = new
            mass[u : u + 1, :] = mass[u : u + 1, :] * fade + jnp.sum(weight, axis=0, keepdims=True)
            acc[heads, :] = acc[heads, :] * fade + nn(values_t[heads, :], weight.astype(BF))

    def attend_chip(d):
        def body(core, carry):
            use = (p.chip - d >= 0) & ~((d == 0) & (core > p.c)) & ~((d == 4) & (core < p.c))

            @pl.when(use)
            def _():
                attend(d, core)

            return carry

        lax.fori_loop(0, 2, body, 0)

    def kv_in(d):
        @pl.when(p.chip - d >= 0)
        def _():
            got = window.at[d, p.c]
            remote(got, got, kv_send.at[d], kv_recv.at[d], p.sibling()).wait_recv()
            remote(got, got, kv_bsend.at[d], kv_brecv.at[d], p.sibling()).start()

    def kv_beside(d):
        @pl.when(p.chip - d >= 0)
        def _():
            got = window.at[d, 1 - p.c]
            remote(got, got, kv_bsend.at[d], kv_brecv.at[d], p.sibling()).wait_recv()

    kv_beside(0)
    kv_in(1)
    attend_chip(0)

    @pl.when((p.c == 1) & (p.x == 1))
    def _():
        w.nbr_on(0)

    kv_beside(1)
    kv_in(2)
    attend_chip(1)
    kv_beside(2)
    kv_in(3)
    attend_chip(2)
    kv_beside(3)
    kv_in(4)

    @pl.when((p.c == 1) & (p.x == 1))
    def _():
        w.own_along(0)

    @pl.when((p.c == 0) & (p.x == 1))
    def _():
        w.own_along(0)

    @pl.when((p.c == 1) | (p.x == 1))
    def _():
        for i in (1, 2):
            w.own_along(i)

    attend_chip(3)
    kv_beside(4)

    @pl.when(p.c == 1)
    def _():
        @pl.when(p.x == 0)
        def _():
            w.along_on(0, 0)

        @pl.when(p.x == 1)
        def _():
            w.along_on(1, 0)

    attend_chip(4)

    total = jnp.maximum(mass[...], 1e-30)
    lse_out[...] = top[...] + jnp.log(total)
    for u in range(GROUPS):
        heads = slice(u * HD, (u + 1) * HD)
        acc[heads, :] = acc[heads, :] / total[u : u + 1, :]
    ot_out[...] = acc[...]
    o_rows = acc[...].astype(BF).T

    @pl.when(p.c == 0)
    def _():
        w.beside_in(0, 0)

    def project(n, carry):
        cols = pl.ds(pl.multiple_of(n * 256, 256), 256)
        part[:, cols] = nn(o_rows, w.kind_columns(3, 1, cols)).astype(BF)
        return carry

    lax.fori_loop(0, WIDTH // 256, project, 0)
    scatter = scatter_copies(p, part, land, rs_send, rs_recv)
    for copy in scatter:
        copy.start()

    @pl.when((p.c == 0) & (p.x == 0))
    def _():
        w.nbr_on(0)

    @pl.when((p.c == 1) & (p.x == 0))
    def _():
        w.nbr_on(0)

    @pl.when((p.c == 1) | (p.x == 0))
    def _():
        for i in (1, 2):
            w.nbr_on(i)

    for copy in scatter:
        copy.wait()
    mine = pl.ds(pl.multiple_of(p.t * SHARD, SHARD), SHARD)
    summed = scatter_sum(p, part, land)
    hidden = tokens[mine, :].astype(F32) + alive_col[mine, :] * (summed + shifts[0:1, :])
    hidden_out[...] = hidden
    normed, _, _ = normalize(hidden, gains[1:2, :], shifts[3:4, :])
    whole[mine, :] = normed.astype(BF)
    gather = gather_copies(p, whole, ag_send, ag_recv)
    for copy in gather:
        copy.start()

    @pl.when((p.c == 1) & (p.x == 0))
    def _():
        w.along_on(1, 0)

    @pl.when((p.c == 1) & (p.x == 1))
    def _():
        w.along_on(0, 0)

    @pl.when((p.c == 0) & (p.x == 0))
    def _():
        w.along_on(1, 0)

    @pl.when((p.c == 0) & (p.x == 1))
    def _():
        w.along_on(0, 0)

    for i in (1, 2):
        @pl.when((p.c == 1) | (p.x == 1))
        def _():
            w.along_on(0, i)

        @pl.when((p.c == 1) | (p.x == 0))
        def _():
            w.along_on(1, i)

    for copy in gather:
        copy.wait()

    @pl.when(p.c == 0)
    def _():
        w.beside_in(0, 1)
        w.beside_in(0, 2)

    for i in range(3):
        w.beside_in(1, i)

    out_copies = [
        pltpu.make_async_copy(dffn, dffn_out, out_sem.at[0]),
        pltpu.make_async_copy(window, window_out, out_sem.at[1]),
        pltpu.make_async_copy(whole, low2_out, out_sem.at[2]),
        pltpu.make_async_copy(low1, low1_out, out_sem.at[3]),
        pltpu.make_async_copy(qt, qt_out, out_sem.at[4]),
    ]
    for u in range(GROUPS):
        out_copies.append(pltpu.make_async_copy(store.at[4 * u], proj_out.at[u, 0:3], out_sem.at[5 + 2 * u]))
        out_copies.append(pltpu.make_async_copy(store.at[4 * u + 1, 0], proj_out.at[u, 3], out_sem.at[6 + 2 * u]))
    for copy in out_copies:
        copy.start()

    for n in range(4):
        pre = nt(w.kind_panels(4 + n), whole[...])
        at_bias = 2 * HD + n * HD
        pre = pre + jnp.concatenate([bias_t[at_bias : at_bias + HD, u : u + 1] for u in range(GROUPS)], axis=0)
        value, slope = gelu_parts(pre)
        d_act = nt(w.kind_panels(8 + n), dffn[...])
        low_value, low_grad = value.astype(BF), (d_act * slope).astype(BF)
        units = slice(n * SPAN, (n + 1) * SPAN)
        gt[units, :] = low_value
        dft[units, :] = low_grad
        g_rows[:, units] = low_value.T
        turned = low_grad.T
        df_rows[:, units] = turned
        unit_out[2 + n : 3 + n, :] = jnp.sum(turned.astype(F32), axis=0, keepdims=True)
    unit_out[0:2, :] = jnp.zeros((2, SPAN), F32)
    unit_out[6:8, :] = jnp.zeros((2, SPAN), F32)
    gt_out[...] = gt[...]
    dft_out[...] = dft[...]

    def feed(n, carry):
        cols = pl.ds(pl.multiple_of(n * 256, 256), 256)
        dn2_out[:, cols] = nn(df_rows[...], w.kind_columns(4, 4, cols)).astype(BF)
        ffn_out[:, cols] = nn(g_rows[...], w.kind_columns(8, 4, cols)).astype(BF)
        return carry

    lax.fori_loop(0, WIDTH // 256, feed, 0)

    for i in range(3):
        w.drain(i)
    mine_kv = window.at[0, p.c]
    for d in range(1, 5):
        @pl.when(p.chip + d < 8)
        def _():
            remote(mine_kv, mine_kv, kv_send.at[d], kv_recv.at[d], p.sibling()).wait_send()
    for d in range(5):
        @pl.when(p.chip - d >= 0)
        def _():
            remote(mine_kv, mine_kv, kv_bsend.at[d], kv_brecv.at[d], p.sibling()).wait_send()
    for copy in out_copies:
        copy.wait()


def forward_call(lengths, tokens, cotangent, alive_row, alive_col, panels, bias_t, gains, shifts):
    vmem = pl.BlockSpec(memory_space=pltpu.VMEM)
    anywhere = pl.BlockSpec(memory_space=pl.ANY)
    shape = jax.ShapeDtypeStruct
    dma = pltpu.SemaphoreType.DMA
    return pl.pallas_call(
        forward_kernel,
        in_specs=[pl.BlockSpec(memory_space=pltpu.SMEM)] + [vmem] * 8,
        out_specs=[anywhere, anywhere, anywhere, vmem, vmem, vmem, anywhere, vmem, vmem, vmem, vmem, anywhere, anywhere, vmem],
        out_shape=[
            shape((ROWS, WIDTH), BF),
            shape((SPAN, ROWS), BF),
            shape((5, 2, EXT, 2 * SPAN), BF),
            shape((SPAN, ROWS), F32),
            shape((8, ROWS), F32),
            shape((SHARD, WIDTH), F32),
            shape((ROWS, WIDTH), BF),
            shape((UNITS, ROWS), BF),
            shape((UNITS, ROWS), BF),
            shape((ROWS, WIDTH), BF),
            shape((ROWS, WIDTH), BF),
            shape((GROUPS, 4, HD, WIDTH), BF),
            shape((ROWS, WIDTH), BF),
            shape((8, SPAN), F32),
        ],
        scratch_shapes=[
            pltpu.VMEM((16, 3, HD, WIDTH), BF),
            pltpu.VMEM((5, 2, EXT, 2 * SPAN), BF),
            pltpu.VMEM((ROWS, WIDTH), BF),
            pltpu.VMEM((SPAN, ROWS), BF),
            pltpu.VMEM((SPAN, ROWS), F32),
            pltpu.VMEM((8, ROWS), F32),
            pltpu.VMEM((8, ROWS), F32),
            pltpu.VMEM((ROWS, WIDTH), BF),
            pltpu.VMEM((7, SHARD, WIDTH), BF),
            pltpu.VMEM((ROWS, WIDTH), BF),
            pltpu.VMEM((ROWS, UNITS), BF),
            pltpu.VMEM((ROWS, UNITS), BF),
            pltpu.VMEM((UNITS, ROWS), BF),
            pltpu.VMEM((UNITS, ROWS), BF),
            pltpu.VMEM((ROWS, WIDTH), BF),
            dma((16, 3)), dma((3,)), dma((2, 3, 3)), dma((8, 3)),
            dma((5,)), dma((5,)), dma((5,)), dma((5,)),
            dma((7,)), dma((7,)), dma((7,)), dma((7,)), dma((13,)),
        ],
        compiler_params=pltpu.CompilerParams(
            collective_id=0, has_side_effects=True, vmem_limit_bytes=56 * 2**20
        ),
        name="layer_forward",
    )(lengths, tokens, cotangent, alive_row, alive_col, panels, bias_t, gains, shifts)


def head_columns(values, head):
    owner = lax.broadcasted_iota(jnp.int32, values.shape, 1) // HD
    return jnp.where(owner == head, values, jnp.zeros_like(values))


def norm_back(grad, unit, factor, gain):
    d_gain = jnp.sum(grad * unit, axis=0, keepdims=True)
    d_shift = jnp.sum(grad, axis=0, keepdims=True)
    d_unit = grad * gain
    d_in = factor * (
        d_unit
        - jnp.mean(d_unit, axis=-1, keepdims=True)
        - unit * jnp.mean(d_unit * unit, axis=-1, keepdims=True)
    )
    return d_in, d_gain, d_shift


class PanelSums:
    def __init__(self, place, grads, pair, line, last, result, sems):
        self.p, self.grads = place, grads
        self.pair, self.line, self.last, self.result = pair, line, last, result
        self.pair_send, self.pair_recv, self.line_send, self.line_recv, self.last_send, self.last_recv = sems

    def kind(self, k):
        return (k // 2 + self.p.x) % 2

    def pair_copy(self, u, k, i):
        return remote(
            self.grads.at[4 * u + k, i],
            self.pair.at[2 * u + k // 2, i],
            self.pair_send.at[2 * u + k // 2, i],
            self.pair_recv.at[2 * u + k // 2, i],
            self.p.sibling(),
        )

    def to_pair(self, k, i):
        @pl.when(self.p.c != k % 2)
        def _():
            for u in range(GROUPS):
                self.pair_copy(u, k, i).start()

    def line_copy(self, n, k, i):
        head = (self.p.z + Z_STEPS[n]) % 4
        kind = self.kind(k)
        return remote(
            self.grads.at[4 * head + k, i],
            self.line.at[n, kind, i],
            self.line_send.at[n, kind, i],
            self.line_recv.at[n, kind, i],
            self.p.along(Z_STEPS[n]),
        )

    def pair_add(self, k, i):
        @pl.when(self.p.c == k % 2)
        def _():
            def add(step, carry):
                u, rows = step // 4, pl.ds(pl.multiple_of((step % 4) * 16, 16), 16)
                self.grads[4 * u + k, i, rows, :] = (
                    self.grads[4 * u + k, i, rows, :].astype(F32)
                    + self.pair[2 * u + k // 2, i, rows, :].astype(F32)
                ).astype(BF)
                return carry

            for u in range(GROUPS):
                self.pair_copy(u, k, i).wait_recv()
            lax.fori_loop(0, 4 * GROUPS, add, 0)
            for n in range(3):
                self.line_copy(n, k, i).start()

    def across_copy(self, k, i):
        return remote(
            self.grads.at[4 * self.p.z + k, i],
            self.last.at[i],
            self.last_send.at[i],
            self.last_recv.at[i],
            self.p.across(),
        )

    def line_add(self, k, i):
        kind = self.kind(k)

        @pl.when(self.p.c == k % 2)
        def _():
            for n in range(3):
                self.line_copy(n, k, i).wait_recv()

            def add(step, carry):
                rows = pl.ds(pl.multiple_of(step * 16, 16), 16)
                total = self.grads[4 * self.p.z + k, i, rows, :].astype(F32)
                for n in range(3):
                    total = total + self.line[n, kind, i, rows, :].astype(F32)
                self.grads[4 * self.p.z + k, i, rows, :] = total.astype(BF)

                @pl.when(self.p.x == k // 2)
                def _():
                    self.result[i, rows, :] = total

                return carry

            lax.fori_loop(0, HD // 16, add, 0)

            @pl.when(self.p.x != k // 2)
            def _():
                self.across_copy(k, i).start()

    def last_add(self, i):
        own = 2 * self.p.x + self.p.c
        self.across_copy(own, i).wait_recv()
        self.result[i] = self.result[i] + self.last[i].astype(F32)

    def drain(self):
        for k in range(4):
            for i in range(3):
                @pl.when(self.p.c != k % 2)
                def _():
                    for u in range(GROUPS):
                        self.pair_copy(u, k, i).wait_send()

                @pl.when(self.p.c == k % 2)
                def _():
                    for n in range(3):
                        self.line_copy(n, k, i).wait_send()

                    @pl.when(self.p.x != k // 2)
                    def _():
                        self.across_copy(k, i).wait_send()


def backward_kernel(
    lengths, alive_row, alive_col, gains, shifts, dn2_part, gt, dft, ot, lse, hidden, unit_rows, qt,
    tokens_any, cot_any, dffn_any, low2_any, low1_any, window_any, proj_any, ffn_any,
    out_any, grad_any, result, vec_out, unit_out,
    grads, pair, line, last, window, d_kv, kv_pair, kv_far, dffn, low2, low1, proj, ffn_part, x_mine, cot_mine,
    branch, out_whole, in_whole, dn1_part, land, q_rows, q_cols, do_rows, do_cols, delta, dqt, dkv_sum, d_hidden,
    bank, bank_land, small, small_pair, small_all, bank_back,
    rs_send, rs_recv, ag_send, ag_recv, pair_send, pair_recv, line_send, line_recv, last_send, last_recv,
    kv_bsend, kv_brecv, kv_send, kv_recv, v1_send, v1_recv, v2_send, v2_recv, v3_send, v3_recv, v4_send, v4_recv,
    load_sem, out_sem,
):
    p = Place()
    sums = PanelSums(
        p, grads, pair, line, last, result,
        (pair_send, pair_recv, line_send, line_recv, last_send, last_recv),
    )
    mine = pl.ds(pl.multiple_of(p.t * SHARD, SHARD), SHARD)
    sources = [
        (dffn_any, dffn), (low2_any, low2), (tokens_any.at[mine], x_mine), (cot_any.at[mine], cot_mine),
        (proj_any, proj), (window_any, window), (low1_any, low1), (ffn_any, ffn_part),
    ]
    loads = [pltpu.make_async_copy(a, b, load_sem.at[n]) for n, (a, b) in enumerate(sources)]
    for load in loads:
        load.start()
    p.greet()
    first_scatter = scatter_copies(p, dn2_part, land.at[0], rs_send.at[0], rs_recv.at[0])
    for copy in first_scatter:
        copy.start()

    def kinds_grad(j, left, right):
        def tile(n, carry):
            cols = pl.ds(pl.multiple_of(n * 256, 256), 256)
            made = nn(left, right[:, cols]).astype(BF)
            for u in range(GROUPS):
                grads[4 * u + j // 3, j % 3, :, cols] = made[u * HD : (u + 1) * HD]
            return carry

        lax.fori_loop(0, WIDTH // 256, tile, 0)

    loads[0].wait()
    loads[1].wait()
    for n in (0, 1, 2, 3):
        kinds_grad(8 + n, gt[n * SPAN : (n + 1) * SPAN, :], dffn)
        sums.to_pair((8 + n) // 3, (8 + n) % 3)
    for n in (2, 3, 0, 1):
        kinds_grad(4 + n, dft[n * SPAN : (n + 1) * SPAN, :], low2)
        sums.to_pair((4 + n) // 3, (4 + n) % 3)

    loads[2].wait()
    loads[3].wait()
    live = alive_col[mine, :]
    grad_out = cot_mine[...].astype(F32)
    _, unit2, factor2 = normalize(hidden[...], gains[1:2, :], shifts[3:4, :])
    for copy in first_scatter:
        copy.wait()
    d_norm2 = scatter_sum(p, dn2_part, land.at[0])
    d_in, d_gain2, d_shift2 = norm_back(d_norm2, unit2, factor2, gains[1:2, :])
    d_hidden[...] = grad_out + d_in
    d_branch = (live * d_hidden[...]).astype(BF)
    branch[mine, :] = d_branch
    first_gather = gather_copies(p, branch, ag_send.at[0], ag_recv.at[0])
    for copy in first_gather:
        copy.start()

    def to_bank(row, values):
        for n in range(8):
            bank[n, row : row + 1, :] = values[:, n * 256 : (n + 1) * 256]

    to_bank(1, d_gain2)
    to_bank(2, jnp.sum(d_branch.astype(F32), axis=0, keepdims=True))
    to_bank(3, jnp.sum(live * grad_out, axis=0, keepdims=True))
    to_bank(5, d_shift2)
    to_bank(6, jnp.zeros((1, WIDTH), F32))
    to_bank(7, jnp.zeros((1, WIDTH), F32))

    early = ((3, 0), (3, 1), (3, 2), (2, 2), (2, 0), (2, 1), (1, 1), (1, 2))
    for k, i in early:
        sums.pair_add(k, i)

    loads[4].wait()
    loads[5].wait()
    scaled = (qt[...].astype(F32) * (HD ** -0.5)).astype(BF)
    scaled_rows = scaled.T
    for u in range(GROUPS):
        q_rows[u] = head_rows(scaled, u)
        q_cols[u] = head_columns(scaled_rows, u)
    dqt[...] = jnp.zeros_like(dqt)
    dkv_sum[...] = jnp.zeros_like(dkv_sum)
    code, at = query_code(p, lengths, alive_row[...])

    for copy in first_gather:
        copy.wait()
    w_out = jnp.concatenate([proj[u, 3] for u in range(GROUPS)], axis=0)
    do_t = nt(w_out, branch[...]).astype(BF)
    do_turned = do_t.T
    for u in range(GROUPS):
        heads = slice(u * HD, (u + 1) * HD)
        do_rows[u] = head_rows(do_t, u)
        do_cols[u] = head_columns(do_turned, u)
        delta[u : u + 1, :] = jnp.sum(do_t[heads, :].astype(F32) * ot[heads, :], axis=0, keepdims=True)
    loads[7].wait()
    out_scatter = scatter_copies(p, ffn_part, land.at[1], rs_send.at[1], rs_recv.at[1])
    for copy in out_scatter:
        copy.start()
    kinds_grad(3, ot[...].astype(BF), branch)
    sums.to_pair(1, 0)

    def kv_pair_copy(d):
        return remote(d_kv.at[d, 1 - p.c], kv_pair.at[d], kv_bsend.at[d], kv_brecv.at[d], p.sibling())

    def kv_far_copy(d):
        return remote(d_kv.at[d, p.c], kv_far.at[d], kv_send.at[d], kv_recv.at[d], p.chip_at(-d))

    def finish(d):
        @pl.when(p.chip - d >= 0)
        def _():
            @pl.when(((p.c == 0) & (d <= 3)) | ((p.c == 1) & (d >= 1)))
            def _():
                kv_pair_copy(d).wait_recv()
                d_kv[d, p.c] = (d_kv[d, p.c].astype(F32) + kv_pair[d].astype(F32)).astype(BF)

            @pl.when(d >= 1)
            def _():
                kv_far_copy(d).start()

    def block_back(step, carry):
        d = 4 - step // 2
        core = (1 - p.c + step) % 2
        use = (p.chip - d >= 0) & ~((d == 0) & (core > p.c)) & ~((d == 4) & (core < p.c))

        @pl.when(use)
        def _():
            bias = block_bias(p, lengths, window, d, core, code, at)
            keys = window[d, core, 0:ROWS, 0:SPAN]
            values = window[d, core, 0:ROWS, SPAN : 2 * SPAN]
            keys_t = keys.T
            d_key = jnp.zeros((ROWS, SPAN), F32)
            d_value = jnp.zeros((ROWS, SPAN), F32)
            for u in range(GROUPS):
                heads = slice(u * HD, (u + 1) * HD)
                prob = jnp.exp(nn(keys, q_rows[u]) + bias - lse[u : u + 1, :])
                d_prob = nn(values, do_rows[u])
                d_score = (prob * (d_prob - delta[u : u + 1, :])).astype(BF)
                d_value = d_value + nn(prob.astype(BF), do_cols[u])
                d_key = d_key + nn(d_score, q_cols[u])
                dqt[heads, :] = dqt[heads, :] + nn(keys_t[heads, :], d_score)
            d_kv[d, core, :, 0:SPAN] = d_key.astype(BF)
            d_kv[d, core, :, SPAN : 2 * SPAN] = d_value.astype(BF)

            @pl.when(core != p.c)
            def _():
                kv_pair_copy(d).start()

        @pl.when((step % 2 == 1) & (step > 1))
        def _():
            finish(d + 1)

        return carry

    lax.fori_loop(0, 10, block_back, 0)
    finish(0)
    sums.pair_add(1, 0)

    dq_t = (dqt[...] * (HD ** -0.5)).astype(BF)
    dq = dq_t.T
    small[8:16, :] = unit_rows[...]
    small[8:9, :] = jnp.sum(dq.astype(F32), axis=0, keepdims=True)
    loads[6].wait()
    kinds_grad(0, dq_t, low1)
    sums.to_pair(0, 0)

    for copy in out_scatter:
        copy.wait()
    summed = scatter_sum(p, ffn_part, land.at[1])
    out_whole[mine, :] = (hidden[...] + live * (summed + shifts[1:2, :])).astype(BF)

    dkv_sum[...] = d_kv[0, p.c].astype(F32)
    for d in (1, 2, 3, 4):
        @pl.when(p.chip + d < 8)
        def _():
            kv_far_copy(d).wait_recv()
            dkv_sum[...] = dkv_sum[...] + kv_far[d].astype(F32)

    dkv = dkv_sum[...].astype(BF)
    dkv_t = dkv.T
    small[9:10, :] = jnp.sum(dkv[:, SPAN:].astype(F32), axis=0, keepdims=True)

    def norm1_part(n, carry):
        cols = pl.ds(pl.multiple_of(n * 256, 256), 256)
        total = jnp.zeros((ROWS, 256), F32)
        for i, left in enumerate((dq, dkv[:, :SPAN], dkv[:, SPAN:])):
            total = total + nn(left, jnp.concatenate([proj[u, i, :, cols] for u in range(GROUPS)], axis=0))
        dn1_part[:, cols] = total.astype(BF)
        return carry

    lax.fori_loop(0, WIDTH // 256, norm1_part, 0)
    last_scatter = scatter_copies(p, dn1_part, land.at[2], rs_send.at[2], rs_recv.at[2])
    for copy in last_scatter:
        copy.start()
    kinds_grad(1, dkv_t[:SPAN], low1)
    sums.to_pair(0, 1)
    kinds_grad(2, dkv_t[SPAN:], low1)
    sums.to_pair(0, 2)
    for i in range(3):
        sums.pair_add(0, i)
    out_gather = gather_copies(p, out_whole, ag_send.at[1], ag_recv.at[1])
    for copy in out_gather:
        copy.start()
    for k, i in early:
        sums.line_add(k, i)
    sums.line_add(1, 0)

    _, unit1, factor1 = normalize(x_mine[...].astype(F32), gains[0:1, :], shifts[2:3, :])
    for copy in last_scatter:
        copy.wait()
    d_norm1 = scatter_sum(p, dn1_part, land.at[2])
    d_in, d_gain1, d_shift1 = norm_back(d_norm1, unit1, factor1, gains[0:1, :])
    in_whole[mine, :] = (d_hidden[...] + d_in).astype(BF)
    last_gather = gather_copies(p, in_whole, ag_send.at[2], ag_recv.at[2])
    for copy in last_gather:
        copy.start()
    to_bank(0, d_gain1)
    to_bank(4, d_shift1)

    slices = []
    for n, (dy, dx) in enumerate(T_STEPS):
        to = p.tensor_at(dy, dx)
        slices.append(remote(bank.at[to], bank_land.at[n], v1_send.at[n], v1_recv.at[n], {"tensor": to}))
    for copy in slices:
        copy.start()
    for copy in slices:
        copy.wait()
    total = bank[p.t]
    for n in range(len(T_STEPS)):
        total = total + bank_land[n]
    small[0:8, :] = total
    pair_small = remote(small, small_pair, v2_send, v2_recv, p.sibling())
    pair_small.start()

    for i in range(3):
        sums.line_add(0, i)

    pair_small.wait()
    here = p.z * 2 + p.x
    small_all[here] = small[...] + small_pair[...]
    spread = []
    for n in range(1, 8):
        to = p.seq((p.z + n // 2) % 4, (p.x + n % 2) % 2, p.c)
        spread.append(remote(small_all.at[here], small_all.at[here], v3_send.at[n - 1], v3_recv.at[n - 1], to))
    for copy in spread:
        copy.start()
    for i in range(3):
        sums.last_add(i)
    for copy in spread:
        copy.wait()
    total = small_all[0]
    for n in range(1, 8):
        total = total + small_all[n]
    bank_back[p.t] = total[0:8, :]
    unit_out[...] = total[8:16, :]
    back = []
    for n, (dy, dx) in enumerate(T_STEPS):
        to = {"tensor": p.tensor_at(dy, dx)}
        back.append(remote(bank_back.at[p.t], bank_back.at[p.t], v4_send.at[n], v4_recv.at[n], to))
    for copy in back:
        copy.start()

    for copy in out_gather:
        copy.wait()
    for copy in last_gather:
        copy.wait()
    stores = [
        pltpu.make_async_copy(out_whole, out_any, out_sem.at[0]),
        pltpu.make_async_copy(in_whole, grad_any, out_sem.at[1]),
    ]
    for copy in stores:
        copy.start()
    for copy in back:
        copy.wait()
    vec_out[...] = bank_back[...]
    sums.drain()
    for d in range(5):
        @pl.when((p.chip - d >= 0) & (((p.c == 1) & (d <= 3)) | ((p.c == 0) & (d >= 1))))
        def _():
            kv_pair_copy(d).wait_send()

        if d >= 1:
            @pl.when(p.chip - d >= 0)
            def _():
                kv_far_copy(d).wait_send()

    for copy in stores:
        copy.wait()


def backward_call(
    lengths, alive_row, alive_col, gains, shifts, dn2_part, gt, dft, ot, lse, hidden, unit_rows, qt,
    tokens, cotangent, dffn, low2, low1, window, proj, ffn_part,
):
    vmem = pl.BlockSpec(memory_space=pltpu.VMEM)
    anywhere = pl.BlockSpec(memory_space=pl.ANY)
    shape = jax.ShapeDtypeStruct
    dma = pltpu.SemaphoreType.DMA
    rows_low = pltpu.VMEM((ROWS, WIDTH), BF)
    shard_low = pltpu.VMEM((SHARD, WIDTH), BF)
    masked = pltpu.VMEM((GROUPS, SPAN, ROWS), BF)
    return pl.pallas_call(
        backward_kernel,
        in_specs=[pl.BlockSpec(memory_space=pltpu.SMEM)] + [vmem] * 12 + [anywhere] * 8,
        out_specs=[anywhere, anywhere, vmem, vmem, vmem],
        out_shape=[
            shape((ROWS, WIDTH), BF),
            shape((ROWS, WIDTH), BF),
            shape((3, HD, WIDTH), F32),
            shape((8, 8, 256), F32),
            shape((8, SPAN), F32),
        ],
        scratch_shapes=[
            pltpu.VMEM((16, 3, HD, WIDTH), BF),
            pltpu.VMEM((8, 3, HD, WIDTH), BF),
            pltpu.VMEM((3, 2, 3, HD, WIDTH), BF),
            pltpu.VMEM((3, HD, WIDTH), BF),
            pltpu.VMEM((5, 2, EXT, 2 * SPAN), BF),
            pltpu.VMEM((5, 2, ROWS, 2 * SPAN), BF),
            pltpu.VMEM((5, ROWS, 2 * SPAN), BF),
            pltpu.VMEM((5, ROWS, 2 * SPAN), BF),
            rows_low, rows_low, rows_low,
            pltpu.VMEM((GROUPS, 4, HD, WIDTH), BF),
            rows_low, shard_low, shard_low,
            rows_low, rows_low, rows_low, rows_low,
            pltpu.VMEM((3, 7, SHARD, WIDTH), BF),
            masked, masked, masked, masked,
            pltpu.VMEM((8, ROWS), F32),
            pltpu.VMEM((SPAN, ROWS), F32),
            pltpu.VMEM((ROWS, 2 * SPAN), F32),
            pltpu.VMEM((SHARD, WIDTH), F32),
            pltpu.VMEM((8, 8, 256), F32),
            pltpu.VMEM((7, 8, 256), F32),
            pltpu.VMEM((16, 256), F32),
            pltpu.VMEM((16, 256), F32),
            pltpu.VMEM((8, 16, 256), F32),
            pltpu.VMEM((8, 8, 256), F32),
            dma((3, 7)), dma((3, 7)), dma((3, 7)), dma((3, 7)),
            dma((8, 3)), dma((8, 3)), dma((3, 2, 3)), dma((3, 2, 3)), dma((3,)), dma((3,)),
            dma((5,)), dma((5,)), dma((5,)), dma((5,)),
            dma((7,)), dma((7,)), dma, dma, dma((7,)), dma((7,)), dma((7,)), dma((7,)),
            dma((8,)), dma((2,)),
        ],
        compiler_params=pltpu.CompilerParams(
            collective_id=1, has_side_effects=True, vmem_limit_bytes=60 * 2**20
        ),
        name="layer_backward",
    )(
        lengths, alive_row, alive_col, gains, shifts, dn2_part, gt, dft, ot, lse, hidden, unit_rows, qt,
        tokens, cotangent, dffn, low2, low1, window, proj, ffn_part,
    )


def high(left, right):
    return jnp.dot(left, right, precision=HIGH, preferred_element_type=F32)


def muon_kernel(grads, panel_mom, panels, new_panels, new_mom):
    count = panels.shape[0]
    eye = jnp.where(
        lax.broadcasted_iota(jnp.int32, (HD, HD), 0) == lax.broadcasted_iota(jnp.int32, (HD, HD), 1), 1.0, 0.0
    )
    scale, gram, chain = [], [], [None] * count
    for n in range(count):
        moment = DECAY * panel_mom[n] + grads[n]
        new_mom[n] = moment
        factor = lax.rsqrt(jnp.sum(moment * moment, axis=(0, 1), keepdims=True) + 1e-06)
        current = moment * factor
        scale.append(factor)
        gram.append(
            lax.dot_general(
                current, current, (((1,), (1,)), ((), ())), precision=HIGH, preferred_element_type=F32
            )
        )
    for sweep in range(NS_ITERS):
        squares = [high(a, a) for a in gram]
        steps = [NS_A * eye + NS_B * a + NS_C * s for a, s in zip(gram, squares)]
        chain = [m if sweep == 0 else high(m, c) for m, c in zip(steps, chain)]
        if sweep < NS_ITERS - 1:
            halves = [high(m, a) for m, a in zip(steps, gram)]
            gram = [high(h, m) for h, m in zip(halves, steps)]
    for n in range(count):
        direction = high(chain[n], new_mom[n] * scale[n])
        size_u = jnp.sum(direction * direction, axis=(0, 1), keepdims=True)
        held = panels[n]
        size_w = jnp.sum(held * held, axis=(0, 1), keepdims=True)
        new_panels[n] = held - LR_MATRIX * jnp.sqrt(size_w) * lax.rsqrt(size_u + 1e-06) * direction


def muon_call(grads, panel_mom, panels):
    vmem = pl.BlockSpec(memory_space=pltpu.VMEM)
    shape = jax.ShapeDtypeStruct(panels.shape, F32)
    return pl.pallas_call(
        muon_kernel,
        in_specs=[vmem] * 3,
        out_specs=[vmem, vmem],
        out_shape=[shape, shape],
        compiler_params=pltpu.CompilerParams(vmem_limit_bytes=32 * 2**20),
        name="panel_step",
    )(grads, panel_mom, panels)


def per_device(
    tokens, cotangent, exits, lengths, panels, panel_mom,
    unit_bias, unit_bias_mom, gains, gains_mom, vec_bias, vec_bias_mom,
):
    live = (exits >= LAYER).astype(F32)
    alive_row, alive_col = live[None, :], live[:, None]
    (
        low1, qt, window, ot, lse, hidden, low2, gt, dft, ffn_part, dn2_part, proj, dffn, unit_rows,
    ) = forward_call(
        lengths, tokens, cotangent, alive_row, alive_col, panels, unit_bias.T, gains, vec_bias
    )
    output, input_grad, panel_grads, vec_sums, unit_sums = backward_call(
        lengths, alive_row, alive_col, gains, vec_bias, dn2_part, gt, dft, ot, lse, hidden, unit_rows, qt,
        tokens, cotangent, dffn, low2, low1, window, proj, ffn_part,
    )
    new_panels, moment = muon_call(panel_grads, panel_mom, panels)
    vec_sums = vec_sums.transpose(1, 0, 2).reshape(8, WIDTH)
    unit_sum = unit_sums[0:6].reshape(6, GROUPS, HD).transpose(1, 0, 2).reshape(GROUPS, 6 * HD)
    unit_moment = DECAY * unit_bias_mom + unit_sum
    gains_moment = DECAY * gains_mom + vec_sums[0:2]
    vec_moment = DECAY * vec_bias_mom + vec_sums[2:6]
    return (
        output, input_grad.astype(F32), new_panels, moment,
        unit_bias - LR_VECTOR * unit_moment, unit_moment,
        gains - LR_VECTOR * gains_moment, gains_moment,
        vec_bias - LR_VECTOR * vec_moment, vec_moment,
    )


def solution(mesh):
    held = P(("tensor", "seq"), None, None)
    return jax.shard_map(
        per_device,
        mesh=mesh,
        in_specs=(
            P("seq", None), P("seq", None), P("seq"), P(), held, held,
            P("tensor", None), P("tensor", None), P(), P(), P(), P(),
        ),
        out_specs=(
            P("seq", None), P("seq", None), held, held,
            P("tensor", None), P("tensor", None), P(), P(), P(), P(),
        ),
        check_vma=False,
    )
```

```python
import functools
import math

import jax
import jax.numpy as jnp
from jax import lax
from jax.experimental import pallas as pl
from jax.experimental.pallas import tpu as pltpu
from jax.sharding import PartitionSpec as P

LAYER = 12
NS_ITERS = 5
EPS = 1e-05
NS_A = 3.4445
NS_B = -4.775
NS_C = 2.0315
LR_MATRIX = 0.5
LR_VECTOR = 0.002
DECAY = 0.5
HIGH = lax.Precision.HIGHEST
MESH = pl.DeviceIdType.MESH

ROWS = 256
WIDTH = 2048
GROUPS = 4
HD = 64
SPAN = GROUPS * HD
UNITS = 4 * SPAN
SHARD = 32
EXT = ROWS + 16
MASKED = -1e30
FLOOR = -1e28
BF = jnp.bfloat16
F32 = jnp.float32

NEAR = (1, 3)
HALF = 32
T_STEPS = tuple((dy, dx) for dy in (2, 1, 3, 0) for dx in (1, 0) if (dy, dx) != (0, 0))


def nt(left, right):
    return lax.dot_general(left, right, (((1,), (1,)), ((), ())), preferred_element_type=F32)


def nn(left, right):
    return jnp.dot(left, right, preferred_element_type=F32)


def normalize(values, gain, shift):
    mean = jnp.mean(values, axis=-1, keepdims=True)
    centred = values - mean
    factor = lax.rsqrt(jnp.mean(centred * centred, axis=-1, keepdims=True) + EPS)
    return centred * factor * gain + shift, centred * factor, factor


class Place:
    def __init__(self):
        self.s = lax.axis_index("seq")
        self.t = lax.axis_index("tensor")
        self.z, self.x, self.c = self.s // 4, (self.s // 2) % 2, self.s % 2
        self.chip = self.s // 2
        self.y, self.h = self.t // 2, self.t % 2

    def seq(self, z, x, c):
        return {"seq": z * 4 + x * 2 + c}

    def sibling(self):
        return self.seq(self.z, self.x, 1 - self.c)

    def across(self):
        return self.seq(self.z, 1 - self.x, self.c)

    def along(self, step):
        return self.seq((self.z + step) % 4, self.x, self.c)

    def chip_at(self, step):
        return {"seq": (self.chip + step) * 2 + self.c}

    def tensor_at(self, dy, dx):
        return ((self.y + dy) % 4) * 2 + (self.h + dx) % 2

    def greet(self):
        barrier = pltpu.get_barrier_semaphore()
        count = 0
        for dz in range(4):
            for dx in range(2):
                if (dz, dx) != (0, 0):
                    to = self.seq((self.z + dz) % 4, (self.x + dx) % 2, self.c)
                    pl.semaphore_signal(barrier, inc=1, device_id=to, device_id_type=MESH)
                    count += 1
        pl.semaphore_signal(barrier, inc=1, device_id=self.sibling(), device_id_type=MESH)
        count += 1
        for dy, dx in T_STEPS:
            to = {"tensor": self.tensor_at(dy, dx)}
            pl.semaphore_signal(barrier, inc=1, device_id=to, device_id_type=MESH)
            count += 1
        pl.semaphore_wait(barrier, count)


def remote(src, dst, send, recv, to):
    return pltpu.make_async_remote_copy(
        src_ref=src, dst_ref=dst, send_sem=send, recv_sem=recv, device_id=to, device_id_type=MESH
    )


def scatter_copies(place, part, land, send, recv):
    out = []
    for i, (dy, dx) in enumerate(T_STEPS):
        to = place.tensor_at(dy, dx)
        rows = pl.ds(pl.multiple_of(to * SHARD, SHARD), SHARD)
        out.append(remote(part.at[rows], land.at[i], send.at[i], recv.at[i], {"tensor": to}))
    return out


def scatter_sum(place, part, land):
    mine = pl.ds(pl.multiple_of(place.t * SHARD, SHARD), SHARD)
    total = part[mine, :].astype(F32)
    for i in range(len(T_STEPS)):
        total = total + land[i].astype(F32)
    return total


def gather_copies(place, whole, send, recv):
    mine = pl.ds(pl.multiple_of(place.t * SHARD, SHARD), SHARD)
    out = []
    for i, (dy, dx) in enumerate(T_STEPS):
        to = place.tensor_at(dy, dx)
        out.append(remote(whole.at[mine], whole.at[mine], send.at[i], recv.at[i], {"tensor": to}))
    return out


def column_of(row):
    n = row.shape[1]
    down = lax.broadcasted_iota(jnp.int32, (n, n), 0)
    over = lax.broadcasted_iota(jnp.int32, (n, n), 1)
    return jnp.sum(jnp.where(down == over, row, 0.0), axis=1, keepdims=True)


def segment_of(positions, lengths):
    end = jnp.int32(0)
    segment = jnp.zeros(positions.shape, F32)
    for i in range(4):
        end = end + lengths[i]
        segment = segment + jnp.where(positions >= end, 1.0, 0.0)
    return segment


def query_code(place, lengths, alive_row):
    at = place.s * ROWS + lax.broadcasted_iota(jnp.int32, (1, ROWS), 1)
    return jnp.where(alive_row > 0.5, segment_of(at, lengths), -2.0), at


def block_bias(place, lengths, window, dist, core, code, at):
    first = ((place.chip - dist) * 2 + core) * ROWS
    keys = first + lax.broadcasted_iota(jnp.int32, (ROWS, 1), 0)
    live = column_of(window[dist, core, ROWS:EXT, 0:ROWS].astype(F32)[0:1])
    key_code = jnp.where(live > 0.5, segment_of(keys, lengths), -1.0)
    same = jnp.where(key_code == code, 0.0, MASKED)
    return jnp.where(keys <= at, same, MASKED)


def head_rows(values, head):
    owner = lax.broadcasted_iota(jnp.int32, values.shape, 0) // HD
    return jnp.where(owner == head, values, jnp.zeros_like(values))


class Panels:
    def __init__(self, place, store, recv, across, along, half_send, half_recv, beside):
        self.p, self.store, self.recv = place, store, recv
        self.sx, self.sz, self.sh, self.rh, self.sc = across, along, half_send, half_recv, beside

    def piece(self, which, i, send, to):
        ref = self.store.at[which, i]
        return remote(ref, ref, send, self.recv.at[which, i], to)

    def across_copy(self, k, i):
        return self.piece(4 * self.p.z + k, i, self.sx.at[i], self.p.across())

    def along_copy(self, k, i, n):
        return self.piece(4 * self.p.z + k, i, self.sz.at[k // 2, n, i], self.p.along(NEAR[n]))

    def half_copy(self, k, i, n):
        which = 4 * ((self.p.z - NEAR[n]) % 4) + k
        ref = self.store.at[which, i, pl.ds(n * HALF, HALF)]
        return remote(ref, ref, self.sh.at[k // 2, n, i], self.rh.at[k // 2, n, i], self.p.along(NEAR[n]))

    def beside_copy(self, k, i, slot):
        which = 4 * ((self.p.z - (0, 1, 3, 2)[slot]) % 4) + k
        return self.piece(which, i, self.sc.at[k // 2, slot, i], self.p.sibling())

    def arrived(self, which, i):
        self.piece(which, i, self.sx.at[0], self.p.sibling()).wait_recv()

    def across(self, k, i):
        @pl.when((self.p.c == k % 2) & (self.p.x == k // 2))
        def _():
            self.across_copy(k, i).start()

    def along(self, k, i, ways=(0, 1), first=True):
        @pl.when(self.p.c == k % 2)
        def _():
            if first:
                @pl.when(self.p.x != k // 2)
                def _():
                    self.arrived(4 * self.p.z + k, i)

            for n in ways:
                self.along_copy(k, i, n).start()
            if first:
                self.beside_copy(k, i, 0).start()

    def pass_on(self, k, i):
        @pl.when(self.p.c == k % 2)
        def _():
            for n in (0, 1):
                self.arrived(4 * ((self.p.z - NEAR[n]) % 4) + k, i)
                self.half_copy(k, i, n).start()
                self.beside_copy(k, i, 1 + n).start()

    def far_in(self, k, i):
        @pl.when(self.p.c == k % 2)
        def _():
            for n in (0, 1):
                self.half_copy(k, i, n).wait_recv()
            self.beside_copy(k, i, 3).start()

    def beside_in(self, k, i):
        @pl.when(self.p.c != k % 2)
        def _():
            for u in range(4):
                self.arrived(4 * u + k, i)

    def drain(self, k, i):
        @pl.when(self.p.c == k % 2)
        def _():
            @pl.when(self.p.x == k // 2)
            def _():
                self.across_copy(k, i).wait_send()

            for n in (0, 1):
                self.along_copy(k, i, n).wait_send()
                self.half_copy(k, i, n).wait_send()
            for slot in range(4):
                self.beside_copy(k, i, slot).wait_send()

    def kind_panels(self, j):
        return jnp.concatenate([self.store[4 * u + j // 3, j % 3] for u in range(GROUPS)], axis=0)

    def kind_columns(self, first, count, cols):
        parts = [
            self.store[4 * u + j // 3, j % 3, :, cols]
            for j in range(first, first + count)
            for u in range(GROUPS)
        ]
        return jnp.concatenate(parts, axis=0)


def gelu_parts(f):
    cdf = 0.5 * (1.0 + lax.erf(f * (2.0 ** -0.5)))
    pdf = jnp.exp(-0.5 * f * f) * (1.0 / math.sqrt(2.0 * math.pi))
    return f * cdf, cdf + f * pdf


def forward_kernel(
    lengths, tokens, cotangent, alive_row, alive_col, panels, bias_t, gains, shifts,
    low1_out, qt_out, window_out, ot_out, lse_out, hidden_out, low2_out, gt_out, dft_out, ffn_out, dn2_out, proj_out,
    dffn_out, unit_out,
    store, window, low1, qt, acc, top, mass, part, land, whole, g_rows, df_rows, dft, gt, dffn,
    w_recv, w_across, w_along, w_half_send, w_half_recv, w_beside, kv_send, kv_recv, kv_bsend, kv_brecv, rs_send, rs_recv, ag_send, ag_recv, out_sem,
):
    p = Place()
    w = Panels(p, store, w_recv, w_across, w_along, w_half_send, w_half_recv, w_beside)
    p.greet()

    for i in range(3):
        store[p.s, i] = panels[i].astype(BF)

    order = (1, 2, 0)

    for i in order:
        w.across(0, i)
    for k in (2, 3):
        for i in range(3):
            w.across(k, i)

    @pl.when(p.x == 0)
    def _():
        for i in order:
            w.along(0, i)

    def norm1(r, carry):
        rows = pl.ds(pl.multiple_of(r * 32, 32), 32)
        normed, _, _ = normalize(tokens[rows, :].astype(F32), gains[0:1, :], shifts[2:3, :])
        low1[rows, :] = normed.astype(BF)
        dffn[rows, :] = (cotangent[rows, :].astype(F32) * alive_col[rows, :]).astype(BF)
        return carry

    lax.fori_loop(0, ROWS // 32, norm1, 0)

    @pl.when(p.x == 1)
    def _():
        for i in order:
            w.along(0, i)

    for i in order:
        w.pass_on(0, i)
    for i in order:
        w.far_in(0, i)
        w.beside_in(0, i)
        made = nt(w.kind_panels(i), low1[...])
        if i == 1:
            window[0, p.c, 0:ROWS, 0:SPAN] = made.astype(BF).T
        elif i == 2:
            bias = jnp.concatenate([bias_t[HD : 2 * HD, u : u + 1] for u in range(GROUPS)], axis=0)
            window[0, p.c, 0:ROWS, SPAN : 2 * SPAN] = (made + bias).astype(BF).T
            row = jnp.broadcast_to(alive_row[...], (16, ROWS)).astype(BF)
            window[0, p.c, ROWS:EXT, 0:SPAN] = row
            window[0, p.c, ROWS:EXT, SPAN : 2 * SPAN] = jnp.zeros((16, SPAN), BF)
            mine = window.at[0, p.c]
            remote(mine, mine, kv_bsend.at[0], kv_brecv.at[0], p.sibling()).start()
            for d in (2, 1, 4, 3):
                @pl.when(p.chip + d < 8)
                def _():
                    remote(mine, window.at[d, p.c], kv_send.at[d], kv_recv.at[d], p.chip_at(d)).start()
        else:
            bias = jnp.concatenate([bias_t[0:HD, u : u + 1] for u in range(GROUPS)], axis=0)
            qt[...] = (made + bias).astype(BF)

    for i in range(3):
        w.across(1, i)

    @pl.when(p.x == 0)
    def _():
        w.along(1, 0)

    for i in range(3):
        w.along(3, i, ways=(1,))
        w.along(2, i, ways=(1,))

    acc[...] = jnp.zeros_like(acc)
    top[...] = jnp.full_like(top, FLOOR)
    mass[...] = jnp.zeros_like(mass)
    code, at = query_code(p, lengths, alive_row[...])
    scaled = (qt[...].astype(F32) * (HD ** -0.5)).astype(BF)

    def attend(d, core):
        bias = block_bias(p, lengths, window, d, core, code, at)
        keys = window[d, core, 0:ROWS, 0:SPAN]
        values_t = window[d, core, 0:ROWS, SPAN : 2 * SPAN].T
        for u in range(GROUPS):
            heads = slice(u * HD, (u + 1) * HD)
            score = nn(keys, head_rows(scaled, u)) + bias
            old = top[u : u + 1, :]
            new = jnp.maximum(old, jnp.max(score, axis=0, keepdims=True))
            weight = jnp.exp(score - new)
            fade = jnp.exp(old - new)
            top[u : u + 1, :] = new
            mass[u : u + 1, :] = mass[u : u + 1, :] * fade + jnp.sum(weight, axis=0, keepdims=True)
            acc[heads, :] = acc[heads, :] * fade + nn(values_t[heads, :], weight.astype(BF))

    def attend_chip(d):
        def body(core, carry):
            use = (p.chip - d >= 0) & ~((d == 0) & (core > p.c)) & ~((d == 4) & (core < p.c))

            @pl.when(use)
            def _():
                attend(d, core)

            return carry

        lax.fori_loop(0, 2, body, 0)

    def kv_in(d):
        @pl.when(p.chip - d >= 0)
        def _():
            got = window.at[d, p.c]
            remote(got, got, kv_send.at[d], kv_recv.at[d], p.sibling()).wait_recv()
            remote(got, got, kv_bsend.at[d], kv_brecv.at[d], p.sibling()).start()

    def kv_beside(d):
        @pl.when(p.chip - d >= 0)
        def _():
            got = window.at[d, 1 - p.c]
            remote(got, got, kv_bsend.at[d], kv_brecv.at[d], p.sibling()).wait_recv()

    kv_beside(0)
    kv_in(1)
    attend_chip(0)

    @pl.when(p.x == 1)
    def _():
        w.along(1, 0)

    kv_beside(1)
    kv_in(2)
    attend_chip(1)
    w.pass_on(1, 0)
    kv_beside(2)
    kv_in(3)
    for i in range(3):
        w.along(3, i, ways=(0,), first=False)
        w.along(2, i, ways=(0,), first=False)
    attend_chip(2)
    kv_beside(3)
    kv_in(4)
    for i in (1, 2):
        w.along(1, i)
    attend_chip(3)
    w.far_in(1, 0)
    kv_beside(4)
    attend_chip(4)

    total = jnp.maximum(mass[...], 1e-30)
    lse_out[...] = top[...] + jnp.log(total)
    for u in range(GROUPS):
        heads = slice(u * HD, (u + 1) * HD)
        acc[heads, :] = acc[heads, :] / total[u : u + 1, :]
    ot_out[...] = acc[...]
    o_rows = acc[...].astype(BF).T

    w.beside_in(1, 0)

    def project(n, carry):
        cols = pl.ds(pl.multiple_of(n * 256, 256), 256)
        part[:, cols] = nn(o_rows, w.kind_columns(3, 1, cols)).astype(BF)
        return carry

    lax.fori_loop(0, WIDTH // 256, project, 0)
    scatter = scatter_copies(p, part, land, rs_send, rs_recv)
    for copy in scatter:
        copy.start()

    for k, i in ((3, 0), (2, 0), (3, 1), (2, 1)):
        w.pass_on(k, i)
    for copy in scatter:
        copy.wait()
    mine = pl.ds(pl.multiple_of(p.t * SHARD, SHARD), SHARD)
    summed = scatter_sum(p, part, land)
    hidden = tokens[mine, :].astype(F32) + alive_col[mine, :] * (summed + shifts[0:1, :])
    hidden_out[...] = hidden
    normed, _, _ = normalize(hidden, gains[1:2, :], shifts[3:4, :])
    whole[mine, :] = normed.astype(BF)
    gather = gather_copies(p, whole, ag_send, ag_recv)
    for copy in gather:
        copy.start()

    for k, i in ((3, 2), (2, 2), (1, 1), (1, 2)):
        w.pass_on(k, i)
    rest = ((3, 0), (2, 0), (3, 1), (2, 1), (3, 2), (2, 2), (1, 1), (1, 2))
    for k, i in rest:
        w.far_in(k, i)
    for copy in gather:
        copy.wait()
    for k, i in rest:
        w.beside_in(k, i)

    out_copies = [
        pltpu.make_async_copy(dffn, dffn_out, out_sem.at[0]),
        pltpu.make_async_copy(window, window_out, out_sem.at[1]),
        pltpu.make_async_copy(whole, low2_out, out_sem.at[2]),
        pltpu.make_async_copy(low1, low1_out, out_sem.at[3]),
        pltpu.make_async_copy(qt, qt_out, out_sem.at[4]),
    ]
    for u in range(GROUPS):
        out_copies.append(pltpu.make_async_copy(store.at[4 * u], proj_out.at[u, 0:3], out_sem.at[5 + 2 * u]))
        out_copies.append(pltpu.make_async_copy(store.at[4 * u + 1, 0], proj_out.at[u, 3], out_sem.at[6 + 2 * u]))
    for copy in out_copies:
        copy.start()

    for n in range(4):
        pre = nt(w.kind_panels(4 + n), whole[...])
        at_bias = 2 * HD + n * HD
        pre = pre + jnp.concatenate([bias_t[at_bias : at_bias + HD, u : u + 1] for u in range(GROUPS)], axis=0)
        value, slope = gelu_parts(pre)
        d_act = nt(w.kind_panels(8 + n), dffn[...])
        low_value, low_grad = value.astype(BF), (d_act * slope).astype(BF)
        units = slice(n * SPAN, (n + 1) * SPAN)
        gt[units, :] = low_value
        dft[units, :] = low_grad
        g_rows[:, units] = low_value.T
        turned = low_grad.T
        df_rows[:, units] = turned
        unit_out[2 + n : 3 + n, :] = jnp.sum(turned.astype(F32), axis=0, keepdims=True)
    unit_out[0:2, :] = jnp.zeros((2, SPAN), F32)
    unit_out[6:8, :] = jnp.zeros((2, SPAN), F32)
    gt_out[...] = gt[...]
    dft_out[...] = dft[...]

    def feed(n, carry):
        cols = pl.ds(pl.multiple_of(n * 256, 256), 256)
        dn2_out[:, cols] = nn(df_rows[...], w.kind_columns(4, 4, cols)).astype(BF)
        ffn_out[:, cols] = nn(g_rows[...], w.kind_columns(8, 4, cols)).astype(BF)
        return carry

    lax.fori_loop(0, WIDTH // 256, feed, 0)

    for k in range(4):
        for i in range(3):
            w.drain(k, i)
    mine_kv = window.at[0, p.c]
    for d in range(1, 5):
        @pl.when(p.chip + d < 8)
        def _():
            remote(mine_kv, mine_kv, kv_send.at[d], kv_recv.at[d], p.sibling()).wait_send()
    for d in range(5):
        @pl.when(p.chip - d >= 0)
        def _():
            remote(mine_kv, mine_kv, kv_bsend.at[d], kv_brecv.at[d], p.sibling()).wait_send()
    for copy in out_copies:
        copy.wait()


def forward_call(lengths, tokens, cotangent, alive_row, alive_col, panels, bias_t, gains, shifts):
    vmem = pl.BlockSpec(memory_space=pltpu.VMEM)
    anywhere = pl.BlockSpec(memory_space=pl.ANY)
    shape = jax.ShapeDtypeStruct
    dma = pltpu.SemaphoreType.DMA
    return pl.pallas_call(
        forward_kernel,
        in_specs=[pl.BlockSpec(memory_space=pltpu.SMEM)] + [vmem] * 8,
        out_specs=[anywhere, anywhere, anywhere, vmem, vmem, vmem, anywhere, vmem, vmem, vmem, vmem, anywhere, anywhere, vmem],
        out_shape=[
            shape((ROWS, WIDTH), BF),
            shape((SPAN, ROWS), BF),
            shape((5, 2, EXT, 2 * SPAN), BF),
            shape((SPAN, ROWS), F32),
            shape((8, ROWS), F32),
            shape((SHARD, WIDTH), F32),
            shape((ROWS, WIDTH), BF),
            shape((UNITS, ROWS), BF),
            shape((UNITS, ROWS), BF),
            shape((ROWS, WIDTH), BF),
            shape((ROWS, WIDTH), BF),
            shape((GROUPS, 4, HD, WIDTH), BF),
            shape((ROWS, WIDTH), BF),
            shape((8, SPAN), F32),
        ],
        scratch_shapes=[
            pltpu.VMEM((16, 3, HD, WIDTH), BF),
            pltpu.VMEM((5, 2, EXT, 2 * SPAN), BF),
            pltpu.VMEM((ROWS, WIDTH), BF),
            pltpu.VMEM((SPAN, ROWS), BF),
            pltpu.VMEM((SPAN, ROWS), F32),
            pltpu.VMEM((8, ROWS), F32),
            pltpu.VMEM((8, ROWS), F32),
            pltpu.VMEM((ROWS, WIDTH), BF),
            pltpu.VMEM((7, SHARD, WIDTH), BF),
            pltpu.VMEM((ROWS, WIDTH), BF),
            pltpu.VMEM((ROWS, UNITS), BF),
            pltpu.VMEM((ROWS, UNITS), BF),
            pltpu.VMEM((UNITS, ROWS), BF),
            pltpu.VMEM((UNITS, ROWS), BF),
            pltpu.VMEM((ROWS, WIDTH), BF),
            dma((16, 3)), dma((3,)), dma((2, 2, 3)), dma((2, 2, 3)), dma((2, 2, 3)), dma((2, 4, 3)),
            dma((5,)), dma((5,)), dma((5,)), dma((5,)),
            dma((7,)), dma((7,)), dma((7,)), dma((7,)), dma((13,)),
        ],
        compiler_params=pltpu.CompilerParams(
            collective_id=0, has_side_effects=True, vmem_limit_bytes=56 * 2**20
        ),
        name="layer_forward",
    )(lengths, tokens, cotangent, alive_row, alive_col, panels, bias_t, gains, shifts)


def head_columns(values, head):
    owner = lax.broadcasted_iota(jnp.int32, values.shape, 1) // HD
    return jnp.where(owner == head, values, jnp.zeros_like(values))


def norm_back(grad, unit, factor, gain):
    d_gain = jnp.sum(grad * unit, axis=0, keepdims=True)
    d_shift = jnp.sum(grad, axis=0, keepdims=True)
    d_unit = grad * gain
    d_in = factor * (
        d_unit
        - jnp.mean(d_unit, axis=-1, keepdims=True)
        - unit * jnp.mean(d_unit * unit, axis=-1, keepdims=True)
    )
    return d_in, d_gain, d_shift


class PanelSums:
    def __init__(self, place, grads, pair, half, line, last, result, sems):
        self.p, self.grads = place, grads
        self.pair, self.half, self.line, self.last, self.result = pair, half, line, last, result
        self.pair_send, self.pair_recv, self.half_send, self.half_recv = sems[:4]
        self.line_send, self.line_recv, self.last_send, self.last_recv = sems[4:]

    def pair_copy(self, u, k, i):
        return remote(
            self.grads.at[4 * u + k, i],
            self.pair.at[2 * u + k // 2, i],
            self.pair_send.at[2 * u + k // 2, i],
            self.pair_recv.at[2 * u + k // 2, i],
            self.p.sibling(),
        )

    def to_pair(self, k, i):
        @pl.when(self.p.c != k % 2)
        def _():
            for u in range(GROUPS):
                self.pair_copy(u, k, i).start()

    def half_copy(self, n, k, i):
        rows = pl.ds(n * HALF, HALF)
        return remote(
            self.grads.at[4 * ((self.p.z + 2) % 4) + k, i, rows],
            self.half.at[k // 2, n, i],
            self.half_send.at[k // 2, n, i],
            self.half_recv.at[k // 2, n, i],
            self.p.along(NEAR[n]),
        )

    def line_copy(self, n, k, i):
        return remote(
            self.grads.at[4 * ((self.p.z + NEAR[n]) % 4) + k, i],
            self.line.at[k // 2, n, i],
            self.line_send.at[k // 2, n, i],
            self.line_recv.at[k // 2, n, i],
            self.p.along(NEAR[n]),
        )

    def pair_add(self, k, i):
        @pl.when(self.p.c == k % 2)
        def _():
            def add(step, carry):
                u, rows = step // 4, pl.ds(pl.multiple_of((step % 4) * 16, 16), 16)
                self.grads[4 * u + k, i, rows, :] = (
                    self.grads[4 * u + k, i, rows, :].astype(F32)
                    + self.pair[2 * u + k // 2, i, rows, :].astype(F32)
                ).astype(BF)
                return carry

            for u in range(GROUPS):
                self.pair_copy(u, k, i).wait_recv()
            lax.fori_loop(0, 4 * GROUPS, add, 0)
            for n in (0, 1):
                self.half_copy(n, k, i).start()

    def line_mid(self, k, i):
        @pl.when(self.p.c == k % 2)
        def _():
            for n in (0, 1):
                self.half_copy(n, k, i).wait_recv()
                which = 4 * ((self.p.z + NEAR[n]) % 4) + k

                def add(step, carry):
                    here = pl.ds(pl.multiple_of(step * 16, 16), 16)
                    rows = pl.ds(pl.multiple_of(n * HALF + step * 16, 16), 16)
                    self.grads[which, i, rows, :] = (
                        self.grads[which, i, rows, :].astype(F32)
                        + self.half[k // 2, n, i, here, :].astype(F32)
                    ).astype(BF)
                    return carry

                lax.fori_loop(0, HALF // 16, add, 0)
                self.line_copy(n, k, i).start()

    def across_copy(self, k, i):
        return remote(
            self.grads.at[4 * self.p.z + k, i],
            self.last.at[i],
            self.last_send.at[i],
            self.last_recv.at[i],
            self.p.across(),
        )

    def line_add(self, k, i):
        @pl.when(self.p.c == k % 2)
        def _():
            for n in (0, 1):
                self.line_copy(n, k, i).wait_recv()

            def add(step, carry):
                rows = pl.ds(pl.multiple_of(step * 16, 16), 16)
                total = self.grads[4 * self.p.z + k, i, rows, :].astype(F32)
                for n in (0, 1):
                    total = total + self.line[k // 2, n, i, rows, :].astype(F32)
                self.grads[4 * self.p.z + k, i, rows, :] = total.astype(BF)

                @pl.when(self.p.x == k // 2)
                def _():
                    self.result[i, rows, :] = total

                return carry

            lax.fori_loop(0, HD // 16, add, 0)

            @pl.when(self.p.x != k // 2)
            def _():
                self.across_copy(k, i).start()

    def last_add(self, i):
        own = 2 * self.p.x + self.p.c
        self.across_copy(own, i).wait_recv()
        self.result[i] = self.result[i] + self.last[i].astype(F32)

    def drain(self):
        for k in range(4):
            for i in range(3):
                @pl.when(self.p.c != k % 2)
                def _():
                    for u in range(GROUPS):
                        self.pair_copy(u, k, i).wait_send()

                @pl.when(self.p.c == k % 2)
                def _():
                    for n in (0, 1):
                        self.half_copy(n, k, i).wait_send()
                        self.line_copy(n, k, i).wait_send()

                    @pl.when(self.p.x != k // 2)
                    def _():
                        self.across_copy(k, i).wait_send()


def backward_kernel(
    lengths, alive_row, alive_col, gains, shifts, dn2_part, gt, dft, ot, lse, hidden, unit_rows, qt,
    tokens_any, cot_any, dffn_any, low2_any, low1_any, window_any, proj_any, ffn_any,
    out_any, grad_any, result, vec_out, unit_out,
    grads, pair, half, line, last, window, d_kv, kv_pair, kv_far, dffn, low2, low1, proj, ffn_part, x_mine, cot_mine,
    branch, out_whole, in_whole, dn1_part, land, q_rows, q_cols, do_rows, do_cols, delta, dqt, dkv_sum, d_hidden,
    bank, bank_land, small, small_pair, small_all, bank_back,
    rs_send, rs_recv, ag_send, ag_recv, pair_send, pair_recv, half_send, half_recv,
    line_send, line_recv, last_send, last_recv, kv_bsend, kv_brecv, kv_send, kv_recv, v1_send, v1_recv, v2_send, v2_recv, v3_send, v3_recv, v4_send, v4_recv,
    load_sem, out_sem,
):
    p = Place()
    sums = PanelSums(
        p, grads, pair, half, line, last, result,
        (pair_send, pair_recv, half_send, half_recv, line_send, line_recv, last_send, last_recv),
    )
    mine = pl.ds(pl.multiple_of(p.t * SHARD, SHARD), SHARD)
    sources = [
        (dffn_any, dffn), (low2_any, low2), (tokens_any.at[mine], x_mine), (cot_any.at[mine], cot_mine),
        (proj_any, proj), (window_any, window), (low1_any, low1), (ffn_any, ffn_part),
    ]
    loads = [pltpu.make_async_copy(a, b, load_sem.at[n]) for n, (a, b) in enumerate(sources)]
    for load in loads:
        load.start()
    p.greet()
    first_scatter = scatter_copies(p, dn2_part, land.at[0], rs_send.at[0], rs_recv.at[0])
    for copy in first_scatter:
        copy.start()

    def kinds_grad(j, left, right):
        def tile(n, carry):
            cols = pl.ds(pl.multiple_of(n * 256, 256), 256)
            made = nn(left, right[:, cols]).astype(BF)
            for u in range(GROUPS):
                grads[4 * u + j // 3, j % 3, :, cols] = made[u * HD : (u + 1) * HD]
            return carry

        lax.fori_loop(0, WIDTH // 256, tile, 0)

    loads[0].wait()
    loads[1].wait()
    early = []
    for j in (9, 8, 4, 10, 6, 5, 11, 7):
        n = j % 4
        if j >= 8:
            kinds_grad(j, gt[n * SPAN : (n + 1) * SPAN, :], dffn)
        else:
            kinds_grad(j, dft[n * SPAN : (n + 1) * SPAN, :], low2)
        sums.to_pair(j // 3, j % 3)
        early.append((j // 3, j % 3))
        if len(early) > 1:
            sums.pair_add(*early[-2])
        if len(early) > 4:
            sums.line_mid(*early[-5])

    loads[2].wait()
    loads[3].wait()
    live = alive_col[mine, :]
    grad_out = cot_mine[...].astype(F32)
    _, unit2, factor2 = normalize(hidden[...], gains[1:2, :], shifts[3:4, :])
    for copy in first_scatter:
        copy.wait()
    d_norm2 = scatter_sum(p, dn2_part, land.at[0])
    d_in, d_gain2, d_shift2 = norm_back(d_norm2, unit2, factor2, gains[1:2, :])
    d_hidden[...] = grad_out + d_in
    d_branch = (live * d_hidden[...]).astype(BF)
    branch[mine, :] = d_branch
    first_gather = gather_copies(p, branch, ag_send.at[0], ag_recv.at[0])
    for copy in first_gather:
        copy.start()

    def to_bank(row, values):
        for n in range(8):
            bank[n, row : row + 1, :] = values[:, n * 256 : (n + 1) * 256]

    to_bank(1, d_gain2)
    to_bank(2, jnp.sum(d_branch.astype(F32), axis=0, keepdims=True))
    to_bank(3, jnp.sum(live * grad_out, axis=0, keepdims=True))
    to_bank(5, d_shift2)
    to_bank(6, jnp.zeros((1, WIDTH), F32))
    to_bank(7, jnp.zeros((1, WIDTH), F32))

    sums.pair_add(*early[-1])
    for k, i in early[-4:]:
        sums.line_mid(k, i)

    loads[4].wait()
    loads[5].wait()
    scaled = (qt[...].astype(F32) * (HD ** -0.5)).astype(BF)
    scaled_rows = scaled.T
    for u in range(GROUPS):
        q_rows[u] = head_rows(scaled, u)
        q_cols[u] = head_columns(scaled_rows, u)
    dqt[...] = jnp.zeros_like(dqt)
    dkv_sum[...] = jnp.zeros_like(dkv_sum)
    code, at = query_code(p, lengths, alive_row[...])

    for copy in first_gather:
        copy.wait()
    w_out = jnp.concatenate([proj[u, 3] for u in range(GROUPS)], axis=0)
    do_t = nt(w_out, branch[...]).astype(BF)
    do_turned = do_t.T
    for u in range(GROUPS):
        heads = slice(u * HD, (u + 1) * HD)
        do_rows[u] = head_rows(do_t, u)
        do_cols[u] = head_columns(do_turned, u)
        delta[u : u + 1, :] = jnp.sum(do_t[heads, :].astype(F32) * ot[heads, :], axis=0, keepdims=True)
    loads[7].wait()
    out_scatter = scatter_copies(p, ffn_part, land.at[1], rs_send.at[1], rs_recv.at[1])
    for copy in out_scatter:
        copy.start()
    kinds_grad(3, ot[...].astype(BF), branch)
    sums.to_pair(1, 0)

    def kv_pair_copy(d):
        return remote(d_kv.at[d, 1 - p.c], kv_pair.at[d], kv_bsend.at[d], kv_brecv.at[d], p.sibling())

    def kv_far_copy(d):
        return remote(d_kv.at[d, p.c], kv_far.at[d], kv_send.at[d], kv_recv.at[d], p.chip_at(-d))

    def finish(d):
        @pl.when(p.chip - d >= 0)
        def _():
            @pl.when(((p.c == 0) & (d <= 3)) | ((p.c == 1) & (d >= 1)))
            def _():
                kv_pair_copy(d).wait_recv()
                d_kv[d, p.c] = (d_kv[d, p.c].astype(F32) + kv_pair[d].astype(F32)).astype(BF)

            @pl.when(d >= 1)
            def _():
                kv_far_copy(d).start()

    def block_back(step, carry):
        d = 4 - step // 2
        core = (1 - p.c + step) % 2
        use = (p.chip - d >= 0) & ~((d == 0) & (core > p.c)) & ~((d == 4) & (core < p.c))

        @pl.when(use)
        def _():
            bias = block_bias(p, lengths, window, d, core, code, at)
            keys = window[d, core, 0:ROWS, 0:SPAN]
            values = window[d, core, 0:ROWS, SPAN : 2 * SPAN]
            keys_t = keys.T
            d_key = jnp.zeros((ROWS, SPAN), F32)
            d_value = jnp.zeros((ROWS, SPAN), F32)
            for u in range(GROUPS):
                heads = slice(u * HD, (u + 1) * HD)
                prob = jnp.exp(nn(keys, q_rows[u]) + bias - lse[u : u + 1, :])
                d_prob = nn(values, do_rows[u])
                d_score = (prob * (d_prob - delta[u : u + 1, :])).astype(BF)
                d_value = d_value + nn(prob.astype(BF), do_cols[u])
                d_key = d_key + nn(d_score, q_cols[u])
                dqt[heads, :] = dqt[heads, :] + nn(keys_t[heads, :], d_score)
            d_kv[d, core, :, 0:SPAN] = d_key.astype(BF)
            d_kv[d, core, :, SPAN : 2 * SPAN] = d_value.astype(BF)

            @pl.when(core != p.c)
            def _():
                kv_pair_copy(d).start()

        @pl.when((step % 2 == 1) & (step > 1))
        def _():
            finish(d + 1)

        return carry

    lax.fori_loop(0, 10, block_back, 0)
    finish(0)
    sums.pair_add(1, 0)

    dq_t = (dqt[...] * (HD ** -0.5)).astype(BF)
    dq = dq_t.T
    small[8:16, :] = unit_rows[...]
    small[8:9, :] = jnp.sum(dq.astype(F32), axis=0, keepdims=True)
    loads[6].wait()
    kinds_grad(0, dq_t, low1)
    sums.to_pair(0, 0)

    for copy in out_scatter:
        copy.wait()
    summed = scatter_sum(p, ffn_part, land.at[1])
    out_whole[mine, :] = (hidden[...] + live * (summed + shifts[1:2, :])).astype(BF)
    out_gather = gather_copies(p, out_whole, ag_send.at[1], ag_recv.at[1])
    for copy in out_gather:
        copy.start()
    sums.pair_add(0, 0)
    for k, i in early:
        sums.line_add(k, i)

    dkv_sum[...] = d_kv[0, p.c].astype(F32)
    for d in (1, 2, 3, 4):
        @pl.when(p.chip + d < 8)
        def _():
            kv_far_copy(d).wait_recv()
            dkv_sum[...] = dkv_sum[...] + kv_far[d].astype(F32)

    dkv = dkv_sum[...].astype(BF)
    dkv_t = dkv.T
    small[9:10, :] = jnp.sum(dkv[:, SPAN:].astype(F32), axis=0, keepdims=True)

    def norm1_part(n, carry):
        cols = pl.ds(pl.multiple_of(n * 256, 256), 256)
        total = jnp.zeros((ROWS, 256), F32)
        for i, left in enumerate((dq, dkv[:, :SPAN], dkv[:, SPAN:])):
            total = total + nn(left, jnp.concatenate([proj[u, i, :, cols] for u in range(GROUPS)], axis=0))
        dn1_part[:, cols] = total.astype(BF)
        return carry

    lax.fori_loop(0, WIDTH // 256, norm1_part, 0)
    last_scatter = scatter_copies(p, dn1_part, land.at[2], rs_send.at[2], rs_recv.at[2])
    for copy in last_scatter:
        copy.start()
    kinds_grad(1, dkv_t[:SPAN], low1)
    sums.to_pair(0, 1)
    kinds_grad(2, dkv_t[SPAN:], low1)
    sums.to_pair(0, 2)
    sums.line_mid(1, 0)
    sums.line_mid(0, 0)
    for i in (1, 2):
        sums.pair_add(0, i)
    sums.line_add(1, 0)
    for i in (1, 2):
        sums.line_mid(0, i)

    _, unit1, factor1 = normalize(x_mine[...].astype(F32), gains[0:1, :], shifts[2:3, :])
    for copy in last_scatter:
        copy.wait()
    d_norm1 = scatter_sum(p, dn1_part, land.at[2])
    d_in, d_gain1, d_shift1 = norm_back(d_norm1, unit1, factor1, gains[0:1, :])
    in_whole[mine, :] = (d_hidden[...] + d_in).astype(BF)
    to_bank(0, d_gain1)
    to_bank(4, d_shift1)

    slices = []
    for n, (dy, dx) in enumerate(T_STEPS):
        to = p.tensor_at(dy, dx)
        slices.append(remote(bank.at[to], bank_land.at[n], v1_send.at[n], v1_recv.at[n], {"tensor": to}))
    for copy in slices:
        copy.start()
    last_gather = gather_copies(p, in_whole, ag_send.at[2], ag_recv.at[2])
    for copy in last_gather:
        copy.start()
    for i in range(3):
        sums.line_add(0, i)
    for copy in slices:
        copy.wait()
    total = bank[p.t]
    for n in range(len(T_STEPS)):
        total = total + bank_land[n]
    small[0:8, :] = total
    pair_small = remote(small, small_pair, v2_send, v2_recv, p.sibling())
    pair_small.start()
    pair_small.wait()
    here = p.z * 2 + p.x
    small_all[here] = small[...] + small_pair[...]
    spread = []
    for n in range(1, 8):
        to = p.seq((p.z + n // 2) % 4, (p.x + n % 2) % 2, p.c)
        spread.append(remote(small_all.at[here], small_all.at[here], v3_send.at[n - 1], v3_recv.at[n - 1], to))
    for copy in spread:
        copy.start()
    for i in range(3):
        sums.last_add(i)
    for copy in spread:
        copy.wait()
    total = small_all[0]
    for n in range(1, 8):
        total = total + small_all[n]
    bank_back[p.t] = total[0:8, :]
    unit_out[...] = total[8:16, :]
    back = []
    for n, (dy, dx) in enumerate(T_STEPS):
        to = {"tensor": p.tensor_at(dy, dx)}
        back.append(remote(bank_back.at[p.t], bank_back.at[p.t], v4_send.at[n], v4_recv.at[n], to))
    for copy in back:
        copy.start()

    for copy in out_gather:
        copy.wait()
    for copy in last_gather:
        copy.wait()
    stores = [
        pltpu.make_async_copy(out_whole, out_any, out_sem.at[0]),
        pltpu.make_async_copy(in_whole, grad_any, out_sem.at[1]),
    ]
    for copy in stores:
        copy.start()
    for copy in back:
        copy.wait()
    vec_out[...] = bank_back[...]
    sums.drain()
    for d in range(5):
        @pl.when((p.chip - d >= 0) & (((p.c == 1) & (d <= 3)) | ((p.c == 0) & (d >= 1))))
        def _():
            kv_pair_copy(d).wait_send()

        if d >= 1:
            @pl.when(p.chip - d >= 0)
            def _():
                kv_far_copy(d).wait_send()

    for copy in stores:
        copy.wait()


def backward_call(
    lengths, alive_row, alive_col, gains, shifts, dn2_part, gt, dft, ot, lse, hidden, unit_rows, qt,
    tokens, cotangent, dffn, low2, low1, window, proj, ffn_part,
):
    vmem = pl.BlockSpec(memory_space=pltpu.VMEM)
    anywhere = pl.BlockSpec(memory_space=pl.ANY)
    shape = jax.ShapeDtypeStruct
    dma = pltpu.SemaphoreType.DMA
    rows_low = pltpu.VMEM((ROWS, WIDTH), BF)
    shard_low = pltpu.VMEM((SHARD, WIDTH), BF)
    masked = pltpu.VMEM((GROUPS, SPAN, ROWS), BF)
    return pl.pallas_call(
        backward_kernel,
        in_specs=[pl.BlockSpec(memory_space=pltpu.SMEM)] + [vmem] * 12 + [anywhere] * 8,
        out_specs=[anywhere, anywhere, vmem, vmem, vmem],
        out_shape=[
            shape((ROWS, WIDTH), BF),
            shape((ROWS, WIDTH), BF),
            shape((3, HD, WIDTH), F32),
            shape((8, 8, 256), F32),
            shape((8, SPAN), F32),
        ],
        scratch_shapes=[
            pltpu.VMEM((16, 3, HD, WIDTH), BF),
            pltpu.VMEM((8, 3, HD, WIDTH), BF),
            pltpu.VMEM((2, 2, 3, HALF, WIDTH), BF),
            pltpu.VMEM((2, 2, 3, HD, WIDTH), BF),
            pltpu.VMEM((3, HD, WIDTH), BF),
            pltpu.VMEM((5, 2, EXT, 2 * SPAN), BF),
            pltpu.VMEM((5, 2, ROWS, 2 * SPAN), BF),
            pltpu.VMEM((5, ROWS, 2 * SPAN), BF),
            pltpu.VMEM((5, ROWS, 2 * SPAN), BF),
            rows_low, rows_low, rows_low,
            pltpu.VMEM((GROUPS, 4, HD, WIDTH), BF),
            rows_low, shard_low, shard_low,
            rows_low, rows_low, rows_low, rows_low,
            pltpu.VMEM((3, 7, SHARD, WIDTH), BF),
            masked, masked, masked, masked,
            pltpu.VMEM((8, ROWS), F32),
            pltpu.VMEM((SPAN, ROWS), F32),
            pltpu.VMEM((ROWS, 2 * SPAN), F32),
            pltpu.VMEM((SHARD, WIDTH), F32),
            pltpu.VMEM((8, 8, 256), F32),
            pltpu.VMEM((7, 8, 256), F32),
            pltpu.VMEM((16, 256), F32),
            pltpu.VMEM((16, 256), F32),
            pltpu.VMEM((8, 16, 256), F32),
            pltpu.VMEM((8, 8, 256), F32),
            dma((3, 7)), dma((3, 7)), dma((3, 7)), dma((3, 7)),
            dma((8, 3)), dma((8, 3)), dma((2, 2, 3)), dma((2, 2, 3)), dma((2, 2, 3)), dma((2, 2, 3)), dma((3,)), dma((3,)),
            dma((5,)), dma((5,)), dma((5,)), dma((5,)),
            dma((7,)), dma((7,)), dma, dma, dma((7,)), dma((7,)), dma((7,)), dma((7,)),
            dma((8,)), dma((2,)),
        ],
        compiler_params=pltpu.CompilerParams(
            collective_id=1, has_side_effects=True, vmem_limit_bytes=60 * 2**20
        ),
        name="layer_backward",
    )(
        lengths, alive_row, alive_col, gains, shifts, dn2_part, gt, dft, ot, lse, hidden, unit_rows, qt,
        tokens, cotangent, dffn, low2, low1, window, proj, ffn_part,
    )


def high(left, right):
    return jnp.dot(left, right, precision=HIGH, preferred_element_type=F32)


def muon_kernel(grads, panel_mom, panels, new_panels, new_mom):
    count = panels.shape[0]
    eye = jnp.where(
        lax.broadcasted_iota(jnp.int32, (HD, HD), 0) == lax.broadcasted_iota(jnp.int32, (HD, HD), 1), 1.0, 0.0
    )
    scale, gram, chain = [], [], [None] * count
    for n in range(count):
        moment = DECAY * panel_mom[n] + grads[n]
        new_mom[n] = moment
        factor = lax.rsqrt(jnp.sum(moment * moment, axis=(0, 1), keepdims=True) + 1e-06)
        current = moment * factor
        scale.append(factor)
        gram.append(
            lax.dot_general(
                current, current, (((1,), (1,)), ((), ())), precision=HIGH, preferred_element_type=F32
            )
        )
    for sweep in range(NS_ITERS):
        squares = [high(a, a) for a in gram]
        steps = [NS_A * eye + NS_B * a + NS_C * s for a, s in zip(gram, squares)]
        chain = [m if sweep == 0 else high(m, c) for m, c in zip(steps, chain)]
        if sweep < NS_ITERS - 1:
            halves = [high(m, a) for m, a in zip(steps, gram)]
            gram = [high(h, m) for h, m in zip(halves, steps)]
    for n in range(count):
        direction = high(chain[n], new_mom[n] * scale[n])
        size_u = jnp.sum(direction * direction, axis=(0, 1), keepdims=True)
        held = panels[n]
        size_w = jnp.sum(held * held, axis=(0, 1), keepdims=True)
        new_panels[n] = held - LR_MATRIX * jnp.sqrt(size_w) * lax.rsqrt(size_u + 1e-06) * direction


def muon_call(grads, panel_mom, panels):
    vmem = pl.BlockSpec(memory_space=pltpu.VMEM)
    shape = jax.ShapeDtypeStruct(panels.shape, F32)
    return pl.pallas_call(
        muon_kernel,
        in_specs=[vmem] * 3,
        out_specs=[vmem, vmem],
        out_shape=[shape, shape],
        compiler_params=pltpu.CompilerParams(vmem_limit_bytes=32 * 2**20),
        name="panel_step",
    )(grads, panel_mom, panels)


def per_device(
    tokens, cotangent, exits, lengths, panels, panel_mom,
    unit_bias, unit_bias_mom, gains, gains_mom, vec_bias, vec_bias_mom,
):
    live = (exits >= LAYER).astype(F32)
    alive_row, alive_col = live[None, :], live[:, None]
    (
        low1, qt, window, ot, lse, hidden, low2, gt, dft, ffn_part, dn2_part, proj, dffn, unit_rows,
    ) = forward_call(
        lengths, tokens, cotangent, alive_row, alive_col, panels, unit_bias.T, gains, vec_bias
    )
    output, input_grad, panel_grads, vec_sums, unit_sums = backward_call(
        lengths, alive_row, alive_col, gains, vec_bias, dn2_part, gt, dft, ot, lse, hidden, unit_rows, qt,
        tokens, cotangent, dffn, low2, low1, window, proj, ffn_part,
    )
    new_panels, moment = muon_call(panel_grads, panel_mom, panels)
    vec_sums = vec_sums.transpose(1, 0, 2).reshape(8, WIDTH)
    unit_sum = unit_sums[0:6].reshape(6, GROUPS, HD).transpose(1, 0, 2).reshape(GROUPS, 6 * HD)
    unit_moment = DECAY * unit_bias_mom + unit_sum
    gains_moment = DECAY * gains_mom + vec_sums[0:2]
    vec_moment = DECAY * vec_bias_mom + vec_sums[2:6]
    return (
        output, input_grad.astype(F32), new_panels, moment,
        unit_bias - LR_VECTOR * unit_moment, unit_moment,
        gains - LR_VECTOR * gains_moment, gains_moment,
        vec_bias - LR_VECTOR * vec_moment, vec_moment,
    )


def solution(mesh):
    held = P(("tensor", "seq"), None, None)
    return jax.shard_map(
        per_device,
        mesh=mesh,
        in_specs=(
            P("seq", None), P("seq", None), P("seq"), P(), held, held,
            P("tensor", None), P("tensor", None), P(), P(), P(), P(),
        ),
        out_specs=(
            P("seq", None), P("seq", None), held, held,
            P("tensor", None), P("tensor", None), P(), P(), P(), P(),
        ),
        check_vma=False,
    )
```

```python
import functools
import math

import jax
import jax.numpy as jnp
from jax import lax
from jax.experimental import pallas as pl
from jax.experimental.pallas import tpu as pltpu
from jax.sharding import PartitionSpec as P

LAYER = 12
NS_ITERS = 5
EPS = 1e-05
NS_A = 3.4445
NS_B = -4.775
NS_C = 2.0315
LR_MATRIX = 0.5
LR_VECTOR = 0.002
DECAY = 0.5
HIGH = lax.Precision.HIGHEST
MESH = pl.DeviceIdType.MESH

ROWS = 256
WIDTH = 2048
GROUPS = 4
HD = 64
SPAN = GROUPS * HD
UNITS = 4 * SPAN
SHARD = 32
EXT = ROWS + 16
MASKED = -1e30
FLOOR = -1e28
BF = jnp.bfloat16
F32 = jnp.float32

NEAR = (1, 3)
HALF = 32
T_STEPS = tuple((dy, dx) for dy in (2, 1, 3, 0) for dx in (1, 0) if (dy, dx) != (0, 0))


def nt(left, right):
    return lax.dot_general(left, right, (((1,), (1,)), ((), ())), preferred_element_type=F32)


def nn(left, right):
    return jnp.dot(left, right, preferred_element_type=F32)


def normalize(values, gain, shift):
    mean = jnp.mean(values, axis=-1, keepdims=True)
    centred = values - mean
    factor = lax.rsqrt(jnp.mean(centred * centred, axis=-1, keepdims=True) + EPS)
    return centred * factor * gain + shift, centred * factor, factor


class Place:
    def __init__(self):
        self.s = lax.axis_index("seq")
        self.t = lax.axis_index("tensor")
        self.z, self.x, self.c = self.s // 4, (self.s // 2) % 2, self.s % 2
        self.chip = self.s // 2
        self.y, self.h = self.t // 2, self.t % 2

    def seq(self, z, x, c):
        return {"seq": z * 4 + x * 2 + c}

    def sibling(self):
        return self.seq(self.z, self.x, 1 - self.c)

    def across(self):
        return self.seq(self.z, 1 - self.x, self.c)

    def along(self, step):
        return self.seq((self.z + step) % 4, self.x, self.c)

    def chip_at(self, step):
        return {"seq": (self.chip + step) * 2 + self.c}

    def tensor_at(self, dy, dx):
        return ((self.y + dy) % 4) * 2 + (self.h + dx) % 2

    def greet(self):
        barrier = pltpu.get_barrier_semaphore()
        count = 0
        for dz in range(4):
            for dx in range(2):
                if (dz, dx) != (0, 0):
                    to = self.seq((self.z + dz) % 4, (self.x + dx) % 2, self.c)
                    pl.semaphore_signal(barrier, inc=1, device_id=to, device_id_type=MESH)
                    count += 1
        pl.semaphore_signal(barrier, inc=1, device_id=self.sibling(), device_id_type=MESH)
        count += 1
        for dy, dx in T_STEPS:
            to = {"tensor": self.tensor_at(dy, dx)}
            pl.semaphore_signal(barrier, inc=1, device_id=to, device_id_type=MESH)
            count += 1
        pl.semaphore_wait(barrier, count)


def remote(src, dst, send, recv, to):
    return pltpu.make_async_remote_copy(
        src_ref=src, dst_ref=dst, send_sem=send, recv_sem=recv, device_id=to, device_id_type=MESH
    )


def scatter_copies(place, part, land, send, recv):
    out = []
    for i, (dy, dx) in enumerate(T_STEPS):
        to = place.tensor_at(dy, dx)
        rows = pl.ds(pl.multiple_of(to * SHARD, SHARD), SHARD)
        out.append(remote(part.at[rows], land.at[i], send.at[i], recv.at[i], {"tensor": to}))
    return out


def scatter_sum(place, part, land):
    mine = pl.ds(pl.multiple_of(place.t * SHARD, SHARD), SHARD)
    total = part[mine, :].astype(F32)
    for i in range(len(T_STEPS)):
        total = total + land[i].astype(F32)
    return total


def gather_copies(place, whole, send, recv):
    mine = pl.ds(pl.multiple_of(place.t * SHARD, SHARD), SHARD)
    out = []
    for i, (dy, dx) in enumerate(T_STEPS):
        to = place.tensor_at(dy, dx)
        out.append(remote(whole.at[mine], whole.at[mine], send.at[i], recv.at[i], {"tensor": to}))
    return out


def column_of(row):
    n = row.shape[1]
    down = lax.broadcasted_iota(jnp.int32, (n, n), 0)
    over = lax.broadcasted_iota(jnp.int32, (n, n), 1)
    return jnp.sum(jnp.where(down == over, row, 0.0), axis=1, keepdims=True)


def alive_of(exits):
    return jnp.where(exits[...] >= LAYER, 1.0, 0.0)


def segment_of(positions, lengths):
    end = jnp.int32(0)
    segment = jnp.zeros(positions.shape, F32)
    for i in range(4):
        end = end + lengths[i]
        segment = segment + jnp.where(positions >= end, 1.0, 0.0)
    return segment


def query_code(place, lengths, alive_row):
    at = place.s * ROWS + lax.broadcasted_iota(jnp.int32, (1, ROWS), 1)
    return jnp.where(alive_row > 0.5, segment_of(at, lengths), -2.0), at


def block_bias(place, lengths, window, dist, core, code, at):
    first = ((place.chip - dist) * 2 + core) * ROWS
    keys = first + lax.broadcasted_iota(jnp.int32, (ROWS, 1), 0)
    live = column_of(window[dist, core, ROWS:EXT, 0:ROWS].astype(F32)[0:1])
    key_code = jnp.where(live > 0.5, segment_of(keys, lengths), -1.0)
    same = jnp.where(key_code == code, 0.0, MASKED)
    return jnp.where(keys <= at, same, MASKED)


def head_rows(values, head):
    owner = lax.broadcasted_iota(jnp.int32, values.shape, 0) // HD
    return jnp.where(owner == head, values, jnp.zeros_like(values))


class Panels:
    def __init__(self, place, store, recv, across, along, half_send, half_recv, beside):
        self.p, self.store, self.recv = place, store, recv
        self.sx, self.sz, self.sh, self.rh, self.sc = across, along, half_send, half_recv, beside

    def piece(self, which, i, send, to):
        ref = self.store.at[which, i]
        return remote(ref, ref, send, self.recv.at[which, i], to)

    def across_copy(self, k, i):
        return self.piece(4 * self.p.z + k, i, self.sx.at[i], self.p.across())

    def along_copy(self, k, i, n):
        return self.piece(4 * self.p.z + k, i, self.sz.at[k // 2, n, i], self.p.along(NEAR[n]))

    def half_copy(self, k, i, n):
        which = 4 * ((self.p.z - NEAR[n]) % 4) + k
        ref = self.store.at[which, i, pl.ds(n * HALF, HALF)]
        return remote(ref, ref, self.sh.at[k // 2, n, i], self.rh.at[k // 2, n, i], self.p.along(NEAR[n]))

    def beside_copy(self, k, i, slot):
        which = 4 * ((self.p.z - (0, 1, 3, 2)[slot]) % 4) + k
        return self.piece(which, i, self.sc.at[k // 2, slot, i], self.p.sibling())

    def arrived(self, which, i):
        self.piece(which, i, self.sx.at[0], self.p.sibling()).wait_recv()

    def across(self, k, i):
        @pl.when((self.p.c == k % 2) & (self.p.x == k // 2))
        def _():
            self.across_copy(k, i).start()

    def along(self, k, i, ways=(0, 1), first=True):
        @pl.when(self.p.c == k % 2)
        def _():
            if first:
                @pl.when(self.p.x != k // 2)
                def _():
                    self.arrived(4 * self.p.z + k, i)

            for n in ways:
                self.along_copy(k, i, n).start()
            if first:
                self.beside_copy(k, i, 0).start()

    def pass_on(self, k, i):
        @pl.when(self.p.c == k % 2)
        def _():
            for n in (0, 1):
                self.arrived(4 * ((self.p.z - NEAR[n]) % 4) + k, i)
                self.half_copy(k, i, n).start()
                self.beside_copy(k, i, 1 + n).start()

    def far_in(self, k, i):
        @pl.when(self.p.c == k % 2)
        def _():
            for n in (0, 1):
                self.half_copy(k, i, n).wait_recv()
            self.beside_copy(k, i, 3).start()

    def beside_in(self, k, i):
        @pl.when(self.p.c != k % 2)
        def _():
            for u in range(4):
                self.arrived(4 * u + k, i)

    def drain(self, k, i):
        @pl.when(self.p.c == k % 2)
        def _():
            @pl.when(self.p.x == k // 2)
            def _():
                self.across_copy(k, i).wait_send()

            for n in (0, 1):
                self.along_copy(k, i, n).wait_send()
                self.half_copy(k, i, n).wait_send()
            for slot in range(4):
                self.beside_copy(k, i, slot).wait_send()

    def kind_panels(self, j):
        return jnp.concatenate([self.store[4 * u + j // 3, j % 3] for u in range(GROUPS)], axis=0)

    def kind_columns(self, first, count, cols):
        parts = [
            self.store[4 * u + j // 3, j % 3, :, cols]
            for j in range(first, first + count)
            for u in range(GROUPS)
        ]
        return jnp.concatenate(parts, axis=0)


def gelu_parts(f):
    cdf = 0.5 * (1.0 + lax.erf(f * (2.0 ** -0.5)))
    pdf = jnp.exp(-0.5 * f * f) * (1.0 / math.sqrt(2.0 * math.pi))
    return f * cdf, cdf + f * pdf


def forward_kernel(
    lengths, tokens, cotangent, exits, panels, unit_bias, gains, shifts,
    low1_out, qt_out, window_out, ot_out, lse_out, hidden_out, low2_out, gt_out, dft_out, ffn_out, dn2_out, proj_out,
    dffn_out, unit_out,
    store, window, low1, qt, acc, top, mass, part, land, whole, g_rows, df_rows, dft, gt, dffn, alive_col, q_rows,
    w_recv, w_across, w_along, w_half_send, w_half_recv, w_beside, kv_send, kv_recv, kv_bsend, kv_brecv, rs_send, rs_recv, ag_send, ag_recv, out_sem,
):
    p = Place()
    w = Panels(p, store, w_recv, w_across, w_along, w_half_send, w_half_recv, w_beside)
    p.greet()

    for i in range(3):
        store[p.s, i] = panels[i].astype(BF)

    order = (1, 2, 0)

    for i in order:
        w.across(0, i)
    alive_row = alive_of(exits)
    alive_col[...] = column_of(alive_row)
    bias_t = jnp.concatenate([unit_bias[...], unit_bias[...]], axis=0).T
    for k in (2, 3):
        for i in range(3):
            w.across(k, i)

    @pl.when(p.x == 0)
    def _():
        for i in order:
            w.along(0, i)

    def norm1(r, carry):
        rows = pl.ds(pl.multiple_of(r * 32, 32), 32)
        normed, _, _ = normalize(tokens[rows, :].astype(F32), gains[0:1, :], shifts[2:3, :])
        low1[rows, :] = normed.astype(BF)
        dffn[rows, :] = (cotangent[rows, :].astype(F32) * alive_col[rows, :]).astype(BF)
        return carry

    lax.fori_loop(0, ROWS // 32, norm1, 0)

    @pl.when(p.x == 1)
    def _():
        for i in order:
            w.along(0, i)

    w.pass_on(0, 1)
    w.pass_on(0, 2)
    for i in order:
        if i == 2:
            w.pass_on(0, 0)
        w.far_in(0, i)
        w.beside_in(0, i)
        made = nt(w.kind_panels(i), low1[...])
        if i == 1:
            window[0, p.c, 0:ROWS, 0:SPAN] = made.astype(BF).T
        elif i == 2:
            bias = jnp.concatenate([bias_t[HD : 2 * HD, u : u + 1] for u in range(GROUPS)], axis=0)
            window[0, p.c, 0:ROWS, SPAN : 2 * SPAN] = (made + bias).astype(BF).T
            row = jnp.broadcast_to(alive_row, (16, ROWS)).astype(BF)
            window[0, p.c, ROWS:EXT, 0:SPAN] = row
            window[0, p.c, ROWS:EXT, SPAN : 2 * SPAN] = jnp.zeros((16, SPAN), BF)
            mine = window.at[0, p.c]
            remote(mine, mine, kv_bsend.at[0], kv_brecv.at[0], p.sibling()).start()
            for d in (2, 1, 4, 3):
                @pl.when(p.chip + d < 8)
                def _():
                    remote(mine, window.at[d, p.c], kv_send.at[d], kv_recv.at[d], p.chip_at(d)).start()
        else:
            bias = jnp.concatenate([bias_t[0:HD, u : u + 1] for u in range(GROUPS)], axis=0)
            qt[...] = (made + bias).astype(BF)

    for i in range(3):
        w.across(1, i)

    @pl.when(p.x == 0)
    def _():
        w.along(1, 0)

    for i in range(3):
        w.along(3, i, ways=(1,))
        w.along(2, i, ways=(1,))

    acc[...] = jnp.zeros_like(acc)
    top[...] = jnp.full_like(top, FLOOR)
    mass[...] = jnp.zeros_like(mass)
    code, at = query_code(p, lengths, alive_row)
    scaled = (qt[...].astype(F32) * (HD ** -0.5)).astype(BF)
    for u in range(GROUPS):
        q_rows[u] = head_rows(scaled, u)

    def attend(d, core):
        bias = block_bias(p, lengths, window, d, core, code, at)
        keys = window[d, core, 0:ROWS, 0:SPAN]
        values_t = window[d, core, 0:ROWS, SPAN : 2 * SPAN].T
        old = top[0:GROUPS, :]
        scores = [nn(keys, q_rows[u]) + bias for u in range(GROUPS)]
        new = jnp.maximum(old, jnp.concatenate([jnp.max(s, axis=0, keepdims=True) for s in scores], axis=0))
        fade = jnp.exp(old - new)
        top[0:GROUPS, :] = new
        weights = [jnp.exp(s - new[u : u + 1, :]) for u, s in enumerate(scores)]
        sums = jnp.concatenate([jnp.sum(e, axis=0, keepdims=True) for e in weights], axis=0)
        mass[0:GROUPS, :] = mass[0:GROUPS, :] * fade + sums
        for u in range(GROUPS):
            heads = slice(u * HD, (u + 1) * HD)
            mixed = nn(values_t[heads, :], weights[u].astype(BF))
            acc[heads, :] = acc[heads, :] * fade[u : u + 1, :] + mixed

    def attend_chip(d):
        def body(core, carry):
            use = (p.chip - d >= 0) & ~((d == 0) & (core > p.c)) & ~((d == 4) & (core < p.c))

            @pl.when(use)
            def _():
                attend(d, core)

            return carry

        lax.fori_loop(0, 2, body, 0)

    def kv_in(d):
        @pl.when(p.chip - d >= 0)
        def _():
            got = window.at[d, p.c]
            remote(got, got, kv_send.at[d], kv_recv.at[d], p.sibling()).wait_recv()
            remote(got, got, kv_bsend.at[d], kv_brecv.at[d], p.sibling()).start()

    def kv_beside(d):
        @pl.when(p.chip - d >= 0)
        def _():
            got = window.at[d, 1 - p.c]
            remote(got, got, kv_bsend.at[d], kv_brecv.at[d], p.sibling()).wait_recv()

    kv_beside(0)
    kv_in(1)
    attend_chip(0)

    @pl.when(p.x == 1)
    def _():
        w.along(1, 0)

    kv_beside(1)
    kv_in(2)
    attend_chip(1)
    w.pass_on(1, 0)
    kv_beside(2)
    kv_in(3)
    for i in range(3):
        w.along(3, i, ways=(0,), first=False)
        w.along(2, i, ways=(0,), first=False)
    attend_chip(2)
    kv_beside(3)
    kv_in(4)
    for i in (1, 2):
        w.along(1, i)
    attend_chip(3)
    w.far_in(1, 0)
    kv_beside(4)
    attend_chip(4)

    total = jnp.maximum(mass[...], 1e-30)
    lse_out[...] = top[...] + jnp.log(total)
    for u in range(GROUPS):
        heads = slice(u * HD, (u + 1) * HD)
        acc[heads, :] = acc[heads, :] / total[u : u + 1, :]
    ot_out[...] = acc[...]
    o_rows = acc[...].astype(BF).T

    w.beside_in(1, 0)

    def project(n, carry):
        cols = pl.ds(pl.multiple_of(n * 256, 256), 256)
        part[:, cols] = nn(o_rows, w.kind_columns(3, 1, cols)).astype(BF)
        return carry

    lax.fori_loop(0, WIDTH // 256, project, 0)
    scatter = scatter_copies(p, part, land, rs_send, rs_recv)
    for copy in scatter:
        copy.start()

    for k, i in ((3, 0), (2, 0), (3, 1), (2, 1)):
        w.pass_on(k, i)
    for copy in scatter:
        copy.wait()
    mine = pl.ds(pl.multiple_of(p.t * SHARD, SHARD), SHARD)
    summed = scatter_sum(p, part, land)
    hidden = tokens[mine, :].astype(F32) + alive_col[mine, :] * (summed + shifts[0:1, :])
    hidden_out[...] = hidden
    normed, _, _ = normalize(hidden, gains[1:2, :], shifts[3:4, :])
    whole[mine, :] = normed.astype(BF)
    gather = gather_copies(p, whole, ag_send, ag_recv)
    for copy in gather:
        copy.start()

    for k, i in ((3, 2), (2, 2), (1, 1), (1, 2)):
        w.pass_on(k, i)
    rest = ((3, 0), (2, 0), (3, 1), (2, 1), (3, 2), (2, 2), (1, 1), (1, 2))
    for k, i in rest:
        w.far_in(k, i)
    for copy in gather:
        copy.wait()
    for k, i in rest:
        w.beside_in(k, i)

    out_copies = [
        pltpu.make_async_copy(dffn, dffn_out, out_sem.at[0]),
        pltpu.make_async_copy(window, window_out, out_sem.at[1]),
        pltpu.make_async_copy(whole, low2_out, out_sem.at[2]),
        pltpu.make_async_copy(low1, low1_out, out_sem.at[3]),
        pltpu.make_async_copy(qt, qt_out, out_sem.at[4]),
    ]
    for u in range(GROUPS):
        out_copies.append(pltpu.make_async_copy(store.at[4 * u], proj_out.at[u, 0:3], out_sem.at[5 + 2 * u]))
        out_copies.append(pltpu.make_async_copy(store.at[4 * u + 1, 0], proj_out.at[u, 3], out_sem.at[6 + 2 * u]))
    for copy in out_copies:
        copy.start()

    for n in range(4):
        pre = nt(w.kind_panels(4 + n), whole[...])
        at_bias = 2 * HD + n * HD
        pre = pre + jnp.concatenate([bias_t[at_bias : at_bias + HD, u : u + 1] for u in range(GROUPS)], axis=0)
        value, slope = gelu_parts(pre)
        d_act = nt(w.kind_panels(8 + n), dffn[...])
        low_value, low_grad = value.astype(BF), (d_act * slope).astype(BF)
        units = slice(n * SPAN, (n + 1) * SPAN)
        gt[units, :] = low_value
        dft[units, :] = low_grad
        g_rows[:, units] = low_value.T
        turned = low_grad.T
        df_rows[:, units] = turned
        unit_out[2 + n : 3 + n, :] = jnp.sum(turned.astype(F32), axis=0, keepdims=True)
    unit_out[0:2, :] = jnp.zeros((2, SPAN), F32)
    unit_out[6:8, :] = jnp.zeros((2, SPAN), F32)
    gt_out[...] = gt[...]
    dft_out[...] = dft[...]

    def feed(n, carry):
        cols = pl.ds(pl.multiple_of(n * 256, 256), 256)
        dn2_out[:, cols] = nn(df_rows[...], w.kind_columns(4, 4, cols)).astype(BF)
        ffn_out[:, cols] = nn(g_rows[...], w.kind_columns(8, 4, cols)).astype(BF)
        return carry

    lax.fori_loop(0, WIDTH // 256, feed, 0)

    for k in range(4):
        for i in range(3):
            w.drain(k, i)
    mine_kv = window.at[0, p.c]
    for d in range(1, 5):
        @pl.when(p.chip + d < 8)
        def _():
            remote(mine_kv, mine_kv, kv_send.at[d], kv_recv.at[d], p.sibling()).wait_send()
    for d in range(5):
        @pl.when(p.chip - d >= 0)
        def _():
            remote(mine_kv, mine_kv, kv_bsend.at[d], kv_brecv.at[d], p.sibling()).wait_send()
    for copy in out_copies:
        copy.wait()


def forward_call(lengths, tokens, cotangent, exits, panels, unit_bias, gains, shifts):
    vmem = pl.BlockSpec(memory_space=pltpu.VMEM)
    anywhere = pl.BlockSpec(memory_space=pl.ANY)
    shape = jax.ShapeDtypeStruct
    dma = pltpu.SemaphoreType.DMA
    return pl.pallas_call(
        forward_kernel,
        in_specs=[pl.BlockSpec(memory_space=pltpu.SMEM)] + [vmem] * 7,
        out_specs=[anywhere, anywhere, anywhere, vmem, vmem, vmem, anywhere, vmem, vmem, vmem, vmem, anywhere, anywhere, vmem],
        out_shape=[
            shape((ROWS, WIDTH), BF),
            shape((SPAN, ROWS), BF),
            shape((5, 2, EXT, 2 * SPAN), BF),
            shape((SPAN, ROWS), F32),
            shape((8, ROWS), F32),
            shape((SHARD, WIDTH), F32),
            shape((ROWS, WIDTH), BF),
            shape((UNITS, ROWS), BF),
            shape((UNITS, ROWS), BF),
            shape((ROWS, WIDTH), BF),
            shape((ROWS, WIDTH), BF),
            shape((GROUPS, 4, HD, WIDTH), BF),
            shape((ROWS, WIDTH), BF),
            shape((8, SPAN), F32),
        ],
        scratch_shapes=[
            pltpu.VMEM((16, 3, HD, WIDTH), BF),
            pltpu.VMEM((5, 2, EXT, 2 * SPAN), BF),
            pltpu.VMEM((ROWS, WIDTH), BF),
            pltpu.VMEM((SPAN, ROWS), BF),
            pltpu.VMEM((SPAN, ROWS), F32),
            pltpu.VMEM((8, ROWS), F32),
            pltpu.VMEM((8, ROWS), F32),
            pltpu.VMEM((ROWS, WIDTH), BF),
            pltpu.VMEM((7, SHARD, WIDTH), BF),
            pltpu.VMEM((ROWS, WIDTH), BF),
            pltpu.VMEM((ROWS, UNITS), BF),
            pltpu.VMEM((ROWS, UNITS), BF),
            pltpu.VMEM((UNITS, ROWS), BF),
            pltpu.VMEM((UNITS, ROWS), BF),
            pltpu.VMEM((ROWS, WIDTH), BF),
            pltpu.VMEM((ROWS, 1), F32),
            pltpu.VMEM((GROUPS, SPAN, ROWS), BF),
            dma((16, 3)), dma((3,)), dma((2, 2, 3)), dma((2, 2, 3)), dma((2, 2, 3)), dma((2, 4, 3)),
            dma((5,)), dma((5,)), dma((5,)), dma((5,)),
            dma((7,)), dma((7,)), dma((7,)), dma((7,)), dma((13,)),
        ],
        compiler_params=pltpu.CompilerParams(
            collective_id=0, has_side_effects=True, vmem_limit_bytes=56 * 2**20
        ),
        name="layer_forward",
    )(lengths, tokens, cotangent, exits, panels, unit_bias, gains, shifts)


def head_columns(values, head):
    owner = lax.broadcasted_iota(jnp.int32, values.shape, 1) // HD
    return jnp.where(owner == head, values, jnp.zeros_like(values))


def norm_back(grad, unit, factor, gain):
    d_gain = jnp.sum(grad * unit, axis=0, keepdims=True)
    d_shift = jnp.sum(grad, axis=0, keepdims=True)
    d_unit = grad * gain
    d_in = factor * (
        d_unit
        - jnp.mean(d_unit, axis=-1, keepdims=True)
        - unit * jnp.mean(d_unit * unit, axis=-1, keepdims=True)
    )
    return d_in, d_gain, d_shift


class PanelSums:
    def __init__(self, place, grads, pair, half, line, last, result, sems):
        self.p, self.grads = place, grads
        self.pair, self.half, self.line, self.last, self.result = pair, half, line, last, result
        self.pair_send, self.pair_recv, self.half_send, self.half_recv = sems[:4]
        self.line_send, self.line_recv, self.last_send, self.last_recv = sems[4:]

    def pair_copy(self, u, k, i):
        return remote(
            self.grads.at[4 * u + k, i],
            self.pair.at[2 * u + k // 2, i],
            self.pair_send.at[2 * u + k // 2, i],
            self.pair_recv.at[2 * u + k // 2, i],
            self.p.sibling(),
        )

    def to_pair(self, k, i):
        @pl.when(self.p.c != k % 2)
        def _():
            for u in range(GROUPS):
                self.pair_copy(u, k, i).start()

    def half_copy(self, n, k, i):
        rows = pl.ds(n * HALF, HALF)
        return remote(
            self.grads.at[4 * ((self.p.z + 2) % 4) + k, i, rows],
            self.half.at[k // 2, n, i],
            self.half_send.at[k // 2, n, i],
            self.half_recv.at[k // 2, n, i],
            self.p.along(NEAR[n]),
        )

    def line_copy(self, n, k, i):
        return remote(
            self.grads.at[4 * ((self.p.z + NEAR[n]) % 4) + k, i],
            self.line.at[k // 2, n, i],
            self.line_send.at[k // 2, n, i],
            self.line_recv.at[k // 2, n, i],
            self.p.along(NEAR[n]),
        )

    def pair_add(self, k, i):
        @pl.when(self.p.c == k % 2)
        def _():
            def add(step, carry):
                u, rows = step // 4, pl.ds(pl.multiple_of((step % 4) * 16, 16), 16)
                self.grads[4 * u + k, i, rows, :] = (
                    self.grads[4 * u + k, i, rows, :].astype(F32)
                    + self.pair[2 * u + k // 2, i, rows, :].astype(F32)
                ).astype(BF)
                return carry

            for u in range(GROUPS):
                self.pair_copy(u, k, i).wait_recv()
            lax.fori_loop(0, 4 * GROUPS, add, 0)
            for n in (0, 1):
                self.half_copy(n, k, i).start()

    def line_mid(self, k, i):
        @pl.when(self.p.c == k % 2)
        def _():
            for n in (0, 1):
                self.half_copy(n, k, i).wait_recv()
                which = 4 * ((self.p.z + NEAR[n]) % 4) + k

                def add(step, carry):
                    here = pl.ds(pl.multiple_of(step * 16, 16), 16)
                    rows = pl.ds(pl.multiple_of(n * HALF + step * 16, 16), 16)
                    self.grads[which, i, rows, :] = (
                        self.grads[which, i, rows, :].astype(F32)
                        + self.half[k // 2, n, i, here, :].astype(F32)
                    ).astype(BF)
                    return carry

                lax.fori_loop(0, HALF // 16, add, 0)
                self.line_copy(n, k, i).start()

    def across_copy(self, k, i):
        return remote(
            self.grads.at[4 * self.p.z + k, i],
            self.last.at[i],
            self.last_send.at[i],
            self.last_recv.at[i],
            self.p.across(),
        )

    def line_add(self, k, i):
        @pl.when(self.p.c == k % 2)
        def _():
            for n in (0, 1):
                self.line_copy(n, k, i).wait_recv()

            def add(step, carry):
                rows = pl.ds(pl.multiple_of(step * 16, 16), 16)
                total = self.grads[4 * self.p.z + k, i, rows, :].astype(F32)
                for n in (0, 1):
                    total = total + self.line[k // 2, n, i, rows, :].astype(F32)
                self.grads[4 * self.p.z + k, i, rows, :] = total.astype(BF)

                @pl.when(self.p.x == k // 2)
                def _():
                    self.result[i, rows, :] = total

                return carry

            lax.fori_loop(0, HD // 16, add, 0)

            @pl.when(self.p.x != k // 2)
            def _():
                self.across_copy(k, i).start()

    def last_add(self, i):
        own = 2 * self.p.x + self.p.c
        self.across_copy(own, i).wait_recv()
        self.result[i] = self.result[i] + self.last[i].astype(F32)

    def drain(self):
        for k in range(4):
            for i in range(3):
                @pl.when(self.p.c != k % 2)
                def _():
                    for u in range(GROUPS):
                        self.pair_copy(u, k, i).wait_send()

                @pl.when(self.p.c == k % 2)
                def _():
                    for n in (0, 1):
                        self.half_copy(n, k, i).wait_send()
                        self.line_copy(n, k, i).wait_send()

                    @pl.when(self.p.x != k // 2)
                    def _():
                        self.across_copy(k, i).wait_send()


def backward_kernel(
    lengths, exits, gains, shifts, dn2_part, gt, dft, ot, lse, hidden, unit_rows, qt,
    tokens_any, cot_any, dffn_any, low2_any, low1_any, window_any, proj_any, ffn_any,
    out_any, grad_any, result, vec_out, unit_out,
    grads, pair, half, line, last, window, d_kv, kv_pair, kv_far, dffn, low2, low1, proj, ffn_part, x_rows, cot_mine,
    branch, out_whole, in_whole, dn1_part, land, q_rows, q_cols, do_rows, do_cols, delta, dqt, dkv_sum, d_hidden,
    bank, bank_land, small, small_pair, small_all, bank_back, alive_col, norm1_mean, norm1_factor, mid, y_land, h_land,
    rs_send, rs_recv, ag_send, ag_recv, ys_send, ys_recv, hs_send, hs_recv, pair_send, pair_recv, half_send, half_recv,
    line_send, line_recv, last_send, last_recv, kv_bsend, kv_brecv, kv_send, kv_recv, v1_send, v1_recv, v2_send, v2_recv, v3_send, v3_recv, v4_send, v4_recv,
    load_sem, out_sem,
):
    p = Place()
    sums = PanelSums(
        p, grads, pair, half, line, last, result,
        (pair_send, pair_recv, half_send, half_recv, line_send, line_recv, last_send, last_recv),
    )
    mine = pl.ds(pl.multiple_of(p.t * SHARD, SHARD), SHARD)
    sources = [
        (dffn_any, dffn), (low2_any, low2), (tokens_any, x_rows), (cot_any.at[mine], cot_mine),
        (proj_any, proj), (window_any, window), (low1_any, low1), (ffn_any, ffn_part),
    ]
    loads = [pltpu.make_async_copy(a, b, load_sem.at[n]) for n, (a, b) in enumerate(sources)]
    for load in loads:
        load.start()
    p.greet()
    first_scatter = scatter_copies(p, dn2_part, land.at[0], rs_send.at[0], rs_recv.at[0])
    for copy in first_scatter:
        copy.start()

    def kinds_grad(j, left, right):
        def tile(n, carry):
            cols = pl.ds(pl.multiple_of(n * 256, 256), 256)
            made = nn(left, right[:, cols]).astype(BF)
            for u in range(GROUPS):
                grads[4 * u + j // 3, j % 3, :, cols] = made[u * HD : (u + 1) * HD]
            return carry

        lax.fori_loop(0, WIDTH // 256, tile, 0)

    def four_grads(first, left, right):
        def tile(n, carry):
            cols = pl.ds(pl.multiple_of(n * 256, 256), 256)
            made = nn(left[...], right[:, cols]).astype(BF)
            for j in range(4):
                for u in range(GROUPS):
                    at_row = j * SPAN + u * HD
                    grads[4 * u + (first + j) // 3, (first + j) % 3, :, cols] = made[at_row : at_row + HD]
            return carry

        lax.fori_loop(0, WIDTH // 256, tile, 0)

    loads[0].wait()
    loads[1].wait()
    four_grads(8, gt, dffn)
    for j in (9, 10, 11, 8):
        sums.to_pair(j // 3, j % 3)
    four_grads(4, dft, low2)
    early = [(3, 0), (3, 1), (3, 2), (2, 2)]
    for j in (6, 4, 7, 5):
        sums.to_pair(j // 3, j % 3)
        early.append((j // 3, j % 3))
    for k, i in early:
        sums.pair_add(k, i)

    loads[2].wait()
    loads[3].wait()
    alive_row = alive_of(exits)
    alive_col[...] = column_of(alive_row)
    live = alive_col[mine, :]
    grad_out = cot_mine[...].astype(F32)
    _, unit2, factor2 = normalize(hidden[...], gains[1:2, :], shifts[3:4, :])
    for copy in first_scatter:
        copy.wait()
    d_norm2 = scatter_sum(p, dn2_part, land.at[0])
    d_in, d_gain2, d_shift2 = norm_back(d_norm2, unit2, factor2, gains[1:2, :])
    d_hidden[...] = grad_out + d_in
    d_branch = (live * d_hidden[...]).astype(BF)
    branch[mine, :] = d_branch
    first_gather = gather_copies(p, branch, ag_send.at[0], ag_recv.at[0])
    for copy in first_gather:
        copy.start()

    def to_bank(row, values):
        for n in range(8):
            bank[n, row : row + 1, :] = values[:, n * 256 : (n + 1) * 256]

    to_bank(1, d_gain2)
    to_bank(2, jnp.sum(d_branch.astype(F32), axis=0, keepdims=True))
    to_bank(3, jnp.sum(live * grad_out, axis=0, keepdims=True))
    to_bank(5, d_shift2)
    to_bank(6, jnp.zeros((1, WIDTH), F32))
    to_bank(7, jnp.zeros((1, WIDTH), F32))

    for k, i in early:
        sums.line_mid(k, i)

    loads[4].wait()
    loads[5].wait()
    scaled = (qt[...].astype(F32) * (HD ** -0.5)).astype(BF)
    scaled_rows = scaled.T
    for u in range(GROUPS):
        q_rows[u] = head_rows(scaled, u)
        q_cols[u] = head_columns(scaled_rows, u)
    dqt[...] = jnp.zeros_like(dqt)
    dkv_sum[...] = jnp.zeros_like(dkv_sum)
    code, at = query_code(p, lengths, alive_row)

    for copy in first_gather:
        copy.wait()
    w_out = jnp.concatenate([proj[u, 3] for u in range(GROUPS)], axis=0)
    do_t = nt(w_out, branch[...]).astype(BF)
    do_turned = do_t.T
    for u in range(GROUPS):
        heads = slice(u * HD, (u + 1) * HD)
        do_rows[u] = head_rows(do_t, u)
        do_cols[u] = head_columns(do_turned, u)
        delta[u : u + 1, :] = jnp.sum(do_t[heads, :].astype(F32) * ot[heads, :], axis=0, keepdims=True)
    loads[7].wait()
    both = pl.ds(pl.multiple_of(p.y * 2 * SHARD, 2 * SHARD), 2 * SHARD)
    out_scatter, out_spread = [], []
    for n in range(3):
        to_y = (p.y + n + 1) % 4
        to = {"tensor": to_y * 2 + p.h}
        theirs = pl.ds(pl.multiple_of(to_y * 2 * SHARD, 2 * SHARD), 2 * SHARD)
        out_scatter.append(remote(ffn_part.at[theirs], y_land.at[n], ys_send.at[0, n], ys_recv.at[0, n], to))
        out_spread.append(remote(out_whole.at[both], out_whole.at[both], ys_send.at[1, n], ys_recv.at[1, n], to))
    partner = {"tensor": p.y * 2 + 1 - p.h}
    near = pl.ds(pl.multiple_of(p.h * SHARD, SHARD), SHARD)
    away = pl.ds(pl.multiple_of((1 - p.h) * SHARD, SHARD), SHARD)
    out_swap = remote(mid.at[away], h_land, hs_send.at[0], hs_recv.at[0], partner)
    out_join = remote(out_whole.at[mine], out_whole.at[mine], hs_send.at[1], hs_recv.at[1], partner)
    for copy in out_scatter:
        copy.start()
    kinds_grad(3, ot[...].astype(BF), branch)
    sums.to_pair(1, 0)

    def kv_pair_copy(d):
        return remote(d_kv.at[d, 1 - p.c], kv_pair.at[d], kv_bsend.at[d], kv_brecv.at[d], p.sibling())

    def kv_far_copy(d):
        return remote(d_kv.at[d, p.c], kv_far.at[d], kv_send.at[d], kv_recv.at[d], p.chip_at(-d))

    def finish(d):
        @pl.when(p.chip - d >= 0)
        def _():
            @pl.when(((p.c == 0) & (d <= 3)) | ((p.c == 1) & (d >= 1)))
            def _():
                kv_pair_copy(d).wait_recv()
                d_kv[d, p.c] = (d_kv[d, p.c].astype(F32) + kv_pair[d].astype(F32)).astype(BF)

            @pl.when(d >= 1)
            def _():
                kv_far_copy(d).start()

    def block_back(step, carry):
        d = 4 - step // 2
        core = (1 - p.c + step) % 2
        use = (p.chip - d >= 0) & ~((d == 0) & (core > p.c)) & ~((d == 4) & (core < p.c))

        @pl.when(use)
        def _():
            bias = block_bias(p, lengths, window, d, core, code, at)
            keys = window[d, core, 0:ROWS, 0:SPAN]
            values = window[d, core, 0:ROWS, SPAN : 2 * SPAN]
            keys_t = keys.T
            d_key = jnp.zeros((ROWS, SPAN), F32)
            d_value = jnp.zeros((ROWS, SPAN), F32)
            for u in range(GROUPS):
                heads = slice(u * HD, (u + 1) * HD)
                prob = jnp.exp(nn(keys, q_rows[u]) + bias - lse[u : u + 1, :])
                d_prob = nn(values, do_rows[u])
                d_score = (prob * (d_prob - delta[u : u + 1, :])).astype(BF)
                d_value = d_value + nn(prob.astype(BF), do_cols[u])
                d_key = d_key + nn(d_score, q_cols[u])
                dqt[heads, :] = dqt[heads, :] + nn(keys_t[heads, :], d_score)
            d_kv[d, core, :, 0:SPAN] = d_key.astype(BF)
            d_kv[d, core, :, SPAN : 2 * SPAN] = d_value.astype(BF)

            @pl.when(core != p.c)
            def _():
                kv_pair_copy(d).start()

        @pl.when((step % 2 == 1) & (step > 1))
        def _():
            finish(d + 1)

        return carry

    lax.fori_loop(0, 10, block_back, 0)
    finish(0)
    sums.pair_add(1, 0)
    for copy in out_scatter:
        copy.wait()
    summed = ffn_part[both, :].astype(F32)
    for n in range(3):
        summed = summed + y_land[n].astype(F32)
    mid[...] = summed.astype(BF)
    out_swap.start()

    dq_t = (dqt[...] * (HD ** -0.5)).astype(BF)
    dq = dq_t.T
    small[8:16, :] = unit_rows[...]
    small[8:9, :] = jnp.sum(dq.astype(F32), axis=0, keepdims=True)
    loads[6].wait()
    kinds_grad(0, dq_t, low1)
    sums.to_pair(0, 0)

    for k, i in early:
        sums.line_add(k, i)

    out_swap.wait()
    summed = mid[near, :].astype(F32) + h_land[...].astype(F32)
    out_whole[mine, :] = (hidden[...] + live * (summed + shifts[1:2, :])).astype(BF)
    out_join.start()
    sums.pair_add(0, 0)

    def stats(r, carry):
        rows = pl.ds(pl.multiple_of(r * 32, 32), 32)
        values = x_rows[rows, :].astype(F32)
        mean = jnp.mean(values, axis=-1, keepdims=True)
        centred = values - mean
        norm1_mean[rows, :] = mean
        norm1_factor[rows, :] = lax.rsqrt(jnp.mean(centred * centred, axis=-1, keepdims=True) + EPS)
        return carry

    lax.fori_loop(0, ROWS // 32, stats, 0)

    dkv_sum[...] = d_kv[0, p.c].astype(F32)
    for d in (1, 2, 3, 4):
        @pl.when(p.chip + d < 8)
        def _():
            kv_far_copy(d).wait_recv()
            dkv_sum[...] = dkv_sum[...] + kv_far[d].astype(F32)

    dkv = dkv_sum[...].astype(BF)
    dkv_t = dkv.T
    small[9:10, :] = jnp.sum(dkv[:, SPAN:].astype(F32), axis=0, keepdims=True)

    def norm1_part(n, carry):
        cols = pl.ds(pl.multiple_of(n * 256, 256), 256)
        total = jnp.zeros((ROWS, 256), F32)
        for i, left in enumerate((dq, dkv[:, :SPAN], dkv[:, SPAN:])):
            total = total + nn(left, jnp.concatenate([proj[u, i, :, cols] for u in range(GROUPS)], axis=0))
        dn1_part[:, cols] = total.astype(BF)
        unit = (x_rows[:, cols].astype(F32) - norm1_mean[...]) * norm1_factor[...]
        bank[n, 0:1, :] = jnp.sum(total * unit, axis=0, keepdims=True)
        bank[n, 4:5, :] = jnp.sum(total, axis=0, keepdims=True)
        return carry

    lax.fori_loop(0, WIDTH // 256, norm1_part, 0)
    slices = []
    for n, (dy, dx) in enumerate(T_STEPS):
        to = p.tensor_at(dy, dx)
        slices.append(remote(bank.at[to], bank_land.at[n], v1_send.at[n], v1_recv.at[n], {"tensor": to}))
    for copy in slices:
        copy.start()
    last_scatter = scatter_copies(p, dn1_part, land.at[1], rs_send.at[1], rs_recv.at[1])
    for copy in last_scatter:
        copy.start()
    kinds_grad(1, dkv_t[:SPAN], low1)
    sums.to_pair(0, 1)
    kinds_grad(2, dkv_t[SPAN:], low1)
    sums.to_pair(0, 2)
    for copy in slices:
        copy.wait()
    total = bank[p.t]
    for n in range(len(T_STEPS)):
        total = total + bank_land[n]
    small[0:8, :] = total
    pair_small = remote(small, small_pair, v2_send, v2_recv, p.sibling())
    pair_small.start()
    pair_small.wait()
    here = p.z * 2 + p.x
    small_all[here] = small[...] + small_pair[...]
    spread = []
    for n in range(1, 8):
        to = p.seq((p.z + n // 2) % 4, (p.x + n % 2) % 2, p.c)
        spread.append(remote(small_all.at[here], small_all.at[here], v3_send.at[n - 1], v3_recv.at[n - 1], to))
    for copy in spread:
        copy.start()
    sums.line_mid(1, 0)
    sums.line_mid(0, 0)
    out_join.wait()
    for copy in out_spread:
        copy.start()
    for i in (1, 2):
        sums.pair_add(0, i)
    sums.line_add(1, 0)
    for i in (1, 2):
        sums.line_mid(0, i)

    for copy in spread:
        copy.wait()
    total = small_all[0]
    for n in range(1, 8):
        total = total + small_all[n]
    bank_back[p.t] = total[0:8, :]
    unit_out[...] = total[8:16, :]
    back = []
    for n, (dy, dx) in enumerate(T_STEPS):
        to = {"tensor": p.tensor_at(dy, dx)}
        back.append(remote(bank_back.at[p.t], bank_back.at[p.t], v4_send.at[n], v4_recv.at[n], to))
    for copy in back:
        copy.start()

    _, unit1, factor1 = normalize(x_rows[mine, :].astype(F32), gains[0:1, :], shifts[2:3, :])
    for copy in last_scatter:
        copy.wait()
    d_norm1 = scatter_sum(p, dn1_part, land.at[1])
    d_in, _, _ = norm_back(d_norm1, unit1, factor1, gains[0:1, :])
    in_whole[mine, :] = (d_hidden[...] + d_in).astype(BF)
    last_gather = gather_copies(p, in_whole, ag_send.at[1], ag_recv.at[1])
    for copy in last_gather:
        copy.start()
    for i in range(3):
        sums.line_add(0, i)
    for i in range(3):
        sums.last_add(i)
    for copy in out_spread:
        copy.wait()
    for copy in last_gather:
        copy.wait()
    stores = [
        pltpu.make_async_copy(out_whole, out_any, out_sem.at[0]),
        pltpu.make_async_copy(in_whole, grad_any, out_sem.at[1]),
    ]
    for copy in stores:
        copy.start()
    for copy in back:
        copy.wait()
    vec_out[...] = bank_back[...]
    sums.drain()
    for d in range(5):
        @pl.when((p.chip - d >= 0) & (((p.c == 1) & (d <= 3)) | ((p.c == 0) & (d >= 1))))
        def _():
            kv_pair_copy(d).wait_send()

        if d >= 1:
            @pl.when(p.chip - d >= 0)
            def _():
                kv_far_copy(d).wait_send()

    for copy in stores:
        copy.wait()


def backward_call(
    lengths, exits, gains, shifts, dn2_part, gt, dft, ot, lse, hidden, unit_rows, qt,
    tokens, cotangent, dffn, low2, low1, window, proj, ffn_part,
):
    vmem = pl.BlockSpec(memory_space=pltpu.VMEM)
    anywhere = pl.BlockSpec(memory_space=pl.ANY)
    shape = jax.ShapeDtypeStruct
    dma = pltpu.SemaphoreType.DMA
    rows_low = pltpu.VMEM((ROWS, WIDTH), BF)
    shard_low = pltpu.VMEM((SHARD, WIDTH), BF)
    masked = pltpu.VMEM((GROUPS, SPAN, ROWS), BF)
    return pl.pallas_call(
        backward_kernel,
        in_specs=[pl.BlockSpec(memory_space=pltpu.SMEM)] + [vmem] * 11 + [anywhere] * 8,
        out_specs=[anywhere, anywhere, vmem, vmem, vmem],
        out_shape=[
            shape((ROWS, WIDTH), BF),
            shape((ROWS, WIDTH), BF),
            shape((3, HD, WIDTH), F32),
            shape((8, 8, 256), F32),
            shape((8, SPAN), F32),
        ],
        scratch_shapes=[
            pltpu.VMEM((16, 3, HD, WIDTH), BF),
            pltpu.VMEM((8, 3, HD, WIDTH), BF),
            pltpu.VMEM((2, 2, 3, HALF, WIDTH), BF),
            pltpu.VMEM((2, 2, 3, HD, WIDTH), BF),
            pltpu.VMEM((3, HD, WIDTH), BF),
            pltpu.VMEM((5, 2, EXT, 2 * SPAN), BF),
            pltpu.VMEM((5, 2, ROWS, 2 * SPAN), BF),
            pltpu.VMEM((5, ROWS, 2 * SPAN), BF),
            pltpu.VMEM((5, ROWS, 2 * SPAN), BF),
            rows_low, rows_low, rows_low,
            pltpu.VMEM((GROUPS, 4, HD, WIDTH), BF),
            rows_low, rows_low, shard_low,
            rows_low, rows_low, rows_low, rows_low,
            pltpu.VMEM((2, 7, SHARD, WIDTH), BF),
            masked, masked, masked, masked,
            pltpu.VMEM((8, ROWS), F32),
            pltpu.VMEM((SPAN, ROWS), F32),
            pltpu.VMEM((ROWS, 2 * SPAN), F32),
            pltpu.VMEM((SHARD, WIDTH), F32),
            pltpu.VMEM((8, 8, 256), F32),
            pltpu.VMEM((7, 8, 256), F32),
            pltpu.VMEM((16, 256), F32),
            pltpu.VMEM((16, 256), F32),
            pltpu.VMEM((8, 16, 256), F32),
            pltpu.VMEM((8, 8, 256), F32),
            pltpu.VMEM((ROWS, 1), F32),
            pltpu.VMEM((ROWS, 1), F32),
            pltpu.VMEM((ROWS, 1), F32),
            pltpu.VMEM((2 * SHARD, WIDTH), BF),
            pltpu.VMEM((3, 2 * SHARD, WIDTH), BF),
            shard_low,
            dma((2, 7)), dma((2, 7)), dma((2, 7)), dma((2, 7)),
            dma((2, 3)), dma((2, 3)), dma((2,)), dma((2,)),
            dma((8, 3)), dma((8, 3)), dma((2, 2, 3)), dma((2, 2, 3)), dma((2, 2, 3)), dma((2, 2, 3)), dma((3,)), dma((3,)),
            dma((5,)), dma((5,)), dma((5,)), dma((5,)),
            dma((7,)), dma((7,)), dma, dma, dma((7,)), dma((7,)), dma((7,)), dma((7,)),
            dma((8,)), dma((2,)),
        ],
        compiler_params=pltpu.CompilerParams(
            collective_id=1, has_side_effects=True, vmem_limit_bytes=60 * 2**20
        ),
        name="layer_backward",
    )(
        lengths, exits, gains, shifts, dn2_part, gt, dft, ot, lse, hidden, unit_rows, qt,
        tokens, cotangent, dffn, low2, low1, window, proj, ffn_part,
    )


def high(left, right):
    return jnp.dot(left, right, precision=HIGH, preferred_element_type=F32)


def step_kernel(
    grads, panel_mom, panels, vec_sums, unit_sums, unit_bias, unit_bias_mom, gains, gains_mom, vec_bias, vec_bias_mom,
    in_low, out_low,
    out_any, in_grad, new_panels, new_mom, new_unit, new_unit_mom, new_gains, new_gains_mom, new_vec, new_vec_mom,
    sem,
):
    whole = pltpu.make_async_copy(out_low, out_any, sem)
    whole.start()
    count = panels.shape[0]
    eye = jnp.where(
        lax.broadcasted_iota(jnp.int32, (HD, HD), 0) == lax.broadcasted_iota(jnp.int32, (HD, HD), 1), 1.0, 0.0
    )
    scale, gram, chain = [], [], [None] * count
    for n in range(count):
        moment = DECAY * panel_mom[n] + grads[n]
        new_mom[n] = moment
        factor = lax.rsqrt(jnp.sum(moment * moment, axis=(0, 1), keepdims=True) + 1e-06)
        current = moment * factor
        scale.append(factor)
        gram.append(
            lax.dot_general(
                current, current, (((1,), (1,)), ((), ())), precision=HIGH, preferred_element_type=F32
            )
        )
    in_grad[...] = in_low[...].astype(F32)
    vec_rows = [jnp.concatenate([vec_sums[n, r : r + 1, :] for n in range(8)], axis=1) for r in range(6)]
    unit_rows = [
        jnp.concatenate([unit_sums[n : n + 1, u * HD : (u + 1) * HD] for n in range(6)], axis=1)
        for u in range(GROUPS)
    ]
    for rows, old, old_mom, new, mom in (
        (vec_rows[0:2], gains, gains_mom, new_gains, new_gains_mom),
        (vec_rows[2:6], vec_bias, vec_bias_mom, new_vec, new_vec_mom),
        (unit_rows, unit_bias, unit_bias_mom, new_unit, new_unit_mom),
    ):
        moment = DECAY * old_mom[...] + jnp.concatenate(rows, axis=0)
        mom[...] = moment
        new[...] = old[...] - LR_VECTOR * moment
    for sweep in range(NS_ITERS):
        squares = [high(a, a) for a in gram]
        steps = [NS_A * eye + NS_B * a + NS_C * s for a, s in zip(gram, squares)]
        chain = [m if sweep == 0 else high(m, c) for m, c in zip(steps, chain)]
        if sweep < NS_ITERS - 1:
            halves = [high(m, a) for m, a in zip(steps, gram)]
            gram = [high(h, m) for h, m in zip(halves, steps)]
    for n in range(count):
        direction = high(chain[n], new_mom[n] * scale[n])
        size_u = jnp.sum(direction * direction, axis=(0, 1), keepdims=True)
        held = panels[n]
        size_w = jnp.sum(held * held, axis=(0, 1), keepdims=True)
        new_panels[n] = held - LR_MATRIX * jnp.sqrt(size_w) * lax.rsqrt(size_u + 1e-06) * direction
    whole.wait()


def step_call(*args):
    vmem = pl.BlockSpec(memory_space=pltpu.VMEM)
    anywhere = pl.BlockSpec(memory_space=pl.ANY)
    shape = jax.ShapeDtypeStruct
    panels, unit, gain, vec = (shape(args[n].shape, F32) for n in (2, 5, 7, 9))
    return pl.pallas_call(
        step_kernel,
        in_specs=[vmem] * 12 + [anywhere],
        out_specs=[anywhere] + [vmem] * 9,
        out_shape=[
            shape((ROWS, WIDTH), BF), shape((ROWS, WIDTH), F32), panels, panels, unit, unit, gain, gain, vec, vec,
        ],
        scratch_shapes=[pltpu.SemaphoreType.DMA],
        compiler_params=pltpu.CompilerParams(vmem_limit_bytes=40 * 2**20),
        name="panel_step",
    )(*args)


def per_device(
    tokens, cotangent, exits, lengths, panels, panel_mom,
    unit_bias, unit_bias_mom, gains, gains_mom, vec_bias, vec_bias_mom,
):
    exits = exits[None, :]
    (
        low1, qt, window, ot, lse, hidden, low2, gt, dft, ffn_part, dn2_part, proj, dffn, unit_rows,
    ) = forward_call(
        lengths, tokens, cotangent, exits, panels, unit_bias, gains, vec_bias
    )
    output, input_grad, panel_grads, vec_sums, unit_sums = backward_call(
        lengths, exits, gains, vec_bias, dn2_part, gt, dft, ot, lse, hidden, unit_rows, qt,
        tokens, cotangent, dffn, low2, low1, window, proj, ffn_part,
    )
    return step_call(
        panel_grads, panel_mom, panels, vec_sums, unit_sums, unit_bias, unit_bias_mom,
        gains, gains_mom, vec_bias, vec_bias_mom, input_grad, output,
    )


def solution(mesh):
    held = P(("tensor", "seq"), None, None)
    return jax.shard_map(
        per_device,
        mesh=mesh,
        in_specs=(
            P("seq", None), P("seq", None), P("seq"), P(), held, held,
            P("tensor", None), P("tensor", None), P(), P(), P(), P(),
        ),
        out_specs=(
            P("seq", None), P("seq", None), held, held,
            P("tensor", None), P("tensor", None), P(), P(), P(), P(),
        ),
        check_vma=False,
    )
```

```python
import functools
import math

import jax
import jax.numpy as jnp
from jax import lax
from jax.experimental import pallas as pl
from jax.experimental.pallas import tpu as pltpu
from jax.sharding import PartitionSpec as P

LAYER = 12
NS_ITERS = 5
EPS = 1e-05
NS_A = 3.4445
NS_B = -4.775
NS_C = 2.0315
LR_MATRIX = 0.5
LR_VECTOR = 0.002
DECAY = 0.5
HIGH = lax.Precision.HIGHEST
MESH = pl.DeviceIdType.MESH

ROWS = 256
WIDTH = 2048
GROUPS = 4
HD = 64
SPAN = GROUPS * HD
UNITS = 4 * SPAN
SHARD = 32
EXT = ROWS + 16
MASKED = -1e30
FLOOR = -1e28
BF = jnp.bfloat16
F32 = jnp.float32

NEAR = (1, 3)
HALF = 32
T_STEPS = tuple((dy, dx) for dy in (2, 1, 3, 0) for dx in (1, 0) if (dy, dx) != (0, 0))


def nt(left, right):
    return lax.dot_general(left, right, (((1,), (1,)), ((), ())), preferred_element_type=F32)


def nn(left, right):
    return jnp.dot(left, right, preferred_element_type=F32)


def normalize(values, gain, shift):
    mean = jnp.mean(values, axis=-1, keepdims=True)
    centred = values - mean
    factor = lax.rsqrt(jnp.mean(centred * centred, axis=-1, keepdims=True) + EPS)
    return centred * factor * gain + shift, centred * factor, factor


class Place:
    def __init__(self):
        self.s = lax.axis_index("seq")
        self.t = lax.axis_index("tensor")
        self.z, self.x, self.c = self.s // 4, (self.s // 2) % 2, self.s % 2
        self.chip = self.s // 2
        self.y, self.h = self.t // 2, self.t % 2

    def seq(self, z, x, c):
        return {"seq": z * 4 + x * 2 + c}

    def sibling(self):
        return self.seq(self.z, self.x, 1 - self.c)

    def across(self):
        return self.seq(self.z, 1 - self.x, self.c)

    def along(self, step):
        return self.seq((self.z + step) % 4, self.x, self.c)

    def chip_at(self, step):
        return {"seq": (self.chip + step) * 2 + self.c}

    def tensor_at(self, dy, dx):
        return ((self.y + dy) % 4) * 2 + (self.h + dx) % 2

    def greet(self):
        barrier = pltpu.get_barrier_semaphore()
        count = 0
        for dz in range(4):
            for dx in range(2):
                if (dz, dx) != (0, 0):
                    to = self.seq((self.z + dz) % 4, (self.x + dx) % 2, self.c)
                    pl.semaphore_signal(barrier, inc=1, device_id=to, device_id_type=MESH)
                    count += 1
        pl.semaphore_signal(barrier, inc=1, device_id=self.sibling(), device_id_type=MESH)
        count += 1
        for dy, dx in T_STEPS:
            to = {"tensor": self.tensor_at(dy, dx)}
            pl.semaphore_signal(barrier, inc=1, device_id=to, device_id_type=MESH)
            count += 1
        pl.semaphore_wait(barrier, count)


def remote(src, dst, send, recv, to):
    return pltpu.make_async_remote_copy(
        src_ref=src, dst_ref=dst, send_sem=send, recv_sem=recv, device_id=to, device_id_type=MESH
    )


def scatter_copies(place, part, land, send, recv):
    out = []
    for i, (dy, dx) in enumerate(T_STEPS):
        to = place.tensor_at(dy, dx)
        rows = pl.ds(pl.multiple_of(to * SHARD, SHARD), SHARD)
        out.append(remote(part.at[rows], land.at[i], send.at[i], recv.at[i], {"tensor": to}))
    return out


def scatter_sum(place, part, land):
    mine = pl.ds(pl.multiple_of(place.t * SHARD, SHARD), SHARD)
    total = part[mine, :].astype(F32)
    for i in range(len(T_STEPS)):
        total = total + land[i].astype(F32)
    return total


def gather_copies(place, whole, send, recv):
    mine = pl.ds(pl.multiple_of(place.t * SHARD, SHARD), SHARD)
    out = []
    for i, (dy, dx) in enumerate(T_STEPS):
        to = place.tensor_at(dy, dx)
        out.append(remote(whole.at[mine], whole.at[mine], send.at[i], recv.at[i], {"tensor": to}))
    return out


def column_of(row):
    n = row.shape[1]
    down = lax.broadcasted_iota(jnp.int32, (n, n), 0)
    over = lax.broadcasted_iota(jnp.int32, (n, n), 1)
    return jnp.sum(jnp.where(down == over, row, 0.0), axis=1, keepdims=True)


def alive_of(exits):
    return jnp.where(exits[...] >= LAYER, 1.0, 0.0)


def segment_of(positions, lengths):
    end = jnp.int32(0)
    segment = jnp.zeros(positions.shape, F32)
    for i in range(4):
        end = end + lengths[i]
        segment = segment + jnp.where(positions >= end, 1.0, 0.0)
    return segment


def query_code(place, lengths, alive_row):
    at = place.s * ROWS + lax.broadcasted_iota(jnp.int32, (1, ROWS), 1)
    return jnp.where(alive_row > 0.5, segment_of(at, lengths), -2.0), at


def block_bias(place, lengths, window, dist, core, code, at):
    first = ((place.chip - dist) * 2 + core) * ROWS
    keys = first + lax.broadcasted_iota(jnp.int32, (ROWS, 1), 0)
    live = column_of(window[dist, core, ROWS:EXT, 0:ROWS].astype(F32)[0:1])
    key_code = jnp.where(live > 0.5, segment_of(keys, lengths), -1.0)
    same = jnp.where(key_code == code, 0.0, MASKED)
    return jnp.where(keys <= at, same, MASKED)


def head_rows(values, head):
    owner = lax.broadcasted_iota(jnp.int32, values.shape, 0) // HD
    return jnp.where(owner == head, values, jnp.zeros_like(values))


class Panels:
    def __init__(self, place, store, recv, across, along, half_send, half_recv, beside):
        self.p, self.store, self.recv = place, store, recv
        self.sx, self.sz, self.sh, self.rh, self.sc = across, along, half_send, half_recv, beside

    def piece(self, which, i, send, to):
        ref = self.store.at[which, i]
        return remote(ref, ref, send, self.recv.at[which, i], to)

    def across_copy(self, k, i):
        return self.piece(4 * self.p.z + k, i, self.sx.at[i], self.p.across())

    def along_copy(self, k, i, n):
        return self.piece(4 * self.p.z + k, i, self.sz.at[k // 2, n, i], self.p.along(NEAR[n]))

    def half_copy(self, k, i, n):
        which = 4 * ((self.p.z - NEAR[n]) % 4) + k
        ref = self.store.at[which, i, pl.ds(n * HALF, HALF)]
        return remote(ref, ref, self.sh.at[k // 2, n, i], self.rh.at[k // 2, n, i], self.p.along(NEAR[n]))

    def beside_copy(self, k, i, slot):
        which = 4 * ((self.p.z - (0, 1, 3, 2)[slot]) % 4) + k
        return self.piece(which, i, self.sc.at[k // 2, slot, i], self.p.sibling())

    def arrived(self, which, i):
        self.piece(which, i, self.sx.at[0], self.p.sibling()).wait_recv()

    def across(self, k, i):
        @pl.when((self.p.c == k % 2) & (self.p.x == k // 2))
        def _():
            self.across_copy(k, i).start()

    def along(self, k, i, ways=(0, 1), first=True):
        @pl.when(self.p.c == k % 2)
        def _():
            if first:
                @pl.when(self.p.x != k // 2)
                def _():
                    self.arrived(4 * self.p.z + k, i)

            for n in ways:
                self.along_copy(k, i, n).start()
            if first:
                self.beside_copy(k, i, 0).start()

    def pass_on(self, k, i):
        @pl.when(self.p.c == k % 2)
        def _():
            for n in (0, 1):
                self.arrived(4 * ((self.p.z - NEAR[n]) % 4) + k, i)
                self.half_copy(k, i, n).start()
                self.beside_copy(k, i, 1 + n).start()

    def far_in(self, k, i):
        @pl.when(self.p.c == k % 2)
        def _():
            for n in (0, 1):
                self.half_copy(k, i, n).wait_recv()
            self.beside_copy(k, i, 3).start()

    def beside_in(self, k, i):
        @pl.when(self.p.c != k % 2)
        def _():
            for u in range(4):
                self.arrived(4 * u + k, i)

    def drain(self, k, i):
        @pl.when(self.p.c == k % 2)
        def _():
            @pl.when(self.p.x == k // 2)
            def _():
                self.across_copy(k, i).wait_send()

            for n in (0, 1):
                self.along_copy(k, i, n).wait_send()
                self.half_copy(k, i, n).wait_send()
            for slot in range(4):
                self.beside_copy(k, i, slot).wait_send()

    def kind_panels(self, j):
        return jnp.concatenate([self.store[4 * u + j // 3, j % 3] for u in range(GROUPS)], axis=0)

    def kind_columns(self, first, count, cols):
        parts = [
            self.store[4 * u + j // 3, j % 3, :, cols]
            for j in range(first, first + count)
            for u in range(GROUPS)
        ]
        return jnp.concatenate(parts, axis=0)


def gelu_parts(f):
    cdf = 0.5 * (1.0 + lax.erf(f * (2.0 ** -0.5)))
    pdf = jnp.exp(-0.5 * f * f) * (1.0 / math.sqrt(2.0 * math.pi))
    return f * cdf, cdf + f * pdf


def forward_kernel(
    lengths, tokens, cotangent, exits, panels, unit_bias, gains, shifts,
    low1_out, qt_out, window_out, ot_out, lse_out, hidden_out, low2_out, gt_out, dft_out, ffn_out, dn2_out, proj_out,
    dffn_out, unit_out,
    store, window, low1, qt, acc, top, mass, part, land, whole, g_rows, df_rows, dft, gt, dffn, alive_col, q_rows,
    w_recv, w_across, w_along, w_half_send, w_half_recv, w_beside, kv_send, kv_recv, kv_bsend, kv_brecv, rs_send, rs_recv, ag_send, ag_recv, out_sem,
):
    p = Place()
    w = Panels(p, store, w_recv, w_across, w_along, w_half_send, w_half_recv, w_beside)
    p.greet()

    for i in range(3):
        store[p.s, i] = panels[i].astype(BF)

    order = (1, 2, 0)

    for i in order:
        w.across(0, i)
    alive_row = alive_of(exits)
    alive_col[...] = column_of(alive_row)
    bias_t = jnp.concatenate([unit_bias[...], unit_bias[...]], axis=0).T
    for k in (2, 3):
        for i in range(3):
            w.across(k, i)

    @pl.when(p.x == 0)
    def _():
        for i in order:
            w.along(0, i)

    def norm1(r, carry):
        rows = pl.ds(pl.multiple_of(r * 32, 32), 32)
        normed, _, _ = normalize(tokens[rows, :].astype(F32), gains[0:1, :], shifts[2:3, :])
        low1[rows, :] = normed.astype(BF)
        dffn[rows, :] = (cotangent[rows, :].astype(F32) * alive_col[rows, :]).astype(BF)
        return carry

    lax.fori_loop(0, ROWS // 32, norm1, 0)

    @pl.when(p.x == 1)
    def _():
        for i in order:
            w.along(0, i)

    w.pass_on(0, 1)
    w.pass_on(0, 2)
    for i in order:
        if i == 2:
            w.pass_on(0, 0)
        w.far_in(0, i)
        w.beside_in(0, i)
        made = nt(w.kind_panels(i), low1[...])
        if i == 1:
            window[0, p.c, 0:ROWS, 0:SPAN] = made.astype(BF).T
        elif i == 2:
            bias = jnp.concatenate([bias_t[HD : 2 * HD, u : u + 1] for u in range(GROUPS)], axis=0)
            window[0, p.c, 0:ROWS, SPAN : 2 * SPAN] = (made + bias).astype(BF).T
            row = jnp.broadcast_to(alive_row, (16, ROWS)).astype(BF)
            window[0, p.c, ROWS:EXT, 0:SPAN] = row
            window[0, p.c, ROWS:EXT, SPAN : 2 * SPAN] = jnp.zeros((16, SPAN), BF)
            mine = window.at[0, p.c]
            remote(mine, mine, kv_bsend.at[0], kv_brecv.at[0], p.sibling()).start()
            for d in (2, 1, 4, 3):
                @pl.when(p.chip + d < 8)
                def _():
                    remote(mine, window.at[d, p.c], kv_send.at[d], kv_recv.at[d], p.chip_at(d)).start()
        else:
            bias = jnp.concatenate([bias_t[0:HD, u : u + 1] for u in range(GROUPS)], axis=0)
            qt[...] = (made + bias).astype(BF)

    for i in range(3):
        w.across(1, i)

    @pl.when(p.x == 0)
    def _():
        w.along(1, 0)

    for i in range(3):
        w.along(3, i, ways=(1,))
        w.along(2, i, ways=(1,))

    acc[...] = jnp.zeros_like(acc)
    top[...] = jnp.full_like(top, FLOOR)
    mass[...] = jnp.zeros_like(mass)
    code, at = query_code(p, lengths, alive_row)
    scaled = (qt[...].astype(F32) * (HD ** -0.5)).astype(BF)
    for u in range(GROUPS):
        q_rows[u] = head_rows(scaled, u)

    def attend(d, core):
        bias = block_bias(p, lengths, window, d, core, code, at)
        keys = window[d, core, 0:ROWS, 0:SPAN]
        values_t = window[d, core, 0:ROWS, SPAN : 2 * SPAN].T
        old = top[0:GROUPS, :]
        scores = [nn(keys, q_rows[u]) + bias for u in range(GROUPS)]
        new = jnp.maximum(old, jnp.concatenate([jnp.max(s, axis=0, keepdims=True) for s in scores], axis=0))
        fade = jnp.exp(old - new)
        top[0:GROUPS, :] = new
        weights = [jnp.exp(s - new[u : u + 1, :]) for u, s in enumerate(scores)]
        sums = jnp.concatenate([jnp.sum(e, axis=0, keepdims=True) for e in weights], axis=0)
        mass[0:GROUPS, :] = mass[0:GROUPS, :] * fade + sums
        for u in range(GROUPS):
            heads = slice(u * HD, (u + 1) * HD)
            mixed = nn(values_t[heads, :], weights[u].astype(BF))
            acc[heads, :] = acc[heads, :] * fade[u : u + 1, :] + mixed

    def attend_chip(d):
        def body(core, carry):
            use = (p.chip - d >= 0) & ~((d == 0) & (core > p.c)) & ~((d == 4) & (core < p.c))

            @pl.when(use)
            def _():
                attend(d, core)

            return carry

        lax.fori_loop(0, 2, body, 0)

    def kv_in(d):
        @pl.when(p.chip - d >= 0)
        def _():
            got = window.at[d, p.c]
            remote(got, got, kv_send.at[d], kv_recv.at[d], p.sibling()).wait_recv()
            remote(got, got, kv_bsend.at[d], kv_brecv.at[d], p.sibling()).start()

    def kv_beside(d):
        @pl.when(p.chip - d >= 0)
        def _():
            got = window.at[d, 1 - p.c]
            remote(got, got, kv_bsend.at[d], kv_brecv.at[d], p.sibling()).wait_recv()

    kv_beside(0)
    kv_in(1)
    attend_chip(0)

    @pl.when(p.x == 1)
    def _():
        w.along(1, 0)

    kv_beside(1)
    kv_in(2)
    attend_chip(1)
    w.pass_on(1, 0)
    kv_beside(2)
    kv_in(3)
    for i in range(3):
        w.along(3, i, ways=(0,), first=False)
        w.along(2, i, ways=(0,), first=False)
    attend_chip(2)
    kv_beside(3)
    kv_in(4)
    for i in (1, 2):
        w.along(1, i)
    attend_chip(3)
    w.far_in(1, 0)
    kv_beside(4)
    attend_chip(4)

    total = jnp.maximum(mass[...], 1e-30)
    lse_out[...] = top[...] + jnp.log(total)
    for u in range(GROUPS):
        heads = slice(u * HD, (u + 1) * HD)
        acc[heads, :] = acc[heads, :] / total[u : u + 1, :]
    ot_out[...] = acc[...]
    o_rows = acc[...].astype(BF).T

    w.beside_in(1, 0)

    def project(n, carry):
        cols = pl.ds(pl.multiple_of(n * 256, 256), 256)
        part[:, cols] = nn(o_rows, w.kind_columns(3, 1, cols)).astype(BF)
        return carry

    lax.fori_loop(0, WIDTH // 256, project, 0)
    scatter = scatter_copies(p, part, land, rs_send, rs_recv)
    for copy in scatter:
        copy.start()

    for k, i in ((3, 0), (2, 0), (3, 1), (2, 1)):
        w.pass_on(k, i)
    for copy in scatter:
        copy.wait()
    mine = pl.ds(pl.multiple_of(p.t * SHARD, SHARD), SHARD)
    summed = scatter_sum(p, part, land)
    hidden = tokens[mine, :].astype(F32) + alive_col[mine, :] * (summed + shifts[0:1, :])
    hidden_out[...] = hidden
    normed, _, _ = normalize(hidden, gains[1:2, :], shifts[3:4, :])
    whole[mine, :] = normed.astype(BF)
    gather = gather_copies(p, whole, ag_send, ag_recv)
    for copy in gather:
        copy.start()

    for k, i in ((3, 2), (2, 2), (1, 1), (1, 2)):
        w.pass_on(k, i)
    rest = ((3, 0), (2, 0), (3, 1), (2, 1), (3, 2), (2, 2), (1, 1), (1, 2))
    for k, i in rest:
        w.far_in(k, i)
    for copy in gather:
        copy.wait()
    for k, i in rest:
        w.beside_in(k, i)

    out_copies = [
        pltpu.make_async_copy(dffn, dffn_out, out_sem.at[0]),
        pltpu.make_async_copy(window, window_out, out_sem.at[1]),
        pltpu.make_async_copy(whole, low2_out, out_sem.at[2]),
        pltpu.make_async_copy(low1, low1_out, out_sem.at[3]),
        pltpu.make_async_copy(qt, qt_out, out_sem.at[4]),
    ]
    for u in range(GROUPS):
        out_copies.append(pltpu.make_async_copy(store.at[4 * u], proj_out.at[u, 0:3], out_sem.at[5 + 2 * u]))
        out_copies.append(pltpu.make_async_copy(store.at[4 * u + 1, 0], proj_out.at[u, 3], out_sem.at[6 + 2 * u]))
    for copy in out_copies:
        copy.start()

    for n in range(4):
        pre = nt(w.kind_panels(4 + n), whole[...])
        at_bias = 2 * HD + n * HD
        pre = pre + jnp.concatenate([bias_t[at_bias : at_bias + HD, u : u + 1] for u in range(GROUPS)], axis=0)
        value, slope = gelu_parts(pre)
        d_act = nt(w.kind_panels(8 + n), dffn[...])
        low_value, low_grad = value.astype(BF), (d_act * slope).astype(BF)
        units = slice(n * SPAN, (n + 1) * SPAN)
        gt[units, :] = low_value
        dft[units, :] = low_grad
        g_rows[:, units] = low_value.T
        turned = low_grad.T
        df_rows[:, units] = turned
        unit_out[2 + n : 3 + n, :] = jnp.sum(turned.astype(F32), axis=0, keepdims=True)
    unit_out[0:2, :] = jnp.zeros((2, SPAN), F32)
    unit_out[6:8, :] = jnp.zeros((2, SPAN), F32)
    gt_out[...] = gt[...]
    dft_out[...] = dft[...]

    def feed(n, carry):
        cols = pl.ds(pl.multiple_of(n * 256, 256), 256)
        dn2_out[:, cols] = nn(df_rows[...], w.kind_columns(4, 4, cols)).astype(BF)
        ffn_out[:, cols] = nn(g_rows[...], w.kind_columns(8, 4, cols)).astype(BF)
        return carry

    lax.fori_loop(0, WIDTH // 256, feed, 0)

    for k in range(4):
        for i in range(3):
            w.drain(k, i)
    mine_kv = window.at[0, p.c]
    for d in range(1, 5):
        @pl.when(p.chip + d < 8)
        def _():
            remote(mine_kv, mine_kv, kv_send.at[d], kv_recv.at[d], p.sibling()).wait_send()
    for d in range(5):
        @pl.when(p.chip - d >= 0)
        def _():
            remote(mine_kv, mine_kv, kv_bsend.at[d], kv_brecv.at[d], p.sibling()).wait_send()
    for copy in out_copies:
        copy.wait()


def forward_call(lengths, tokens, cotangent, exits, panels, unit_bias, gains, shifts):
    vmem = pl.BlockSpec(memory_space=pltpu.VMEM)
    anywhere = pl.BlockSpec(memory_space=pl.ANY)
    shape = jax.ShapeDtypeStruct
    dma = pltpu.SemaphoreType.DMA
    return pl.pallas_call(
        forward_kernel,
        in_specs=[pl.BlockSpec(memory_space=pltpu.SMEM)] + [vmem] * 7,
        out_specs=[anywhere, anywhere, anywhere, vmem, vmem, vmem, anywhere, vmem, vmem, vmem, vmem, anywhere, anywhere, vmem],
        out_shape=[
            shape((ROWS, WIDTH), BF),
            shape((SPAN, ROWS), BF),
            shape((5, 2, EXT, 2 * SPAN), BF),
            shape((SPAN, ROWS), F32),
            shape((8, ROWS), F32),
            shape((SHARD, WIDTH), F32),
            shape((ROWS, WIDTH), BF),
            shape((UNITS, ROWS), BF),
            shape((UNITS, ROWS), BF),
            shape((ROWS, WIDTH), BF),
            shape((ROWS, WIDTH), BF),
            shape((GROUPS, 4, HD, WIDTH), BF),
            shape((ROWS, WIDTH), BF),
            shape((8, SPAN), F32),
        ],
        scratch_shapes=[
            pltpu.VMEM((16, 3, HD, WIDTH), BF),
            pltpu.VMEM((5, 2, EXT, 2 * SPAN), BF),
            pltpu.VMEM((ROWS, WIDTH), BF),
            pltpu.VMEM((SPAN, ROWS), BF),
            pltpu.VMEM((SPAN, ROWS), F32),
            pltpu.VMEM((8, ROWS), F32),
            pltpu.VMEM((8, ROWS), F32),
            pltpu.VMEM((ROWS, WIDTH), BF),
            pltpu.VMEM((7, SHARD, WIDTH), BF),
            pltpu.VMEM((ROWS, WIDTH), BF),
            pltpu.VMEM((ROWS, UNITS), BF),
            pltpu.VMEM((ROWS, UNITS), BF),
            pltpu.VMEM((UNITS, ROWS), BF),
            pltpu.VMEM((UNITS, ROWS), BF),
            pltpu.VMEM((ROWS, WIDTH), BF),
            pltpu.VMEM((ROWS, 1), F32),
            pltpu.VMEM((GROUPS, SPAN, ROWS), BF),
            dma((16, 3)), dma((3,)), dma((2, 2, 3)), dma((2, 2, 3)), dma((2, 2, 3)), dma((2, 4, 3)),
            dma((5,)), dma((5,)), dma((5,)), dma((5,)),
            dma((7,)), dma((7,)), dma((7,)), dma((7,)), dma((13,)),
        ],
        compiler_params=pltpu.CompilerParams(
            collective_id=0, has_side_effects=True, vmem_limit_bytes=56 * 2**20
        ),
        name="layer_forward",
    )(lengths, tokens, cotangent, exits, panels, unit_bias, gains, shifts)


def head_columns(values, head):
    owner = lax.broadcasted_iota(jnp.int32, values.shape, 1) // HD
    return jnp.where(owner == head, values, jnp.zeros_like(values))


def norm_back(grad, unit, factor, gain):
    d_gain = jnp.sum(grad * unit, axis=0, keepdims=True)
    d_shift = jnp.sum(grad, axis=0, keepdims=True)
    d_unit = grad * gain
    d_in = factor * (
        d_unit
        - jnp.mean(d_unit, axis=-1, keepdims=True)
        - unit * jnp.mean(d_unit * unit, axis=-1, keepdims=True)
    )
    return d_in, d_gain, d_shift


class PanelSums:
    def __init__(self, place, grads, pair, half, line, last, result, sems):
        self.p, self.grads = place, grads
        self.pair, self.half, self.line, self.last, self.result = pair, half, line, last, result
        self.pair_send, self.pair_recv, self.half_send, self.half_recv = sems[:4]
        self.line_send, self.line_recv, self.last_send, self.last_recv = sems[4:]

    def pair_copy(self, u, k, i):
        return remote(
            self.grads.at[4 * u + k, i],
            self.pair.at[2 * u + k // 2, i],
            self.pair_send.at[2 * u + k // 2, i],
            self.pair_recv.at[2 * u + k // 2, i],
            self.p.sibling(),
        )

    def to_pair(self, k, i):
        @pl.when(self.p.c != k % 2)
        def _():
            for u in range(GROUPS):
                self.pair_copy(u, k, i).start()

    def half_copy(self, n, k, i):
        rows = pl.ds(n * HALF, HALF)
        return remote(
            self.grads.at[4 * ((self.p.z + 2) % 4) + k, i, rows],
            self.half.at[k // 2, n, i],
            self.half_send.at[k // 2, n, i],
            self.half_recv.at[k // 2, n, i],
            self.p.along(NEAR[n]),
        )

    def line_copy(self, n, k, i):
        return remote(
            self.grads.at[4 * ((self.p.z + NEAR[n]) % 4) + k, i],
            self.line.at[k // 2, n, i],
            self.line_send.at[k // 2, n, i],
            self.line_recv.at[k // 2, n, i],
            self.p.along(NEAR[n]),
        )

    def pair_add(self, k, i):
        @pl.when(self.p.c == k % 2)
        def _():
            def add(step, carry):
                u, rows = step // 4, pl.ds(pl.multiple_of((step % 4) * 16, 16), 16)
                self.grads[4 * u + k, i, rows, :] = (
                    self.grads[4 * u + k, i, rows, :].astype(F32)
                    + self.pair[2 * u + k // 2, i, rows, :].astype(F32)
                ).astype(BF)
                return carry

            for u in range(GROUPS):
                self.pair_copy(u, k, i).wait_recv()
            lax.fori_loop(0, 4 * GROUPS, add, 0)
            for n in (0, 1):
                self.half_copy(n, k, i).start()

    def line_mid(self, k, i):
        @pl.when(self.p.c == k % 2)
        def _():
            for n in (0, 1):
                self.half_copy(n, k, i).wait_recv()
                which = 4 * ((self.p.z + NEAR[n]) % 4) + k

                def add(step, carry):
                    here = pl.ds(pl.multiple_of(step * 16, 16), 16)
                    rows = pl.ds(pl.multiple_of(n * HALF + step * 16, 16), 16)
                    self.grads[which, i, rows, :] = (
                        self.grads[which, i, rows, :].astype(F32)
                        + self.half[k // 2, n, i, here, :].astype(F32)
                    ).astype(BF)
                    return carry

                lax.fori_loop(0, HALF // 16, add, 0)
                self.line_copy(n, k, i).start()

    def across_copy(self, k, i):
        return remote(
            self.grads.at[4 * self.p.z + k, i],
            self.last.at[i],
            self.last_send.at[i],
            self.last_recv.at[i],
            self.p.across(),
        )

    def line_add(self, k, i):
        @pl.when(self.p.c == k % 2)
        def _():
            for n in (0, 1):
                self.line_copy(n, k, i).wait_recv()

            def add(step, carry):
                rows = pl.ds(pl.multiple_of(step * 16, 16), 16)
                total = self.grads[4 * self.p.z + k, i, rows, :].astype(F32)
                for n in (0, 1):
                    total = total + self.line[k // 2, n, i, rows, :].astype(F32)
                self.grads[4 * self.p.z + k, i, rows, :] = total.astype(BF)

                @pl.when(self.p.x == k // 2)
                def _():
                    self.result[i, rows, :] = total

                return carry

            lax.fori_loop(0, HD // 16, add, 0)

            @pl.when(self.p.x != k // 2)
            def _():
                self.across_copy(k, i).start()

    def last_add(self, i):
        own = 2 * self.p.x + self.p.c
        self.across_copy(own, i).wait_recv()
        self.result[i] = self.result[i] + self.last[i].astype(F32)

    def drain(self):
        for k in range(4):
            for i in range(3):
                @pl.when(self.p.c != k % 2)
                def _():
                    for u in range(GROUPS):
                        self.pair_copy(u, k, i).wait_send()

                @pl.when(self.p.c == k % 2)
                def _():
                    for n in (0, 1):
                        self.half_copy(n, k, i).wait_send()
                        self.line_copy(n, k, i).wait_send()

                    @pl.when(self.p.x != k // 2)
                    def _():
                        self.across_copy(k, i).wait_send()


def backward_kernel(
    lengths, exits, gains, shifts, dn2_part, gt, dft, ot, lse, hidden, unit_rows, qt,
    tokens_any, cot_any, dffn_any, low2_any, low1_any, window_any, proj_any, ffn_any,
    out_any, grad_any, result, vec_out, unit_out,
    grads, pair, half, line, last, window, d_kv, kv_pair, kv_far, dffn, low2, low1, proj, ffn_part, x_rows, cot_mine,
    branch, out_whole, in_whole, dn1_part, land, q_rows, q_cols, do_rows, do_cols, delta, dqt, dkv_sum, d_hidden,
    bank, bank_land, small, small_pair, small_all, bank_back, alive_col, norm1_mean, norm1_factor, mid, y_land, h_land,
    rs_send, rs_recv, ag_send, ag_recv, ys_send, ys_recv, hs_send, hs_recv, pair_send, pair_recv, half_send, half_recv,
    line_send, line_recv, last_send, last_recv, kv_bsend, kv_brecv, kv_send, kv_recv, v1_send, v1_recv, v2_send, v2_recv, v3_send, v3_recv, v4_send, v4_recv,
    load_sem, out_sem,
):
    p = Place()
    sums = PanelSums(
        p, grads, pair, half, line, last, result,
        (pair_send, pair_recv, half_send, half_recv, line_send, line_recv, last_send, last_recv),
    )
    mine = pl.ds(pl.multiple_of(p.t * SHARD, SHARD), SHARD)
    sources = [
        (dffn_any, dffn), (low2_any, low2), (tokens_any, x_rows), (cot_any.at[mine], cot_mine),
        (proj_any, proj), (window_any, window), (low1_any, low1), (ffn_any, ffn_part),
    ]
    loads = [pltpu.make_async_copy(a, b, load_sem.at[n]) for n, (a, b) in enumerate(sources)]
    for load in loads:
        load.start()
    p.greet()
    first_scatter = scatter_copies(p, dn2_part, land.at[0], rs_send.at[0], rs_recv.at[0])
    for copy in first_scatter:
        copy.start()

    def kinds_grad(j, left, right):
        def tile(n, carry):
            cols = pl.ds(pl.multiple_of(n * 256, 256), 256)
            made = nn(left, right[:, cols]).astype(BF)
            for u in range(GROUPS):
                grads[4 * u + j // 3, j % 3, :, cols] = made[u * HD : (u + 1) * HD]
            return carry

        lax.fori_loop(0, WIDTH // 256, tile, 0)

    def four_grads(first, left, right):
        def tile(n, carry):
            cols = pl.ds(pl.multiple_of(n * 256, 256), 256)
            made = nn(left[...], right[:, cols]).astype(BF)
            for j in range(4):
                for u in range(GROUPS):
                    at_row = j * SPAN + u * HD
                    grads[4 * u + (first + j) // 3, (first + j) % 3, :, cols] = made[at_row : at_row + HD]
            return carry

        lax.fori_loop(0, WIDTH // 256, tile, 0)

    loads[0].wait()
    loads[1].wait()
    four_grads(8, gt, dffn)
    for j in (9, 10, 11, 8):
        sums.to_pair(j // 3, j % 3)
    four_grads(4, dft, low2)
    early = [(3, 0), (3, 1), (3, 2), (2, 2)]
    for j in (6, 4, 7, 5):
        sums.to_pair(j // 3, j % 3)
        early.append((j // 3, j % 3))
    for k, i in early:
        sums.pair_add(k, i)

    loads[2].wait()
    loads[3].wait()
    alive_row = alive_of(exits)
    alive_col[...] = column_of(alive_row)
    live = alive_col[mine, :]
    grad_out = cot_mine[...].astype(F32)
    _, unit2, factor2 = normalize(hidden[...], gains[1:2, :], shifts[3:4, :])
    for copy in first_scatter:
        copy.wait()
    d_norm2 = scatter_sum(p, dn2_part, land.at[0])
    d_in, d_gain2, d_shift2 = norm_back(d_norm2, unit2, factor2, gains[1:2, :])
    d_hidden[...] = grad_out + d_in
    d_branch = (live * d_hidden[...]).astype(BF)
    branch[mine, :] = d_branch
    first_gather = gather_copies(p, branch, ag_send.at[0], ag_recv.at[0])
    for copy in first_gather:
        copy.start()

    def to_bank(row, values):
        for n in range(8):
            bank[n, row : row + 1, :] = values[:, n * 256 : (n + 1) * 256]

    to_bank(1, d_gain2)
    to_bank(2, jnp.sum(d_branch.astype(F32), axis=0, keepdims=True))
    to_bank(3, jnp.sum(live * grad_out, axis=0, keepdims=True))
    to_bank(5, d_shift2)
    to_bank(6, jnp.zeros((1, WIDTH), F32))
    to_bank(7, jnp.zeros((1, WIDTH), F32))

    for k, i in early:
        sums.line_mid(k, i)

    loads[4].wait()
    loads[5].wait()
    scaled = (qt[...].astype(F32) * (HD ** -0.5)).astype(BF)
    scaled_rows = scaled.T
    for u in range(GROUPS):
        q_rows[u] = head_rows(scaled, u)
        q_cols[u] = head_columns(scaled_rows, u)
    dqt[...] = jnp.zeros_like(dqt)
    dkv_sum[...] = jnp.zeros_like(dkv_sum)
    code, at = query_code(p, lengths, alive_row)

    for copy in first_gather:
        copy.wait()
    w_out = jnp.concatenate([proj[u, 3] for u in range(GROUPS)], axis=0)
    do_t = nt(w_out, branch[...]).astype(BF)
    do_turned = do_t.T
    for u in range(GROUPS):
        heads = slice(u * HD, (u + 1) * HD)
        do_rows[u] = head_rows(do_t, u)
        do_cols[u] = head_columns(do_turned, u)
        delta[u : u + 1, :] = jnp.sum(do_t[heads, :].astype(F32) * ot[heads, :], axis=0, keepdims=True)
    loads[7].wait()
    both = pl.ds(pl.multiple_of(p.y * 2 * SHARD, 2 * SHARD), 2 * SHARD)
    out_scatter, out_spread = [], []
    for n in range(3):
        to_y = (p.y + n + 1) % 4
        to = {"tensor": to_y * 2 + p.h}
        theirs = pl.ds(pl.multiple_of(to_y * 2 * SHARD, 2 * SHARD), 2 * SHARD)
        out_scatter.append(remote(ffn_part.at[theirs], y_land.at[n], ys_send.at[0, n], ys_recv.at[0, n], to))
        out_spread.append(remote(out_whole.at[both], out_whole.at[both], ys_send.at[1, n], ys_recv.at[1, n], to))
    partner = {"tensor": p.y * 2 + 1 - p.h}
    near = pl.ds(pl.multiple_of(p.h * SHARD, SHARD), SHARD)
    away = pl.ds(pl.multiple_of((1 - p.h) * SHARD, SHARD), SHARD)
    out_swap = remote(mid.at[away], h_land, hs_send.at[0], hs_recv.at[0], partner)
    out_join = remote(out_whole.at[mine], out_whole.at[mine], hs_send.at[1], hs_recv.at[1], partner)
    for copy in out_scatter:
        copy.start()
    kinds_grad(3, ot[...].astype(BF), branch)
    sums.to_pair(1, 0)

    def kv_pair_copy(d):
        return remote(d_kv.at[d, 1 - p.c], kv_pair.at[d], kv_bsend.at[d], kv_brecv.at[d], p.sibling())

    def kv_far_copy(d):
        return remote(d_kv.at[d, p.c], kv_far.at[d], kv_send.at[d], kv_recv.at[d], p.chip_at(-d))

    def finish(d):
        @pl.when(p.chip - d >= 0)
        def _():
            @pl.when(((p.c == 0) & (d <= 3)) | ((p.c == 1) & (d >= 1)))
            def _():
                kv_pair_copy(d).wait_recv()
                d_kv[d, p.c] = (d_kv[d, p.c].astype(F32) + kv_pair[d].astype(F32)).astype(BF)

            @pl.when(d >= 1)
            def _():
                kv_far_copy(d).start()

    def block_back(step, carry):
        d = 4 - step // 2
        core = (1 - p.c + step) % 2
        use = (p.chip - d >= 0) & ~((d == 0) & (core > p.c)) & ~((d == 4) & (core < p.c))

        @pl.when(use)
        def _():
            bias = block_bias(p, lengths, window, d, core, code, at)
            keys = window[d, core, 0:ROWS, 0:SPAN]
            values = window[d, core, 0:ROWS, SPAN : 2 * SPAN]
            keys_t = keys.T
            d_key = jnp.zeros((ROWS, SPAN), F32)
            d_value = jnp.zeros((ROWS, SPAN), F32)
            probs = [jnp.exp(nn(keys, q_rows[u]) + bias - lse[u : u + 1, :]) for u in range(GROUPS)]
            d_scores = [
                (probs[u] * (nn(values, do_rows[u]) - delta[u : u + 1, :])).astype(BF) for u in range(GROUPS)
            ]
            for u in range(GROUPS):
                d_value = d_value + nn(probs[u].astype(BF), do_cols[u])
            for u in range(GROUPS):
                d_key = d_key + nn(d_scores[u], q_cols[u])
            for u in range(GROUPS):
                heads = slice(u * HD, (u + 1) * HD)
                dqt[heads, :] = dqt[heads, :] + nn(keys_t[heads, :], d_scores[u])
            d_kv[d, core, :, 0:SPAN] = d_key.astype(BF)
            d_kv[d, core, :, SPAN : 2 * SPAN] = d_value.astype(BF)

            @pl.when(core != p.c)
            def _():
                kv_pair_copy(d).start()

        @pl.when((step % 2 == 1) & (step > 1))
        def _():
            finish(d + 1)

        return carry

    lax.fori_loop(0, 10, block_back, 0)
    finish(0)
    sums.pair_add(1, 0)
    for copy in out_scatter:
        copy.wait()
    summed = ffn_part[both, :].astype(F32)
    for n in range(3):
        summed = summed + y_land[n].astype(F32)
    mid[...] = summed.astype(BF)
    out_swap.start()

    dq_t = (dqt[...] * (HD ** -0.5)).astype(BF)
    dq = dq_t.T
    small[8:16, :] = unit_rows[...]
    small[8:9, :] = jnp.sum(dq.astype(F32), axis=0, keepdims=True)
    loads[6].wait()
    kinds_grad(0, dq_t, low1)
    sums.to_pair(0, 0)

    for k, i in early:
        sums.line_add(k, i)

    out_swap.wait()
    summed = mid[near, :].astype(F32) + h_land[...].astype(F32)
    out_whole[mine, :] = (hidden[...] + live * (summed + shifts[1:2, :])).astype(BF)
    out_join.start()
    sums.pair_add(0, 0)

    def stats(r, carry):
        rows = pl.ds(pl.multiple_of(r * 32, 32), 32)
        values = x_rows[rows, :].astype(F32)
        mean = jnp.mean(values, axis=-1, keepdims=True)
        centred = values - mean
        norm1_mean[rows, :] = mean
        norm1_factor[rows, :] = lax.rsqrt(jnp.mean(centred * centred, axis=-1, keepdims=True) + EPS)
        return carry

    lax.fori_loop(0, ROWS // 32, stats, 0)

    dkv_sum[...] = d_kv[0, p.c].astype(F32)
    for d in (1, 2, 3, 4):
        @pl.when(p.chip + d < 8)
        def _():
            kv_far_copy(d).wait_recv()
            dkv_sum[...] = dkv_sum[...] + kv_far[d].astype(F32)

    dkv = dkv_sum[...].astype(BF)
    dkv_t = dkv.T
    small[9:10, :] = jnp.sum(dkv[:, SPAN:].astype(F32), axis=0, keepdims=True)

    def norm1_part(n, carry):
        cols = pl.ds(pl.multiple_of(n * 256, 256), 256)
        total = jnp.zeros((ROWS, 256), F32)
        for i, left in enumerate((dq, dkv[:, :SPAN], dkv[:, SPAN:])):
            total = total + nn(left, jnp.concatenate([proj[u, i, :, cols] for u in range(GROUPS)], axis=0))
        dn1_part[:, cols] = total.astype(BF)
        unit = (x_rows[:, cols].astype(F32) - norm1_mean[...]) * norm1_factor[...]
        bank[n, 0:1, :] = jnp.sum(total * unit, axis=0, keepdims=True)
        bank[n, 4:5, :] = jnp.sum(total, axis=0, keepdims=True)
        return carry

    lax.fori_loop(0, WIDTH // 256, norm1_part, 0)
    slices = []
    for n, (dy, dx) in enumerate(T_STEPS):
        to = p.tensor_at(dy, dx)
        slices.append(remote(bank.at[to], bank_land.at[n], v1_send.at[n], v1_recv.at[n], {"tensor": to}))
    for copy in slices:
        copy.start()
    last_scatter = scatter_copies(p, dn1_part, land.at[1], rs_send.at[1], rs_recv.at[1])
    for copy in last_scatter:
        copy.start()
    kinds_grad(1, dkv_t[:SPAN], low1)
    sums.to_pair(0, 1)
    kinds_grad(2, dkv_t[SPAN:], low1)
    sums.to_pair(0, 2)
    for copy in slices:
        copy.wait()
    total = bank[p.t]
    for n in range(len(T_STEPS)):
        total = total + bank_land[n]
    small[0:8, :] = total
    pair_small = remote(small, small_pair, v2_send, v2_recv, p.sibling())
    pair_small.start()
    pair_small.wait()
    here = p.z * 2 + p.x
    small_all[here] = small[...] + small_pair[...]
    spread = []
    for n in range(1, 8):
        to = p.seq((p.z + n // 2) % 4, (p.x + n % 2) % 2, p.c)
        spread.append(remote(small_all.at[here], small_all.at[here], v3_send.at[n - 1], v3_recv.at[n - 1], to))
    for copy in spread:
        copy.start()
    sums.line_mid(1, 0)
    sums.line_mid(0, 0)
    out_join.wait()
    for copy in out_spread:
        copy.start()
    for i in (1, 2):
        sums.pair_add(0, i)
    sums.line_add(1, 0)
    for i in (1, 2):
        sums.line_mid(0, i)

    for copy in spread:
        copy.wait()
    total = small_all[0]
    for n in range(1, 8):
        total = total + small_all[n]
    bank_back[p.t] = total[0:8, :]
    unit_out[...] = total[8:16, :]
    back = []
    for n, (dy, dx) in enumerate(T_STEPS):
        to = {"tensor": p.tensor_at(dy, dx)}
        back.append(remote(bank_back.at[p.t], bank_back.at[p.t], v4_send.at[n], v4_recv.at[n], to))
    for copy in back:
        copy.start()

    _, unit1, factor1 = normalize(x_rows[mine, :].astype(F32), gains[0:1, :], shifts[2:3, :])
    for copy in last_scatter:
        copy.wait()
    d_norm1 = scatter_sum(p, dn1_part, land.at[1])
    d_in, _, _ = norm_back(d_norm1, unit1, factor1, gains[0:1, :])
    in_whole[mine, :] = (d_hidden[...] + d_in).astype(BF)
    last_gather = gather_copies(p, in_whole, ag_send.at[1], ag_recv.at[1])
    for copy in last_gather:
        copy.start()
    for i in range(3):
        sums.line_add(0, i)
    for i in range(3):
        sums.last_add(i)
    for copy in out_spread:
        copy.wait()
    for copy in last_gather:
        copy.wait()
    stores = [
        pltpu.make_async_copy(out_whole, out_any, out_sem.at[0]),
        pltpu.make_async_copy(in_whole, grad_any, out_sem.at[1]),
    ]
    for copy in stores:
        copy.start()
    for copy in back:
        copy.wait()
    vec_out[...] = bank_back[...]
    sums.drain()
    for d in range(5):
        @pl.when((p.chip - d >= 0) & (((p.c == 1) & (d <= 3)) | ((p.c == 0) & (d >= 1))))
        def _():
            kv_pair_copy(d).wait_send()

        if d >= 1:
            @pl.when(p.chip - d >= 0)
            def _():
                kv_far_copy(d).wait_send()

    for copy in stores:
        copy.wait()


def backward_call(
    lengths, exits, gains, shifts, dn2_part, gt, dft, ot, lse, hidden, unit_rows, qt,
    tokens, cotangent, dffn, low2, low1, window, proj, ffn_part,
):
    vmem = pl.BlockSpec(memory_space=pltpu.VMEM)
    anywhere = pl.BlockSpec(memory_space=pl.ANY)
    shape = jax.ShapeDtypeStruct
    dma = pltpu.SemaphoreType.DMA
    rows_low = pltpu.VMEM((ROWS, WIDTH), BF)
    shard_low = pltpu.VMEM((SHARD, WIDTH), BF)
    masked = pltpu.VMEM((GROUPS, SPAN, ROWS), BF)
    return pl.pallas_call(
        backward_kernel,
        in_specs=[pl.BlockSpec(memory_space=pltpu.SMEM)] + [vmem] * 11 + [anywhere] * 8,
        out_specs=[anywhere, anywhere, vmem, vmem, vmem],
        out_shape=[
            shape((ROWS, WIDTH), BF),
            shape((ROWS, WIDTH), BF),
            shape((3, HD, WIDTH), F32),
            shape((8, 8, 256), F32),
            shape((8, SPAN), F32),
        ],
        scratch_shapes=[
            pltpu.VMEM((16, 3, HD, WIDTH), BF),
            pltpu.VMEM((8, 3, HD, WIDTH), BF),
            pltpu.VMEM((2, 2, 3, HALF, WIDTH), BF),
            pltpu.VMEM((2, 2, 3, HD, WIDTH), BF),
            pltpu.VMEM((3, HD, WIDTH), BF),
            pltpu.VMEM((5, 2, EXT, 2 * SPAN), BF),
            pltpu.VMEM((5, 2, ROWS, 2 * SPAN), BF),
            pltpu.VMEM((5, ROWS, 2 * SPAN), BF),
            pltpu.VMEM((5, ROWS, 2 * SPAN), BF),
            rows_low, rows_low, rows_low,
            pltpu.VMEM((GROUPS, 4, HD, WIDTH), BF),
            rows_low, rows_low, shard_low,
            rows_low, rows_low, rows_low, rows_low,
            pltpu.VMEM((2, 7, SHARD, WIDTH), BF),
            masked, masked, masked, masked,
            pltpu.VMEM((8, ROWS), F32),
            pltpu.VMEM((SPAN, ROWS), F32),
            pltpu.VMEM((ROWS, 2 * SPAN), F32),
            pltpu.VMEM((SHARD, WIDTH), F32),
            pltpu.VMEM((8, 8, 256), F32),
            pltpu.VMEM((7, 8, 256), F32),
            pltpu.VMEM((16, 256), F32),
            pltpu.VMEM((16, 256), F32),
            pltpu.VMEM((8, 16, 256), F32),
            pltpu.VMEM((8, 8, 256), F32),
            pltpu.VMEM((ROWS, 1), F32),
            pltpu.VMEM((ROWS, 1), F32),
            pltpu.VMEM((ROWS, 1), F32),
            pltpu.VMEM((2 * SHARD, WIDTH), BF),
            pltpu.VMEM((3, 2 * SHARD, WIDTH), BF),
            shard_low,
            dma((2, 7)), dma((2, 7)), dma((2, 7)), dma((2, 7)),
            dma((2, 3)), dma((2, 3)), dma((2,)), dma((2,)),
            dma((8, 3)), dma((8, 3)), dma((2, 2, 3)), dma((2, 2, 3)), dma((2, 2, 3)), dma((2, 2, 3)), dma((3,)), dma((3,)),
            dma((5,)), dma((5,)), dma((5,)), dma((5,)),
            dma((7,)), dma((7,)), dma, dma, dma((7,)), dma((7,)), dma((7,)), dma((7,)),
            dma((8,)), dma((2,)),
        ],
        compiler_params=pltpu.CompilerParams(
            collective_id=1, has_side_effects=True, vmem_limit_bytes=60 * 2**20
        ),
        name="layer_backward",
    )(
        lengths, exits, gains, shifts, dn2_part, gt, dft, ot, lse, hidden, unit_rows, qt,
        tokens, cotangent, dffn, low2, low1, window, proj, ffn_part,
    )


def high(left, right):
    return jnp.dot(left, right, precision=HIGH, preferred_element_type=F32)


def step_kernel(
    grads, panel_mom, panels, vec_sums, unit_sums, unit_bias, unit_bias_mom, gains, gains_mom, vec_bias, vec_bias_mom,
    in_low, out_low,
    out_any, in_grad, new_panels, new_mom, new_unit, new_unit_mom, new_gains, new_gains_mom, new_vec, new_vec_mom,
    sem,
):
    whole = pltpu.make_async_copy(out_low, out_any, sem)
    whole.start()
    count = panels.shape[0]
    eye = jnp.where(
        lax.broadcasted_iota(jnp.int32, (HD, HD), 0) == lax.broadcasted_iota(jnp.int32, (HD, HD), 1), 1.0, 0.0
    )
    scale, gram, chain = [], [], [None] * count
    for n in range(count):
        moment = DECAY * panel_mom[n] + grads[n]
        new_mom[n] = moment
        factor = lax.rsqrt(jnp.sum(moment * moment, axis=(0, 1), keepdims=True) + 1e-06)
        current = moment * factor
        scale.append(factor)
        gram.append(
            lax.dot_general(
                current, current, (((1,), (1,)), ((), ())), precision=HIGH, preferred_element_type=F32
            )
        )
    in_grad[...] = in_low[...].astype(F32)
    vec_rows = [jnp.concatenate([vec_sums[n, r : r + 1, :] for n in range(8)], axis=1) for r in range(6)]
    unit_rows = [
        jnp.concatenate([unit_sums[n : n + 1, u * HD : (u + 1) * HD] for n in range(6)], axis=1)
        for u in range(GROUPS)
    ]
    for rows, old, old_mom, new, mom in (
        (vec_rows[0:2], gains, gains_mom, new_gains, new_gains_mom),
        (vec_rows[2:6], vec_bias, vec_bias_mom, new_vec, new_vec_mom),
        (unit_rows, unit_bias, unit_bias_mom, new_unit, new_unit_mom),
    ):
        moment = DECAY * old_mom[...] + jnp.concatenate(rows, axis=0)
        mom[...] = moment
        new[...] = old[...] - LR_VECTOR * moment
    for sweep in range(NS_ITERS):
        squares = [high(a, a) for a in gram]
        steps = [NS_A * eye + NS_B * a + NS_C * s for a, s in zip(gram, squares)]
        chain = [m if sweep == 0 else high(m, c) for m, c in zip(steps, chain)]
        if sweep < NS_ITERS - 1:
            halves = [high(m, a) for m, a in zip(steps, gram)]
            gram = [high(h, m) for h, m in zip(halves, steps)]
    for n in range(count):
        direction = high(chain[n], new_mom[n] * scale[n])
        size_u = jnp.sum(direction * direction, axis=(0, 1), keepdims=True)
        held = panels[n]
        size_w = jnp.sum(held * held, axis=(0, 1), keepdims=True)
        new_panels[n] = held - LR_MATRIX * jnp.sqrt(size_w) * lax.rsqrt(size_u + 1e-06) * direction
    whole.wait()


def step_call(*args):
    vmem = pl.BlockSpec(memory_space=pltpu.VMEM)
    anywhere = pl.BlockSpec(memory_space=pl.ANY)
    shape = jax.ShapeDtypeStruct
    panels, unit, gain, vec = (shape(args[n].shape, F32) for n in (2, 5, 7, 9))
    return pl.pallas_call(
        step_kernel,
        in_specs=[vmem] * 12 + [anywhere],
        out_specs=[anywhere] + [vmem] * 9,
        out_shape=[
            shape((ROWS, WIDTH), BF), shape((ROWS, WIDTH), F32), panels, panels, unit, unit, gain, gain, vec, vec,
        ],
        scratch_shapes=[pltpu.SemaphoreType.DMA],
        compiler_params=pltpu.CompilerParams(vmem_limit_bytes=60 * 2**20),
        name="panel_step",
    )(*args)


def per_device(
    tokens, cotangent, exits, lengths, panels, panel_mom,
    unit_bias, unit_bias_mom, gains, gains_mom, vec_bias, vec_bias_mom,
):
    exits = exits[None, :]
    (
        low1, qt, window, ot, lse, hidden, low2, gt, dft, ffn_part, dn2_part, proj, dffn, unit_rows,
    ) = forward_call(
        lengths, tokens, cotangent, exits, panels, unit_bias, gains, vec_bias
    )
    output, input_grad, panel_grads, vec_sums, unit_sums = backward_call(
        lengths, exits, gains, vec_bias, dn2_part, gt, dft, ot, lse, hidden, unit_rows, qt,
        tokens, cotangent, dffn, low2, low1, window, proj, ffn_part,
    )
    return step_call(
        panel_grads, panel_mom, panels, vec_sums, unit_sums, unit_bias, unit_bias_mom,
        gains, gains_mom, vec_bias, vec_bias_mom, input_grad, output,
    )


def solution(mesh):
    held = P(("tensor", "seq"), None, None)
    return jax.shard_map(
        per_device,
        mesh=mesh,
        in_specs=(
            P("seq", None), P("seq", None), P("seq"), P(), held, held,
            P("tensor", None), P("tensor", None), P(), P(), P(), P(),
        ),
        out_specs=(
            P("seq", None), P("seq", None), held, held,
            P("tensor", None), P("tensor", None), P(), P(), P(), P(),
        ),
        check_vma=False,
    )
```

```python
import functools
import math

import jax
import jax.numpy as jnp
from jax import lax
from jax.experimental import pallas as pl
from jax.experimental.pallas import tpu as pltpu
from jax.sharding import PartitionSpec as P

LAYER = 12
NS_ITERS = 5
EPS = 1e-05
NS_A = 3.4445
NS_B = -4.775
NS_C = 2.0315
LR_MATRIX = 0.5
LR_VECTOR = 0.002
DECAY = 0.5
HIGH = lax.Precision.HIGHEST
MESH = pl.DeviceIdType.MESH

ROWS = 256
WIDTH = 2048
GROUPS = 4
HD = 64
SPAN = GROUPS * HD
UNITS = 4 * SPAN
SHARD = 32
EXT = ROWS + 16
MASKED = -1e30
FLOOR = -1e28
BF = jnp.bfloat16
F32 = jnp.float32

NEAR = (1, 3)
HALF = 32
T_STEPS = tuple((dy, dx) for dy in (2, 1, 3, 0) for dx in (1, 0) if (dy, dx) != (0, 0))


def nt(left, right):
    return lax.dot_general(left, right, (((1,), (1,)), ((), ())), preferred_element_type=F32)


def nn(left, right):
    return jnp.dot(left, right, preferred_element_type=F32)


def normalize(values, gain, shift):
    mean = jnp.mean(values, axis=-1, keepdims=True)
    centred = values - mean
    factor = lax.rsqrt(jnp.mean(centred * centred, axis=-1, keepdims=True) + EPS)
    return centred * factor * gain + shift, centred * factor, factor


class Place:
    def __init__(self):
        self.s = lax.axis_index("seq")
        self.t = lax.axis_index("tensor")
        self.z, self.x, self.c = self.s // 4, (self.s // 2) % 2, self.s % 2
        self.chip = self.s // 2
        self.y, self.h = self.t // 2, self.t % 2

    def seq(self, z, x, c):
        return {"seq": z * 4 + x * 2 + c}

    def sibling(self):
        return self.seq(self.z, self.x, 1 - self.c)

    def across(self):
        return self.seq(self.z, 1 - self.x, self.c)

    def along(self, step):
        return self.seq((self.z + step) % 4, self.x, self.c)

    def chip_at(self, step):
        return {"seq": (self.chip + step) * 2 + self.c}

    def tensor_at(self, dy, dx):
        return ((self.y + dy) % 4) * 2 + (self.h + dx) % 2

    def greet(self):
        barrier = pltpu.get_barrier_semaphore()
        count = 0
        for dz in range(4):
            for dx in range(2):
                if (dz, dx) != (0, 0):
                    to = self.seq((self.z + dz) % 4, (self.x + dx) % 2, self.c)
                    pl.semaphore_signal(barrier, inc=1, device_id=to, device_id_type=MESH)
                    count += 1
        pl.semaphore_signal(barrier, inc=1, device_id=self.sibling(), device_id_type=MESH)
        count += 1
        for dy, dx in T_STEPS:
            to = {"tensor": self.tensor_at(dy, dx)}
            pl.semaphore_signal(barrier, inc=1, device_id=to, device_id_type=MESH)
            count += 1
        pl.semaphore_wait(barrier, count)


def remote(src, dst, send, recv, to):
    return pltpu.make_async_remote_copy(
        src_ref=src, dst_ref=dst, send_sem=send, recv_sem=recv, device_id=to, device_id_type=MESH
    )


def scatter_copies(place, part, land, send, recv):
    out = []
    for i, (dy, dx) in enumerate(T_STEPS):
        to = place.tensor_at(dy, dx)
        rows = pl.ds(pl.multiple_of(to * SHARD, SHARD), SHARD)
        out.append(remote(part.at[rows], land.at[i], send.at[i], recv.at[i], {"tensor": to}))
    return out


def scatter_sum(place, part, land):
    mine = pl.ds(pl.multiple_of(place.t * SHARD, SHARD), SHARD)
    total = part[mine, :].astype(F32)
    for i in range(len(T_STEPS)):
        total = total + land[i].astype(F32)
    return total


def gather_copies(place, whole, send, recv):
    mine = pl.ds(pl.multiple_of(place.t * SHARD, SHARD), SHARD)
    out = []
    for i, (dy, dx) in enumerate(T_STEPS):
        to = place.tensor_at(dy, dx)
        out.append(remote(whole.at[mine], whole.at[mine], send.at[i], recv.at[i], {"tensor": to}))
    return out


def column_of(row):
    n = row.shape[1]
    down = lax.broadcasted_iota(jnp.int32, (n, n), 0)
    over = lax.broadcasted_iota(jnp.int32, (n, n), 1)
    return jnp.sum(jnp.where(down == over, row, 0.0), axis=1, keepdims=True)


def alive_of(exits):
    return jnp.where(exits[...] >= LAYER, 1.0, 0.0)


def segment_of(positions, lengths):
    end = jnp.int32(0)
    segment = jnp.zeros(positions.shape, F32)
    for i in range(4):
        end = end + lengths[i]
        segment = segment + jnp.where(positions >= end, 1.0, 0.0)
    return segment


def query_code(place, lengths, alive_row):
    at = place.s * ROWS + lax.broadcasted_iota(jnp.int32, (1, ROWS), 1)
    return jnp.where(alive_row > 0.5, segment_of(at, lengths), -2.0), at


def block_bias(place, lengths, window, dist, core, code, at):
    first = ((place.chip - dist) * 2 + core) * ROWS
    keys = first + lax.broadcasted_iota(jnp.int32, (ROWS, 1), 0)
    live = column_of(window[dist, core, ROWS:EXT, 0:ROWS].astype(F32)[0:1])
    key_code = jnp.where(live > 0.5, segment_of(keys, lengths), -1.0)
    same = jnp.where(key_code == code, 0.0, MASKED)
    return jnp.where(keys <= at, same, MASKED)


def head_rows(values, head):
    owner = lax.broadcasted_iota(jnp.int32, values.shape, 0) // HD
    return jnp.where(owner == head, values, jnp.zeros_like(values))


class Panels:
    def __init__(self, place, store, recv, across, along, half_send, half_recv, beside):
        self.p, self.store, self.recv = place, store, recv
        self.sx, self.sz, self.sh, self.rh, self.sc = across, along, half_send, half_recv, beside

    def piece(self, which, i, send, to):
        ref = self.store.at[which, i]
        return remote(ref, ref, send, self.recv.at[which, i], to)

    def across_copy(self, k, i):
        return self.piece(4 * self.p.z + k, i, self.sx.at[i], self.p.across())

    def along_copy(self, k, i, n):
        return self.piece(4 * self.p.z + k, i, self.sz.at[k // 2, n, i], self.p.along(NEAR[n]))

    def half_copy(self, k, i, n):
        which = 4 * ((self.p.z - NEAR[n]) % 4) + k
        ref = self.store.at[which, i, pl.ds(n * HALF, HALF)]
        return remote(ref, ref, self.sh.at[k // 2, n, i], self.rh.at[k // 2, n, i], self.p.along(NEAR[n]))

    def beside_copy(self, k, i, slot):
        which = 4 * ((self.p.z - (0, 1, 3, 2)[slot]) % 4) + k
        return self.piece(which, i, self.sc.at[k // 2, slot, i], self.p.sibling())

    def arrived(self, which, i):
        self.piece(which, i, self.sx.at[0], self.p.sibling()).wait_recv()

    def across(self, k, i):
        @pl.when((self.p.c == k % 2) & (self.p.x == k // 2))
        def _():
            self.across_copy(k, i).start()

    def along(self, k, i, ways=(0, 1), first=True):
        @pl.when(self.p.c == k % 2)
        def _():
            if first:
                @pl.when(self.p.x != k // 2)
                def _():
                    self.arrived(4 * self.p.z + k, i)

            for n in ways:
                self.along_copy(k, i, n).start()
            if first:
                self.beside_copy(k, i, 0).start()

    def pass_on(self, k, i):
        @pl.when(self.p.c == k % 2)
        def _():
            for n in (0, 1):
                self.arrived(4 * ((self.p.z - NEAR[n]) % 4) + k, i)
                self.half_copy(k, i, n).start()
                self.beside_copy(k, i, 1 + n).start()

    def far_in(self, k, i):
        @pl.when(self.p.c == k % 2)
        def _():
            for n in (0, 1):
                self.half_copy(k, i, n).wait_recv()
            self.beside_copy(k, i, 3).start()

    def beside_in(self, k, i):
        @pl.when(self.p.c != k % 2)
        def _():
            for u in range(4):
                self.arrived(4 * u + k, i)

    def drain(self, k, i):
        @pl.when(self.p.c == k % 2)
        def _():
            @pl.when(self.p.x == k // 2)
            def _():
                self.across_copy(k, i).wait_send()

            for n in (0, 1):
                self.along_copy(k, i, n).wait_send()
                self.half_copy(k, i, n).wait_send()
            for slot in range(4):
                self.beside_copy(k, i, slot).wait_send()

    def kind_panels(self, j):
        return jnp.concatenate([self.store[4 * u + j // 3, j % 3] for u in range(GROUPS)], axis=0)

    def kind_columns(self, first, count, cols):
        parts = [
            self.store[4 * u + j // 3, j % 3, :, cols]
            for j in range(first, first + count)
            for u in range(GROUPS)
        ]
        return jnp.concatenate(parts, axis=0)


def gelu_parts(f):
    cdf = 0.5 * (1.0 + lax.erf(f * (2.0 ** -0.5)))
    pdf = jnp.exp(-0.5 * f * f) * (1.0 / math.sqrt(2.0 * math.pi))
    return f * cdf, cdf + f * pdf


def forward_kernel(
    lengths, tokens, cotangent, exits, panels, unit_bias, gains, shifts,
    low1_out, qt_out, window_out, ot_out, lse_out, hidden_out, low2_out, gt_out, dft_out, ffn_out, dn2_out, proj_out,
    dffn_out, unit_out,
    store, window, low1, qt, acc, top, mass, part, land, whole, g_rows, df_rows, dft, gt, dffn, alive_col, q_rows,
    w_recv, w_across, w_along, w_half_send, w_half_recv, w_beside, kv_send, kv_recv, kv_bsend, kv_brecv, rs_send, rs_recv, ag_send, ag_recv, out_sem,
):
    p = Place()
    w = Panels(p, store, w_recv, w_across, w_along, w_half_send, w_half_recv, w_beside)
    p.greet()

    for i in range(3):
        store[p.s, i] = panels[i].astype(BF)

    order = (1, 2, 0)

    for i in order:
        w.across(0, i)
    alive_row = alive_of(exits)
    alive_col[...] = column_of(alive_row)
    bias_t = jnp.concatenate([unit_bias[...], unit_bias[...]], axis=0).T
    for k in (2, 3):
        for i in range(3):
            w.across(k, i)

    @pl.when(p.x == 0)
    def _():
        for i in order:
            w.along(0, i)

    def norm1(r, carry):
        rows = pl.ds(pl.multiple_of(r * 32, 32), 32)
        normed, _, _ = normalize(tokens[rows, :].astype(F32), gains[0:1, :], shifts[2:3, :])
        low1[rows, :] = normed.astype(BF)
        dffn[rows, :] = (cotangent[rows, :].astype(F32) * alive_col[rows, :]).astype(BF)
        return carry

    lax.fori_loop(0, ROWS // 32, norm1, 0)

    @pl.when(p.x == 1)
    def _():
        for i in order:
            w.along(0, i)

    w.pass_on(0, 1)
    w.pass_on(0, 2)
    for i in order:
        if i == 2:
            w.pass_on(0, 0)
        w.far_in(0, i)
        w.beside_in(0, i)
        made = nt(w.kind_panels(i), low1[...])
        if i == 1:
            window[0, p.c, 0:ROWS, 0:SPAN] = made.astype(BF).T
        elif i == 2:
            bias = jnp.concatenate([bias_t[HD : 2 * HD, u : u + 1] for u in range(GROUPS)], axis=0)
            window[0, p.c, 0:ROWS, SPAN : 2 * SPAN] = (made + bias).astype(BF).T
            row = jnp.broadcast_to(alive_row, (16, ROWS)).astype(BF)
            window[0, p.c, ROWS:EXT, 0:SPAN] = row
            window[0, p.c, ROWS:EXT, SPAN : 2 * SPAN] = jnp.zeros((16, SPAN), BF)
            mine = window.at[0, p.c]
            remote(mine, mine, kv_bsend.at[0], kv_brecv.at[0], p.sibling()).start()
            for d in (2, 1, 4, 3):
                @pl.when(p.chip + d < 8)
                def _():
                    remote(mine, window.at[d, p.c], kv_send.at[d], kv_recv.at[d], p.chip_at(d)).start()
        else:
            bias = jnp.concatenate([bias_t[0:HD, u : u + 1] for u in range(GROUPS)], axis=0)
            qt[...] = (made + bias).astype(BF)

    for i in range(3):
        w.across(1, i)

    @pl.when(p.x == 0)
    def _():
        w.along(1, 0)

    for i in range(3):
        w.along(3, i, ways=(1,))
        w.along(2, i, ways=(1,))

    acc[...] = jnp.zeros_like(acc)
    top[...] = jnp.full_like(top, FLOOR)
    mass[...] = jnp.zeros_like(mass)
    code, at = query_code(p, lengths, alive_row)
    scaled = (qt[...].astype(F32) * (HD ** -0.5)).astype(BF)
    for u in range(GROUPS):
        q_rows[u] = head_rows(scaled, u)

    def attend(d, core):
        bias = block_bias(p, lengths, window, d, core, code, at)
        keys = window[d, core, 0:ROWS, 0:SPAN]
        values_t = window[d, core, 0:ROWS, SPAN : 2 * SPAN].T
        old = top[0:GROUPS, :]
        scores = [nn(keys, q_rows[u]) + bias for u in range(GROUPS)]
        new = jnp.maximum(old, jnp.concatenate([jnp.max(s, axis=0, keepdims=True) for s in scores], axis=0))
        fade = jnp.exp(old - new)
        top[0:GROUPS, :] = new
        weights = [jnp.exp(s - new[u : u + 1, :]) for u, s in enumerate(scores)]
        sums = jnp.concatenate([jnp.sum(e, axis=0, keepdims=True) for e in weights], axis=0)
        mass[0:GROUPS, :] = mass[0:GROUPS, :] * fade + sums
        for u in range(GROUPS):
            heads = slice(u * HD, (u + 1) * HD)
            mixed = nn(values_t[heads, :], weights[u].astype(BF))
            acc[heads, :] = acc[heads, :] * fade[u : u + 1, :] + mixed

    def attend_chip(d):
        def body(core, carry):
            use = (p.chip - d >= 0) & ~((d == 0) & (core > p.c)) & ~((d == 4) & (core < p.c))

            @pl.when(use)
            def _():
                attend(d, core)

            return carry

        lax.fori_loop(0, 2, body, 0)

    def kv_in(d):
        @pl.when(p.chip - d >= 0)
        def _():
            got = window.at[d, p.c]
            remote(got, got, kv_send.at[d], kv_recv.at[d], p.sibling()).wait_recv()
            remote(got, got, kv_bsend.at[d], kv_brecv.at[d], p.sibling()).start()

    def kv_beside(d):
        @pl.when(p.chip - d >= 0)
        def _():
            got = window.at[d, 1 - p.c]
            remote(got, got, kv_bsend.at[d], kv_brecv.at[d], p.sibling()).wait_recv()

    kv_beside(0)
    kv_in(1)
    attend_chip(0)

    @pl.when(p.x == 1)
    def _():
        w.along(1, 0)

    kv_beside(1)
    kv_in(2)
    attend_chip(1)
    w.pass_on(1, 0)
    kv_beside(2)
    kv_in(3)
    for i in range(3):
        w.along(3, i, ways=(0,), first=False)
        w.along(2, i, ways=(0,), first=False)
    attend_chip(2)
    kv_beside(3)
    kv_in(4)
    for i in (1, 2):
        w.along(1, i)
    attend_chip(3)
    w.far_in(1, 0)
    kv_beside(4)
    attend_chip(4)

    total = jnp.maximum(mass[...], 1e-30)
    lse_out[...] = top[...] + jnp.log(total)
    for u in range(GROUPS):
        heads = slice(u * HD, (u + 1) * HD)
        acc[heads, :] = acc[heads, :] / total[u : u + 1, :]
    ot_out[...] = acc[...]
    o_rows = acc[...].astype(BF).T

    w.beside_in(1, 0)

    def project(n, carry):
        cols = pl.ds(pl.multiple_of(n * 256, 256), 256)
        part[:, cols] = nn(o_rows, w.kind_columns(3, 1, cols)).astype(BF)
        return carry

    lax.fori_loop(0, WIDTH // 256, project, 0)
    scatter = scatter_copies(p, part, land, rs_send, rs_recv)
    for copy in scatter:
        copy.start()

    for k, i in ((3, 0), (2, 0), (3, 1), (2, 1)):
        w.pass_on(k, i)
    for copy in scatter:
        copy.wait()
    mine = pl.ds(pl.multiple_of(p.t * SHARD, SHARD), SHARD)
    summed = scatter_sum(p, part, land)
    hidden = tokens[mine, :].astype(F32) + alive_col[mine, :] * (summed + shifts[0:1, :])
    hidden_out[...] = hidden
    normed, _, _ = normalize(hidden, gains[1:2, :], shifts[3:4, :])
    whole[mine, :] = normed.astype(BF)
    gather = gather_copies(p, whole, ag_send, ag_recv)
    for copy in gather:
        copy.start()

    for k, i in ((3, 2), (2, 2), (1, 1), (1, 2)):
        w.pass_on(k, i)
    rest = ((3, 0), (2, 0), (3, 1), (2, 1), (3, 2), (2, 2), (1, 1), (1, 2))
    for k, i in rest:
        w.far_in(k, i)
    for copy in gather:
        copy.wait()
    for k, i in rest:
        w.beside_in(k, i)

    out_copies = [
        pltpu.make_async_copy(dffn, dffn_out, out_sem.at[0]),
        pltpu.make_async_copy(window, window_out, out_sem.at[1]),
        pltpu.make_async_copy(whole, low2_out, out_sem.at[2]),
        pltpu.make_async_copy(low1, low1_out, out_sem.at[3]),
        pltpu.make_async_copy(qt, qt_out, out_sem.at[4]),
    ]
    for u in range(GROUPS):
        out_copies.append(pltpu.make_async_copy(store.at[4 * u], proj_out.at[u, 0:3], out_sem.at[5 + 2 * u]))
        out_copies.append(pltpu.make_async_copy(store.at[4 * u + 1, 0], proj_out.at[u, 3], out_sem.at[6 + 2 * u]))
    for copy in out_copies:
        copy.start()

    for n in range(4):
        pre = nt(w.kind_panels(4 + n), whole[...])
        at_bias = 2 * HD + n * HD
        pre = pre + jnp.concatenate([bias_t[at_bias : at_bias + HD, u : u + 1] for u in range(GROUPS)], axis=0)
        value, slope = gelu_parts(pre)
        d_act = nt(w.kind_panels(8 + n), dffn[...])
        low_value, low_grad = value.astype(BF), (d_act * slope).astype(BF)
        units = slice(n * SPAN, (n + 1) * SPAN)
        gt[units, :] = low_value
        dft[units, :] = low_grad
        g_rows[:, units] = low_value.T
        turned = low_grad.T
        df_rows[:, units] = turned
        unit_out[2 + n : 3 + n, :] = jnp.sum(turned.astype(F32), axis=0, keepdims=True)
    unit_out[0:2, :] = jnp.zeros((2, SPAN), F32)
    unit_out[6:8, :] = jnp.zeros((2, SPAN), F32)
    gt_out[...] = gt[...]
    dft_out[...] = dft[...]

    def feed(n, carry):
        cols = pl.ds(pl.multiple_of(n * 256, 256), 256)
        dn2_out[:, cols] = nn(df_rows[...], w.kind_columns(4, 4, cols)).astype(BF)
        ffn_out[:, cols] = nn(g_rows[...], w.kind_columns(8, 4, cols)).astype(BF)
        return carry

    lax.fori_loop(0, WIDTH // 256, feed, 0)

    for k in range(4):
        for i in range(3):
            w.drain(k, i)
    mine_kv = window.at[0, p.c]
    for d in range(1, 5):
        @pl.when(p.chip + d < 8)
        def _():
            remote(mine_kv, mine_kv, kv_send.at[d], kv_recv.at[d], p.sibling()).wait_send()
    for d in range(5):
        @pl.when(p.chip - d >= 0)
        def _():
            remote(mine_kv, mine_kv, kv_bsend.at[d], kv_brecv.at[d], p.sibling()).wait_send()
    for copy in out_copies:
        copy.wait()


def forward_call(lengths, tokens, cotangent, exits, panels, unit_bias, gains, shifts):
    vmem = pl.BlockSpec(memory_space=pltpu.VMEM)
    anywhere = pl.BlockSpec(memory_space=pl.ANY)
    shape = jax.ShapeDtypeStruct
    dma = pltpu.SemaphoreType.DMA
    return pl.pallas_call(
        forward_kernel,
        in_specs=[pl.BlockSpec(memory_space=pltpu.SMEM)] + [vmem] * 7,
        out_specs=[anywhere, anywhere, anywhere, vmem, vmem, vmem, anywhere, vmem, vmem, vmem, vmem, anywhere, anywhere, vmem],
        out_shape=[
            shape((ROWS, WIDTH), BF),
            shape((SPAN, ROWS), BF),
            shape((5, 2, EXT, 2 * SPAN), BF),
            shape((SPAN, ROWS), F32),
            shape((8, ROWS), F32),
            shape((SHARD, WIDTH), F32),
            shape((ROWS, WIDTH), BF),
            shape((UNITS, ROWS), BF),
            shape((UNITS, ROWS), BF),
            shape((ROWS, WIDTH), BF),
            shape((ROWS, WIDTH), BF),
            shape((GROUPS, 4, HD, WIDTH), BF),
            shape((ROWS, WIDTH), BF),
            shape((8, SPAN), F32),
        ],
        scratch_shapes=[
            pltpu.VMEM((16, 3, HD, WIDTH), BF),
            pltpu.VMEM((5, 2, EXT, 2 * SPAN), BF),
            pltpu.VMEM((ROWS, WIDTH), BF),
            pltpu.VMEM((SPAN, ROWS), BF),
            pltpu.VMEM((SPAN, ROWS), F32),
            pltpu.VMEM((8, ROWS), F32),
            pltpu.VMEM((8, ROWS), F32),
            pltpu.VMEM((ROWS, WIDTH), BF),
            pltpu.VMEM((7, SHARD, WIDTH), BF),
            pltpu.VMEM((ROWS, WIDTH), BF),
            pltpu.VMEM((ROWS, UNITS), BF),
            pltpu.VMEM((ROWS, UNITS), BF),
            pltpu.VMEM((UNITS, ROWS), BF),
            pltpu.VMEM((UNITS, ROWS), BF),
            pltpu.VMEM((ROWS, WIDTH), BF),
            pltpu.VMEM((ROWS, 1), F32),
            pltpu.VMEM((GROUPS, SPAN, ROWS), BF),
            dma((16, 3)), dma((3,)), dma((2, 2, 3)), dma((2, 2, 3)), dma((2, 2, 3)), dma((2, 4, 3)),
            dma((5,)), dma((5,)), dma((5,)), dma((5,)),
            dma((7,)), dma((7,)), dma((7,)), dma((7,)), dma((13,)),
        ],
        compiler_params=pltpu.CompilerParams(
            collective_id=0, has_side_effects=True, vmem_limit_bytes=56 * 2**20
        ),
        name="layer_forward",
    )(lengths, tokens, cotangent, exits, panels, unit_bias, gains, shifts)


def head_columns(values, head):
    owner = lax.broadcasted_iota(jnp.int32, values.shape, 1) // HD
    return jnp.where(owner == head, values, jnp.zeros_like(values))


def norm_back(grad, unit, factor, gain):
    d_gain = jnp.sum(grad * unit, axis=0, keepdims=True)
    d_shift = jnp.sum(grad, axis=0, keepdims=True)
    d_unit = grad * gain
    d_in = factor * (
        d_unit
        - jnp.mean(d_unit, axis=-1, keepdims=True)
        - unit * jnp.mean(d_unit * unit, axis=-1, keepdims=True)
    )
    return d_in, d_gain, d_shift


class PanelSums:
    def __init__(self, place, grads, pair, half, line, last, result, sems):
        self.p, self.grads = place, grads
        self.pair, self.half, self.line, self.last, self.result = pair, half, line, last, result
        self.pair_send, self.pair_recv, self.half_send, self.half_recv = sems[:4]
        self.line_send, self.line_recv, self.last_send, self.last_recv = sems[4:]

    def pair_copy(self, u, k, i):
        return remote(
            self.grads.at[4 * u + k, i],
            self.pair.at[2 * u + k // 2, i],
            self.pair_send.at[2 * u + k // 2, i],
            self.pair_recv.at[2 * u + k // 2, i],
            self.p.sibling(),
        )

    def to_pair(self, k, i):
        @pl.when(self.p.c != k % 2)
        def _():
            for u in range(GROUPS):
                self.pair_copy(u, k, i).start()

    def half_copy(self, n, k, i):
        rows = pl.ds(n * HALF, HALF)
        return remote(
            self.grads.at[4 * ((self.p.z + 2) % 4) + k, i, rows],
            self.half.at[k // 2, n, i],
            self.half_send.at[k // 2, n, i],
            self.half_recv.at[k // 2, n, i],
            self.p.along(NEAR[n]),
        )

    def line_copy(self, n, k, i):
        return remote(
            self.grads.at[4 * ((self.p.z + NEAR[n]) % 4) + k, i],
            self.line.at[k // 2, n, i],
            self.line_send.at[k // 2, n, i],
            self.line_recv.at[k // 2, n, i],
            self.p.along(NEAR[n]),
        )

    def pair_add(self, k, i):
        @pl.when(self.p.c == k % 2)
        def _():
            def add(step, carry):
                u, rows = step // 4, pl.ds(pl.multiple_of((step % 4) * 16, 16), 16)
                self.grads[4 * u + k, i, rows, :] = (
                    self.grads[4 * u + k, i, rows, :].astype(F32)
                    + self.pair[2 * u + k // 2, i, rows, :].astype(F32)
                ).astype(BF)
                return carry

            for u in range(GROUPS):
                self.pair_copy(u, k, i).wait_recv()
            lax.fori_loop(0, 4 * GROUPS, add, 0)
            for n in (0, 1):
                self.half_copy(n, k, i).start()

    def line_mid(self, k, i):
        @pl.when(self.p.c == k % 2)
        def _():
            for n in (0, 1):
                self.half_copy(n, k, i).wait_recv()
                which = 4 * ((self.p.z + NEAR[n]) % 4) + k

                def add(step, carry):
                    here = pl.ds(pl.multiple_of(step * 16, 16), 16)
                    rows = pl.ds(pl.multiple_of(n * HALF + step * 16, 16), 16)
                    self.grads[which, i, rows, :] = (
                        self.grads[which, i, rows, :].astype(F32)
                        + self.half[k // 2, n, i, here, :].astype(F32)
                    ).astype(BF)
                    return carry

                lax.fori_loop(0, HALF // 16, add, 0)
                self.line_copy(n, k, i).start()

    def across_copy(self, k, i):
        return remote(
            self.grads.at[4 * self.p.z + k, i],
            self.last.at[i],
            self.last_send.at[i],
            self.last_recv.at[i],
            self.p.across(),
        )

    def line_add(self, k, i):
        @pl.when(self.p.c == k % 2)
        def _():
            for n in (0, 1):
                self.line_copy(n, k, i).wait_recv()

            def add(step, carry):
                rows = pl.ds(pl.multiple_of(step * 16, 16), 16)
                total = self.grads[4 * self.p.z + k, i, rows, :].astype(F32)
                for n in (0, 1):
                    total = total + self.line[k // 2, n, i, rows, :].astype(F32)
                self.grads[4 * self.p.z + k, i, rows, :] = total.astype(BF)

                @pl.when(self.p.x == k // 2)
                def _():
                    self.result[i, rows, :] = total

                return carry

            lax.fori_loop(0, HD // 16, add, 0)

            @pl.when(self.p.x != k // 2)
            def _():
                self.across_copy(k, i).start()

    def last_add(self, i):
        own = 2 * self.p.x + self.p.c
        self.across_copy(own, i).wait_recv()
        self.result[i] = self.result[i] + self.last[i].astype(F32)

    def drain(self):
        for k in range(4):
            for i in range(3):
                @pl.when(self.p.c != k % 2)
                def _():
                    for u in range(GROUPS):
                        self.pair_copy(u, k, i).wait_send()

                @pl.when(self.p.c == k % 2)
                def _():
                    for n in (0, 1):
                        self.half_copy(n, k, i).wait_send()
                        self.line_copy(n, k, i).wait_send()

                    @pl.when(self.p.x != k // 2)
                    def _():
                        self.across_copy(k, i).wait_send()


def backward_kernel(
    lengths, exits, gains, shifts, dn2_part, gt, dft, ot, lse, hidden, unit_rows, qt,
    tokens_any, cot_any, dffn_any, low2_any, low1_any, window_any, proj_any, ffn_any,
    out_any, grad_any, result, vec_out, unit_out,
    grads, pair, half, line, last, window, d_kv, kv_pair, kv_far, dffn, low2, low1, proj, ffn_part, x_rows, cot_mine,
    branch, out_whole, in_whole, dn1_part, land, q_rows, q_cols, do_rows, do_cols, delta, dqt, dkv_sum, d_hidden,
    bank, bank_land, small, small_pair, small_all, bank_back, alive_col, norm1_mean, norm1_factor, mid, y_land, h_land,
    rs_send, rs_recv, ag_send, ag_recv, ys_send, ys_recv, hs_send, hs_recv, pair_send, pair_recv, half_send, half_recv,
    line_send, line_recv, last_send, last_recv, kv_bsend, kv_brecv, kv_send, kv_recv, v1_send, v1_recv, v2_send, v2_recv, v3_send, v3_recv, v4_send, v4_recv,
    load_sem, out_sem,
):
    p = Place()
    sums = PanelSums(
        p, grads, pair, half, line, last, result,
        (pair_send, pair_recv, half_send, half_recv, line_send, line_recv, last_send, last_recv),
    )
    mine = pl.ds(pl.multiple_of(p.t * SHARD, SHARD), SHARD)
    sources = [
        (dffn_any, dffn), (low2_any, low2), (tokens_any, x_rows), (cot_any.at[mine], cot_mine),
        (proj_any, proj), (window_any, window), (low1_any, low1), (ffn_any, ffn_part),
    ]
    loads = [pltpu.make_async_copy(a, b, load_sem.at[n]) for n, (a, b) in enumerate(sources)]
    for load in loads:
        load.start()
    p.greet()
    first_scatter = scatter_copies(p, dn2_part, land.at[0], rs_send.at[0], rs_recv.at[0])
    for copy in first_scatter:
        copy.start()

    def kinds_grad(j, left, right):
        def tile(n, carry):
            cols = pl.ds(pl.multiple_of(n * 256, 256), 256)
            made = nn(left, right[:, cols]).astype(BF)
            for u in range(GROUPS):
                grads[4 * u + j // 3, j % 3, :, cols] = made[u * HD : (u + 1) * HD]
            return carry

        lax.fori_loop(0, WIDTH // 256, tile, 0)

    def four_grads(first, left, right):
        def tile(n, carry):
            cols = pl.ds(pl.multiple_of(n * 256, 256), 256)
            made = nn(left[...], right[:, cols]).astype(BF)
            for j in range(4):
                for u in range(GROUPS):
                    at_row = j * SPAN + u * HD
                    grads[4 * u + (first + j) // 3, (first + j) % 3, :, cols] = made[at_row : at_row + HD]
            return carry

        lax.fori_loop(0, WIDTH // 256, tile, 0)

    loads[0].wait()
    loads[1].wait()
    four_grads(8, gt, dffn)
    for j in (9, 10, 11, 8):
        sums.to_pair(j // 3, j % 3)
    four_grads(4, dft, low2)
    early = [(3, 0), (3, 1), (3, 2), (2, 2)]
    for j in (6, 4, 7, 5):
        sums.to_pair(j // 3, j % 3)
        early.append((j // 3, j % 3))
    for k, i in early:
        sums.pair_add(k, i)

    loads[2].wait()
    loads[3].wait()
    alive_row = alive_of(exits)
    alive_col[...] = column_of(alive_row)
    live = alive_col[mine, :]
    grad_out = cot_mine[...].astype(F32)
    _, unit2, factor2 = normalize(hidden[...], gains[1:2, :], shifts[3:4, :])
    for copy in first_scatter:
        copy.wait()
    d_norm2 = scatter_sum(p, dn2_part, land.at[0])
    d_in, d_gain2, d_shift2 = norm_back(d_norm2, unit2, factor2, gains[1:2, :])
    d_hidden[...] = grad_out + d_in
    d_branch = (live * d_hidden[...]).astype(BF)
    branch[mine, :] = d_branch
    first_gather = gather_copies(p, branch, ag_send.at[0], ag_recv.at[0])
    for copy in first_gather:
        copy.start()

    def to_bank(row, values):
        for n in range(8):
            bank[n, row : row + 1, :] = values[:, n * 256 : (n + 1) * 256]

    to_bank(1, d_gain2)
    to_bank(2, jnp.sum(d_branch.astype(F32), axis=0, keepdims=True))
    to_bank(3, jnp.sum(live * grad_out, axis=0, keepdims=True))
    to_bank(5, d_shift2)
    to_bank(6, jnp.zeros((1, WIDTH), F32))
    to_bank(7, jnp.zeros((1, WIDTH), F32))

    for k, i in early:
        sums.line_mid(k, i)

    loads[4].wait()
    loads[5].wait()
    scaled = (qt[...].astype(F32) * (HD ** -0.5)).astype(BF)
    scaled_rows = scaled.T
    for u in range(GROUPS):
        q_rows[u] = head_rows(scaled, u)
        q_cols[u] = head_columns(scaled_rows, u)
    dqt[...] = jnp.zeros_like(dqt)
    dkv_sum[...] = jnp.zeros_like(dkv_sum)
    code, at = query_code(p, lengths, alive_row)

    for copy in first_gather:
        copy.wait()
    w_out = jnp.concatenate([proj[u, 3] for u in range(GROUPS)], axis=0)
    do_t = nt(w_out, branch[...]).astype(BF)
    do_turned = do_t.T
    for u in range(GROUPS):
        heads = slice(u * HD, (u + 1) * HD)
        do_rows[u] = head_rows(do_t, u)
        do_cols[u] = head_columns(do_turned, u)
        delta[u : u + 1, :] = jnp.sum(do_t[heads, :].astype(F32) * ot[heads, :], axis=0, keepdims=True)
    loads[7].wait()
    both = pl.ds(pl.multiple_of(p.y * 2 * SHARD, 2 * SHARD), 2 * SHARD)
    out_scatter, out_spread = [], []
    for n in range(3):
        to_y = (p.y + n + 1) % 4
        to = {"tensor": to_y * 2 + p.h}
        theirs = pl.ds(pl.multiple_of(to_y * 2 * SHARD, 2 * SHARD), 2 * SHARD)
        out_scatter.append(remote(ffn_part.at[theirs], y_land.at[n], ys_send.at[0, n], ys_recv.at[0, n], to))
        out_spread.append(remote(out_whole.at[both], out_whole.at[both], ys_send.at[1, n], ys_recv.at[1, n], to))
    partner = {"tensor": p.y * 2 + 1 - p.h}
    near = pl.ds(pl.multiple_of(p.h * SHARD, SHARD), SHARD)
    away = pl.ds(pl.multiple_of((1 - p.h) * SHARD, SHARD), SHARD)
    out_swap = remote(mid.at[away], h_land, hs_send.at[0], hs_recv.at[0], partner)
    out_join = remote(out_whole.at[mine], out_whole.at[mine], hs_send.at[1], hs_recv.at[1], partner)
    for copy in out_scatter:
        copy.start()
    kinds_grad(3, ot[...].astype(BF), branch)
    sums.to_pair(1, 0)

    def kv_pair_copy(d):
        return remote(d_kv.at[d, 1 - p.c], kv_pair.at[d], kv_bsend.at[d], kv_brecv.at[d], p.sibling())

    def kv_far_copy(d):
        return remote(d_kv.at[d, p.c], kv_far.at[d], kv_send.at[d], kv_recv.at[d], p.chip_at(-d))

    def finish(d):
        @pl.when(p.chip - d >= 0)
        def _():
            @pl.when(((p.c == 0) & (d <= 3)) | ((p.c == 1) & (d >= 1)))
            def _():
                kv_pair_copy(d).wait_recv()
                d_kv[d, p.c] = (d_kv[d, p.c].astype(F32) + kv_pair[d].astype(F32)).astype(BF)

            @pl.when(d >= 1)
            def _():
                kv_far_copy(d).start()

    def block_back(step, carry):
        d = 4 - step // 2
        core = (1 - p.c + step) % 2
        use = (p.chip - d >= 0) & ~((d == 0) & (core > p.c)) & ~((d == 4) & (core < p.c))

        @pl.when(use)
        def _():
            bias = block_bias(p, lengths, window, d, core, code, at)
            keys = window[d, core, 0:ROWS, 0:SPAN]
            values = window[d, core, 0:ROWS, SPAN : 2 * SPAN]
            keys_t = keys.T
            d_key = jnp.zeros((ROWS, SPAN), F32)
            d_value = jnp.zeros((ROWS, SPAN), F32)
            probs = [jnp.exp(nn(keys, q_rows[u]) + bias - lse[u : u + 1, :]) for u in range(GROUPS)]
            d_scores = [
                (probs[u] * (nn(values, do_rows[u]) - delta[u : u + 1, :])).astype(BF) for u in range(GROUPS)
            ]
            for u in range(GROUPS):
                d_value = d_value + nn(probs[u].astype(BF), do_cols[u])
            for u in range(GROUPS):
                d_key = d_key + nn(d_scores[u], q_cols[u])
            for u in range(GROUPS):
                heads = slice(u * HD, (u + 1) * HD)
                dqt[heads, :] = dqt[heads, :] + nn(keys_t[heads, :], d_scores[u])
            d_kv[d, core, :, 0:SPAN] = d_key.astype(BF)
            d_kv[d, core, :, SPAN : 2 * SPAN] = d_value.astype(BF)

            @pl.when(core != p.c)
            def _():
                kv_pair_copy(d).start()

        @pl.when((step % 2 == 1) & (step > 1))
        def _():
            finish(d + 1)

        return carry

    lax.fori_loop(0, 10, block_back, 0)
    finish(0)
    sums.pair_add(1, 0)
    for copy in out_scatter:
        copy.wait()
    summed = ffn_part[both, :].astype(F32)
    for n in range(3):
        summed = summed + y_land[n].astype(F32)
    mid[...] = summed.astype(BF)
    out_swap.start()

    dq_t = (dqt[...] * (HD ** -0.5)).astype(BF)
    dq = dq_t.T
    small[8:16, :] = unit_rows[...]
    small[8:9, :] = jnp.sum(dq.astype(F32), axis=0, keepdims=True)
    loads[6].wait()
    kinds_grad(0, dq_t, low1)
    sums.to_pair(0, 0)

    for k, i in early:
        sums.line_add(k, i)

    out_swap.wait()
    summed = mid[near, :].astype(F32) + h_land[...].astype(F32)
    out_whole[mine, :] = (hidden[...] + live * (summed + shifts[1:2, :])).astype(BF)
    out_join.start()
    sums.pair_add(0, 0)

    def stats(r, carry):
        rows = pl.ds(pl.multiple_of(r * 32, 32), 32)
        values = x_rows[rows, :].astype(F32)
        mean = jnp.mean(values, axis=-1, keepdims=True)
        centred = values - mean
        norm1_mean[rows, :] = mean
        norm1_factor[rows, :] = lax.rsqrt(jnp.mean(centred * centred, axis=-1, keepdims=True) + EPS)
        return carry

    lax.fori_loop(0, ROWS // 32, stats, 0)

    dkv_sum[...] = d_kv[0, p.c].astype(F32)
    for d in (1, 2, 3, 4):
        @pl.when(p.chip + d < 8)
        def _():
            kv_far_copy(d).wait_recv()
            dkv_sum[...] = dkv_sum[...] + kv_far[d].astype(F32)

    dkv = dkv_sum[...].astype(BF)
    dkv_t = dkv.T
    small[9:10, :] = jnp.sum(dkv[:, SPAN:].astype(F32), axis=0, keepdims=True)

    def norm1_part(n, carry):
        cols = pl.ds(pl.multiple_of(n * 256, 256), 256)
        total = jnp.zeros((ROWS, 256), F32)
        for i, left in enumerate((dq, dkv[:, :SPAN], dkv[:, SPAN:])):
            total = total + nn(left, jnp.concatenate([proj[u, i, :, cols] for u in range(GROUPS)], axis=0))
        dn1_part[:, cols] = total.astype(BF)
        unit = (x_rows[:, cols].astype(F32) - norm1_mean[...]) * norm1_factor[...]
        bank[n, 0:1, :] = jnp.sum(total * unit, axis=0, keepdims=True)
        bank[n, 4:5, :] = jnp.sum(total, axis=0, keepdims=True)
        return carry

    lax.fori_loop(0, WIDTH // 256, norm1_part, 0)
    slices = []
    for n, (dy, dx) in enumerate(T_STEPS):
        to = p.tensor_at(dy, dx)
        slices.append(remote(bank.at[to], bank_land.at[n], v1_send.at[n], v1_recv.at[n], {"tensor": to}))
    for copy in slices:
        copy.start()
    last_scatter = scatter_copies(p, dn1_part, land.at[1], rs_send.at[1], rs_recv.at[1])
    for copy in last_scatter:
        copy.start()
    kinds_grad(1, dkv_t[:SPAN], low1)
    sums.to_pair(0, 1)
    kinds_grad(2, dkv_t[SPAN:], low1)
    sums.to_pair(0, 2)
    for copy in slices:
        copy.wait()
    total = bank[p.t]
    for n in range(len(T_STEPS)):
        total = total + bank_land[n]
    small[0:8, :] = total
    pair_small = remote(small, small_pair, v2_send, v2_recv, p.sibling())
    pair_small.start()
    pair_small.wait()
    here = p.z * 2 + p.x
    small_all[here] = small[...] + small_pair[...]
    spread = []
    for n in range(1, 8):
        to = p.seq((p.z + n // 2) % 4, (p.x + n % 2) % 2, p.c)
        spread.append(remote(small_all.at[here], small_all.at[here], v3_send.at[n - 1], v3_recv.at[n - 1], to))
    for copy in spread:
        copy.start()
    sums.line_mid(1, 0)
    sums.line_mid(0, 0)
    out_join.wait()
    for copy in out_spread:
        copy.start()
    for i in (1, 2):
        sums.pair_add(0, i)
    sums.line_add(1, 0)
    for i in (1, 2):
        sums.line_mid(0, i)

    for copy in spread:
        copy.wait()
    total = small_all[0]
    for n in range(1, 8):
        total = total + small_all[n]
    bank_back[p.t] = total[0:8, :]
    unit_out[...] = total[8:16, :]
    back = []
    for n, (dy, dx) in enumerate(T_STEPS):
        to = {"tensor": p.tensor_at(dy, dx)}
        back.append(remote(bank_back.at[p.t], bank_back.at[p.t], v4_send.at[n], v4_recv.at[n], to))
    for copy in back:
        copy.start()

    _, unit1, factor1 = normalize(x_rows[mine, :].astype(F32), gains[0:1, :], shifts[2:3, :])
    for copy in last_scatter:
        copy.wait()
    d_norm1 = scatter_sum(p, dn1_part, land.at[1])
    d_in, _, _ = norm_back(d_norm1, unit1, factor1, gains[0:1, :])
    in_whole[mine, :] = (d_hidden[...] + d_in).astype(BF)
    last_gather = gather_copies(p, in_whole, ag_send.at[1], ag_recv.at[1])
    for copy in last_gather:
        copy.start()
    for i in range(3):
        sums.line_add(0, i)
    for i in range(3):
        sums.last_add(i)
    for copy in out_spread:
        copy.wait()
    for copy in last_gather:
        copy.wait()
    stores = [
        pltpu.make_async_copy(out_whole, out_any, out_sem.at[0]),
        pltpu.make_async_copy(in_whole, grad_any, out_sem.at[1]),
    ]
    for copy in stores:
        copy.start()
    for copy in back:
        copy.wait()
    vec_out[...] = bank_back[...]
    sums.drain()
    for d in range(5):
        @pl.when((p.chip - d >= 0) & (((p.c == 1) & (d <= 3)) | ((p.c == 0) & (d >= 1))))
        def _():
            kv_pair_copy(d).wait_send()

        if d >= 1:
            @pl.when(p.chip - d >= 0)
            def _():
                kv_far_copy(d).wait_send()

    for copy in stores:
        copy.wait()


def backward_call(
    lengths, exits, gains, shifts, dn2_part, gt, dft, ot, lse, hidden, unit_rows, qt,
    tokens, cotangent, dffn, low2, low1, window, proj, ffn_part,
):
    vmem = pl.BlockSpec(memory_space=pltpu.VMEM)
    anywhere = pl.BlockSpec(memory_space=pl.ANY)
    shape = jax.ShapeDtypeStruct
    dma = pltpu.SemaphoreType.DMA
    rows_low = pltpu.VMEM((ROWS, WIDTH), BF)
    shard_low = pltpu.VMEM((SHARD, WIDTH), BF)
    masked = pltpu.VMEM((GROUPS, SPAN, ROWS), BF)
    return pl.pallas_call(
        backward_kernel,
        in_specs=[pl.BlockSpec(memory_space=pltpu.SMEM)] + [vmem] * 11 + [anywhere] * 8,
        out_specs=[anywhere, anywhere, vmem, vmem, vmem],
        out_shape=[
            shape((ROWS, WIDTH), BF),
            shape((ROWS, WIDTH), BF),
            shape((3, HD, WIDTH), F32),
            shape((8, 8, 256), F32),
            shape((8, SPAN), F32),
        ],
        scratch_shapes=[
            pltpu.VMEM((16, 3, HD, WIDTH), BF),
            pltpu.VMEM((8, 3, HD, WIDTH), BF),
            pltpu.VMEM((2, 2, 3, HALF, WIDTH), BF),
            pltpu.VMEM((2, 2, 3, HD, WIDTH), BF),
            pltpu.VMEM((3, HD, WIDTH), BF),
            pltpu.VMEM((5, 2, EXT, 2 * SPAN), BF),
            pltpu.VMEM((5, 2, ROWS, 2 * SPAN), BF),
            pltpu.VMEM((5, ROWS, 2 * SPAN), BF),
            pltpu.VMEM((5, ROWS, 2 * SPAN), BF),
            rows_low, rows_low, rows_low,
            pltpu.VMEM((GROUPS, 4, HD, WIDTH), BF),
            rows_low, rows_low, shard_low,
            rows_low, rows_low, rows_low, rows_low,
            pltpu.VMEM((2, 7, SHARD, WIDTH), BF),
            masked, masked, masked, masked,
            pltpu.VMEM((8, ROWS), F32),
            pltpu.VMEM((SPAN, ROWS), F32),
            pltpu.VMEM((ROWS, 2 * SPAN), F32),
            pltpu.VMEM((SHARD, WIDTH), F32),
            pltpu.VMEM((8, 8, 256), F32),
            pltpu.VMEM((7, 8, 256), F32),
            pltpu.VMEM((16, 256), F32),
            pltpu.VMEM((16, 256), F32),
            pltpu.VMEM((8, 16, 256), F32),
            pltpu.VMEM((8, 8, 256), F32),
            pltpu.VMEM((ROWS, 1), F32),
            pltpu.VMEM((ROWS, 1), F32),
            pltpu.VMEM((ROWS, 1), F32),
            pltpu.VMEM((2 * SHARD, WIDTH), BF),
            pltpu.VMEM((3, 2 * SHARD, WIDTH), BF),
            shard_low,
            dma((2, 7)), dma((2, 7)), dma((2, 7)), dma((2, 7)),
            dma((2, 3)), dma((2, 3)), dma((2,)), dma((2,)),
            dma((8, 3)), dma((8, 3)), dma((2, 2, 3)), dma((2, 2, 3)), dma((2, 2, 3)), dma((2, 2, 3)), dma((3,)), dma((3,)),
            dma((5,)), dma((5,)), dma((5,)), dma((5,)),
            dma((7,)), dma((7,)), dma, dma, dma((7,)), dma((7,)), dma((7,)), dma((7,)),
            dma((8,)), dma((2,)),
        ],
        compiler_params=pltpu.CompilerParams(
            collective_id=1, has_side_effects=True, vmem_limit_bytes=60 * 2**20
        ),
        name="layer_backward",
    )(
        lengths, exits, gains, shifts, dn2_part, gt, dft, ot, lse, hidden, unit_rows, qt,
        tokens, cotangent, dffn, low2, low1, window, proj, ffn_part,
    )


def high(left, right):
    return jnp.dot(left, right, precision=HIGH, preferred_element_type=F32)


def step_kernel(
    grads, panel_mom, panels, vec_sums, unit_sums, unit_bias, unit_bias_mom, gains, gains_mom, vec_bias, vec_bias_mom,
    in_low, out_low,
    out_copy, in_grad, new_panels, new_mom, new_unit, new_unit_mom, new_gains, new_gains_mom, new_vec, new_vec_mom,
):
    out_copy[...] = out_low[...]
    count = panels.shape[0]
    eye = jnp.where(
        lax.broadcasted_iota(jnp.int32, (HD, HD), 0) == lax.broadcasted_iota(jnp.int32, (HD, HD), 1), 1.0, 0.0
    )
    scale, gram, chain = [], [], [None] * count
    for n in range(count):
        moment = DECAY * panel_mom[n] + grads[n]
        new_mom[n] = moment
        factor = lax.rsqrt(jnp.sum(moment * moment, axis=(0, 1), keepdims=True) + 1e-06)
        current = moment * factor
        scale.append(factor)
        gram.append(
            lax.dot_general(
                current, current, (((1,), (1,)), ((), ())), precision=HIGH, preferred_element_type=F32
            )
        )
    in_grad[...] = in_low[...].astype(F32)
    vec_rows = [jnp.concatenate([vec_sums[n, r : r + 1, :] for n in range(8)], axis=1) for r in range(6)]
    unit_rows = [
        jnp.concatenate([unit_sums[n : n + 1, u * HD : (u + 1) * HD] for n in range(6)], axis=1)
        for u in range(GROUPS)
    ]
    for rows, old, old_mom, new, mom in (
        (vec_rows[0:2], gains, gains_mom, new_gains, new_gains_mom),
        (vec_rows[2:6], vec_bias, vec_bias_mom, new_vec, new_vec_mom),
        (unit_rows, unit_bias, unit_bias_mom, new_unit, new_unit_mom),
    ):
        moment = DECAY * old_mom[...] + jnp.concatenate(rows, axis=0)
        mom[...] = moment
        new[...] = old[...] - LR_VECTOR * moment
    for sweep in range(NS_ITERS):
        squares = [high(a, a) for a in gram]
        steps = [NS_A * eye + NS_B * a + NS_C * s for a, s in zip(gram, squares)]
        chain = [m if sweep == 0 else high(m, c) for m, c in zip(steps, chain)]
        if sweep < NS_ITERS - 1:
            halves = [high(m, a) for m, a in zip(steps, gram)]
            gram = [high(h, m) for h, m in zip(halves, steps)]
    for n in range(count):
        direction = high(chain[n], new_mom[n] * scale[n])
        size_u = jnp.sum(direction * direction, axis=(0, 1), keepdims=True)
        held = panels[n]
        size_w = jnp.sum(held * held, axis=(0, 1), keepdims=True)
        new_panels[n] = held - LR_MATRIX * jnp.sqrt(size_w) * lax.rsqrt(size_u + 1e-06) * direction


def step_call(*args):
    vmem = pl.BlockSpec(memory_space=pltpu.VMEM)
    shape = jax.ShapeDtypeStruct
    panels, unit, gain, vec = (shape(args[n].shape, F32) for n in (2, 5, 7, 9))
    return pl.pallas_call(
        step_kernel,
        in_specs=[vmem] * 13,
        out_specs=[vmem] * 10,
        out_shape=[
            shape((ROWS, WIDTH), BF), shape((ROWS, WIDTH), F32), panels, panels, unit, unit, gain, gain, vec, vec,
        ],
        compiler_params=pltpu.CompilerParams(vmem_limit_bytes=60 * 2**20),
        name="panel_step",
    )(*args)


def per_device(
    tokens, cotangent, exits, lengths, panels, panel_mom,
    unit_bias, unit_bias_mom, gains, gains_mom, vec_bias, vec_bias_mom,
):
    exits = exits[None, :]
    (
        low1, qt, window, ot, lse, hidden, low2, gt, dft, ffn_part, dn2_part, proj, dffn, unit_rows,
    ) = forward_call(
        lengths, tokens, cotangent, exits, panels, unit_bias, gains, vec_bias
    )
    output, input_grad, panel_grads, vec_sums, unit_sums = backward_call(
        lengths, exits, gains, vec_bias, dn2_part, gt, dft, ot, lse, hidden, unit_rows, qt,
        tokens, cotangent, dffn, low2, low1, window, proj, ffn_part,
    )
    return step_call(
        panel_grads, panel_mom, panels, vec_sums, unit_sums, unit_bias, unit_bias_mom,
        gains, gains_mom, vec_bias, vec_bias_mom, input_grad, output,
    )


def solution(mesh):
    held = P(("tensor", "seq"), None, None)
    return jax.shard_map(
        per_device,
        mesh=mesh,
        in_specs=(
            P("seq", None), P("seq", None), P("seq"), P(), held, held,
            P("tensor", None), P("tensor", None), P(), P(), P(), P(),
        ),
        out_specs=(
            P("seq", None), P("seq", None), held, held,
            P("tensor", None), P("tensor", None), P(), P(), P(), P(),
        ),
        check_vma=False,
    )
```
